32 devices in a mesh: dp: 8 (over y, x, core), fsdp: 4 (over z).
Axes of the slice: x: 2, y: 2, z: 4, core: 2. Of those that a mesh axis runs over, the one named last changes fastest.
Arguments:
- acts: bfloat16 [4096, 5120], P(('dp', 'fsdp')), may hold values from -6 to 6
- grad_out: bfloat16 [4096, 6912], P('dp', 'fsdp'), may hold values from -0.125 to 0.125
- projection: bfloat16 [5120, 256], replicated, may hold values from -0.375 to 0.375
- moment_one: float32 [256, 6912], P('dp', 'fsdp'), may hold values from -6 to 6
- moment_two: float32 [256, 6912], P('dp', 'fsdp'), may hold values from 0.5 to 4
- master: float32 [5120, 6912], P('dp', 'fsdp'), may hold values from -6 to 6
Outputs:
- moment_one_new: float32 [256, 6912], P('dp', 'fsdp')
- moment_two_new: float32 [256, 6912], P('dp', 'fsdp')
- master_new: float32 [5120, 6912], P('dp', 'fsdp')
- weight_cols: bfloat16 [5120, 6912], P(None, 'fsdp')
The draws below stay inside these ranges and needn't reach their ends.
All inputs are finite; a program needn't handle non-finite values.
Results may differ from the reference program's by a relative error of at most 0.001.
The reference program's roundings to bfloat16 on the way count: a program that leaves them out, or rounds other values in their place, can miss the bound.
Values may be sent and summed in bfloat16 or wider, within the bound.
No kernel may reach another device: no remote copies, remote signals or barrier semaphores. Data moves between devices by JAX's collectives and lax.ppermute only.
A program may use at most 128 MiB of HBM per device.

```python
import math
import jax
import jax.numpy as jnp
from jax import lax

D = 5120
FW = 6912
R = 256
TOK_DEV = 128
STEP = 1000
TOKENS = 4096
N_DP = 8
N_FSDP = 4


def block_scale(stream_key, dims, pieces, least, high):
    loudness, own = 1.0, jax.random.fold_in(stream_key, 6)
    for axis_at, shards_of in pieces:
        steps = jnp.exp(jax.random.uniform(jax.random.fold_in(own, axis_at), (shards_of,), jnp.float32, least / len(pieces), high / len(pieces)))
        loudness = loudness * jnp.repeat(steps, dims[axis_at] // shards_of).reshape([-1 if axis == axis_at else 1 for axis in range(len(dims))])
    return loudness


def bell_draw(key, dims, spread, limit, split=(), kind=jnp.bfloat16):
    result = jax.random.normal(key, dims, jnp.float32) * spread
    if len(split) > 0:
        result = block_scale(key, dims, split, -0.22, 0.18) * result
    return jnp.clip(result, min=-limit, max=limit).astype(kind)


def setup_inputs(seed: int = 0) -> dict:
    key_of = jax.random.split(jax.random.key(seed), 7)
    acts = bell_draw(key_of[0], (TOKENS, D), 1.0, 6.0, ((0, 32),))
    grad_out = bell_draw(key_of[1], (TOKENS, FW), (6 * (TOKENS * D // R) ** -0.5), 0.125, ((0, 8), (1, 4)))
    projection = bell_draw(key_of[2], (D, R), R ** -0.5, 0.375)
    moment_one = bell_draw(key_of[3], (R, FW), 1.0, 6.0, ((0, 8), (1, 4)), jnp.float32)
    moment_two = jnp.clip(jnp.exp(math.log(4.0) - 2.0794415 * jax.random.uniform(key_of[4], (R, FW), jnp.float32) ** block_scale(key_of[4], (R, FW), ((0, 8), (1, 4)), -0.2, 0.2)), 0.5, 4.0)
    master = bell_draw(key_of[5], (D, FW), 1.0, 6.0, ((0, 8), (1, 4)), jnp.float32)
    return {"acts": acts, "grad_out": grad_out, "projection": projection, "moment_one": moment_one, "moment_two": moment_two, "master": master}


BETA_ONE = 0.9
BETA_TWO = 0.999
ADAM_EPS = 1e-08
LEARN_RATE = 0.01

def reference(acts, grad_out, projection, moment_one, moment_two, master):
    act_blocks = acts.reshape(N_DP, N_FSDP * TOK_DEV, D)
    out_blocks = grad_out.reshape(N_DP, N_FSDP * TOK_DEV, FW)

    def add_block(total, pair):
        act_piece, out_piece = pair
        projected = jnp.dot(act_piece, projection, preferred_element_type=jnp.float32).astype(jnp.bfloat16)
        partial_value = jnp.dot(projected.T, out_piece, preferred_element_type=jnp.float32).astype(jnp.bfloat16)
        partial_value = lax.optimization_barrier(partial_value)
        return (total + partial_value.astype(jnp.float32), None)
    grad, unused = lax.scan(add_block, jnp.zeros((R, FW), jnp.float32), (act_blocks, out_blocks))
    moment_one_new = BETA_ONE * moment_one + (1.0 - BETA_ONE) * grad
    moment_two_new = BETA_TWO * moment_two + (1.0 - BETA_TWO) * grad * grad
    correct_one = 1.0 - BETA_ONE ** STEP
    correct_two = 1.0 - BETA_TWO ** STEP
    update = (moment_one_new / correct_one / (jnp.sqrt(moment_two_new / correct_two) + ADAM_EPS)).astype(jnp.bfloat16)
    expanded = jnp.dot(projection, update, preferred_element_type=jnp.float32)
    master_new = master - LEARN_RATE * expanded
    weight_cols = master_new.astype(jnp.bfloat16)
    return (moment_one_new, moment_two_new, master_new, weight_cols)
```

```python
import functools

import jax
import jax.numpy as jnp
from jax import lax
from jax.experimental import pallas as pl
from jax.experimental.pallas import tpu as pltpu
from jax.sharding import PartitionSpec as P

STEP = 1000


BETA_ONE = 0.9
BETA_TWO = 0.999
ADAM_EPS = 1e-08
LEARN_RATE = 0.01
CORRECT_ONE = 1.0 - BETA_ONE**STEP
CORRECT_TWO = 1.0 - BETA_TWO**STEP

VMEM = pl.BlockSpec(memory_space=pltpu.VMEM)
SMEM = pl.BlockSpec(memory_space=pltpu.SMEM)
ANY = pl.BlockSpec(memory_space=pl.ANY)


def adam(grad, moment_one, moment_two):
    moment_one_new = BETA_ONE * moment_one + (1.0 - BETA_ONE) * grad
    moment_two_new = BETA_TWO * moment_two + (1.0 - BETA_TWO) * grad * grad
    update = (
        moment_one_new / CORRECT_ONE / (jnp.sqrt(moment_two_new / CORRECT_TWO) + ADAM_EPS)
    ).astype(jnp.bfloat16)
    return moment_one_new, moment_two_new, update


def plain_body(acts, grad_out, projection, moment_one, moment_two, master):
    projected = jnp.dot(acts, projection, preferred_element_type=jnp.float32).astype(jnp.bfloat16)
    group_proj = lax.all_gather(projected, "fsdp", axis=0, tiled=True)
    partial_value = jnp.einsum(
        "tr,tc->rc", group_proj, grad_out, preferred_element_type=jnp.float32
    )
    partial_value = lax.optimization_barrier(partial_value.astype(jnp.bfloat16))
    grad = lax.psum_scatter(
        partial_value.astype(jnp.float32), "dp", scatter_dimension=0, tiled=True
    )
    moment_one_new, moment_two_new, update = adam(grad, moment_one, moment_two)
    slab_rows = master.shape[0]
    proj_slab = lax.dynamic_slice_in_dim(projection, lax.axis_index("dp") * slab_rows, slab_rows, 0)
    piece = lax.all_gather(update, "dp", axis=0, tiled=True)
    expanded = jnp.dot(proj_slab, piece, preferred_element_type=jnp.float32)
    master_new = master - LEARN_RATE * expanded
    weight_cols = lax.all_gather(master_new.astype(jnp.bfloat16), "dp", axis=0, tiled=True)
    return (moment_one_new, moment_two_new, master_new, weight_cols)


def send(value, axis, size, mask):
    return lax.ppermute(value, axis, [(i, i ^ mask) for i in range(size)])


def partial_kernel(place, grad_t, *refs, n_fsdp, n_dp):
    pieces, outs, (tokens, result) = refs[:n_fsdp], refs[n_fsdp : n_fsdp + n_dp], refs[n_fsdp + n_dp :]
    count = pieces[0].shape[0]
    rows = outs[0].shape[0]
    for k in range(n_fsdp):
        tokens[pl.ds(pl.multiple_of((place[1] ^ k) * count, count), count), :] = pieces[k][...]
    result[...] = lax.dot_general(
        tokens[...].T, grad_t[...], (((1,), (1,)), ((), ())), preferred_element_type=jnp.float32
    ).astype(jnp.bfloat16)
    for k in range(n_dp):
        outs[k][...] = result[pl.ds(pl.multiple_of((place[0] ^ k) * rows, rows), rows), :]


def adam_kernel(moment_one, moment_two, *refs, n_dp):
    pieces, (one_new, two_new, update) = refs[:n_dp], refs[n_dp:]
    grad = pieces[0][...].astype(jnp.float32)
    for k in range(1, n_dp):
        grad = grad + pieces[k][...].astype(jnp.float32)
    one, two, value = adam(grad, moment_one[...], moment_two[...])
    one_new[...] = one
    two_new[...] = two
    cols = value.shape[1]
    update[...] = jnp.zeros_like(update)
    update[:, :cols] = value


def gather_update(place, pieces, wide, tall):
    rows = pieces[0].shape[0]
    for k, piece in enumerate(pieces):
        wide[pl.ds(pl.multiple_of((place[0] ^ k) * rows, rows), rows), :] = piece[...]
    tall[...] = wide[...].T


def expand(tall, slab, first, count):
    return lax.dot_general(
        tall[pl.ds(first, count), :], slab[...], (((1,), (1,)), ((), ())),
        preferred_element_type=jnp.float32,
    )


def weight_kernel(place, slab, master_t, *refs, n_dp, block):
    pieces, weight, (wide, tall) = refs[:n_dp], refs[n_dp], refs[n_dp + 1 :]
    step = pl.program_id(0)

    @pl.when(step == 0)
    def _():
        gather_update(place, pieces, wide, tall)

    first = pl.multiple_of(step * block, block)
    master_new = master_t[...] - LEARN_RATE * expand(tall, slab, first, block)
    weight[...] = master_new.astype(jnp.bfloat16)


def master_kernel(place, slab, master_t, *refs, n_dp, block):
    pieces, out, (wide, tall) = refs[:n_dp], refs[n_dp], refs[n_dp + 1 :]
    step = pl.program_id(0)

    @pl.when(step == 0)
    def _():
        gather_update(place, pieces, wide, tall)

    first = pl.multiple_of(step * block, block)
    out[...] = master_t[...] - LEARN_RATE * expand(tall, slab, first, block)


def expand_call(kernel, dtype, place, projection, master_t, pieces, block):
    cols, slab_rows = master_t.shape
    rank = projection.shape[1]
    wide = pieces[0].shape[1]
    n_dp = len(pieces)
    whole = pl.BlockSpec(pieces[0].shape, lambda i, s: (0, 0))
    return pl.pallas_call(
        functools.partial(kernel, n_dp=n_dp, block=block),
        out_shape=jax.ShapeDtypeStruct((cols, slab_rows), dtype),
        grid_spec=pltpu.PrefetchScalarGridSpec(
            num_scalar_prefetch=1,
            grid=(cols // block,),
            in_specs=[
                pl.BlockSpec((slab_rows, rank), lambda i, s: (s[0], 0)),
                pl.BlockSpec((block, slab_rows), lambda i, s: (i, 0)),
            ]
            + [whole] * n_dp,
            out_specs=pl.BlockSpec((block, slab_rows), lambda i, s: (i, 0)),
            scratch_shapes=[
                pltpu.VMEM((rank, wide), jnp.bfloat16),
                pltpu.VMEM((wide, rank), jnp.bfloat16),
            ],
        ),
        compiler_params=pltpu.CompilerParams(vmem_limit_bytes=32 * 2**20),
        cost_estimate=pl.CostEstimate(
            flops=2 * cols * slab_rows * rank, bytes_accessed=8 * cols * slab_rows, transcendentals=0
        ),
    )(place, projection, master_t, *pieces)


def lay_kernel(place, *refs, spots, fresh):
    refs = refs if fresh else refs[1:]
    pieces, out, sems = refs[: len(spots)], refs[len(spots)], refs[len(spots) + 1]
    copies = []
    for at, ((mask, first), piece) in enumerate(zip(spots, pieces)):
        count, width = piece.shape
        column = pl.multiple_of((place[0] ^ mask) * width, 128)
        copies.append(
            pltpu.make_async_copy(
                piece, out.at[pl.ds(first, count), pl.ds(column, width)], sems.at[at]
            )
        )
    for copy in copies:
        copy.start()
    for copy in copies:
        copy.wait()


def lay(place, out, shape, spots, pieces):
    fresh = out is None
    held = [] if fresh else [out]
    size = sum(2 * 2 * piece.size for piece in pieces)
    return pl.pallas_call(
        functools.partial(lay_kernel, spots=spots, fresh=fresh),
        out_shape=jax.ShapeDtypeStruct(shape, jnp.bfloat16),
        in_specs=[SMEM] + [ANY] * (len(held) + len(pieces)),
        out_specs=ANY,
        scratch_shapes=[pltpu.SemaphoreType.DMA((len(spots),))],
        input_output_aliases={} if fresh else {1: 0},
        cost_estimate=pl.CostEstimate(flops=0, bytes_accessed=size, transcendentals=0),
    )(place, *held, *pieces)


def kernel_body(acts, grad_out, projection, moment_one, moment_two, master, n_dp, n_fsdp):
    cols = grad_out.shape[1]
    rank = projection.shape[1]
    rows = moment_one.shape[0]
    slab_rows = master.shape[0]
    wide = -(-cols // 128) * 128
    place = jnp.stack([lax.axis_index("dp"), lax.axis_index("fsdp")]).astype(jnp.int32)
    master_t = master.T

    projected = jnp.dot(acts, projection, preferred_element_type=jnp.float32).astype(jnp.bfloat16)
    tokens = [projected] + [send(projected, "fsdp", n_fsdp, k) for k in range(1, n_fsdp)]
    parts = pl.pallas_call(
        functools.partial(partial_kernel, n_fsdp=n_fsdp, n_dp=n_dp),
        out_shape=[jax.ShapeDtypeStruct((rows, cols), jnp.bfloat16)] * n_dp,
        in_specs=[SMEM] + [VMEM] * (1 + n_fsdp),
        out_specs=[VMEM] * n_dp,
        scratch_shapes=[
            pltpu.VMEM((n_fsdp * projected.shape[0], rank), jnp.bfloat16),
            pltpu.VMEM((rank, cols), jnp.bfloat16),
        ],
        compiler_params=pltpu.CompilerParams(vmem_limit_bytes=32 * 2**20),
    )(place, grad_out.T, *tokens)
    parts = [parts[0]] + [send(parts[k], "dp", n_dp, k) for k in range(1, n_dp)]
    moment_one_new, moment_two_new, update = pl.pallas_call(
        functools.partial(adam_kernel, n_dp=n_dp),
        out_shape=[
            jax.ShapeDtypeStruct(moment_one.shape, jnp.float32),
            jax.ShapeDtypeStruct(moment_two.shape, jnp.float32),
            jax.ShapeDtypeStruct((rows, wide), jnp.bfloat16),
        ],
        in_specs=[VMEM] * (2 + n_dp),
        out_specs=[VMEM] * 3,
        compiler_params=pltpu.CompilerParams(vmem_limit_bytes=32 * 2**20),
    )(moment_one, moment_two, *parts)
    updates = [update] + [send(update, "dp", n_dp, k) for k in range(1, n_dp)]

    half = cols // 2
    weight = expand_call(weight_kernel, jnp.bfloat16, place, projection, master_t, updates, cols // 4)
    shape = (cols, n_dp * slab_rows)
    one, two = weight[:half], weight[half:]
    one_x, two_y = send(one, "dp", n_dp, 2), send(two, "dp", n_dp, 4)
    two_x, one_y = send(two, "dp", n_dp, 2), send(one, "dp", n_dp, 4)
    weight_c = send(weight, "dp", n_dp, 1)
    out = lay(place, None, shape, ((0, 0),), (weight,))
    one_xy, two_yx = send(one_x, "dp", n_dp, 4), send(two_y, "dp", n_dp, 2)
    one_xc, two_yc = send(one_x, "dp", n_dp, 1), send(two_y, "dp", n_dp, 1)
    master_new = expand_call(master_kernel, jnp.float32, place, projection, master_t, updates, cols // 4)
    out = lay(place, out, shape, ((2, 0), (4, half), (1, 0)), (one_x, two_y, weight_c))
    two_xc, one_yc = send(two_x, "dp", n_dp, 1), send(one_y, "dp", n_dp, 1)
    out = lay(
        place, out, shape, ((2, half), (4, 0), (3, 0), (5, half)), (two_x, one_y, one_xc, two_yc)
    )
    one_xyc, two_yxc = send(one_xy, "dp", n_dp, 1), send(two_yx, "dp", n_dp, 1)
    out = lay(place, out, shape, ((6, 0), (6, half), (3, half), (5, 0)), (one_xy, two_yx, two_xc, one_yc))
    out = lay(place, out, shape, ((7, 0), (7, half)), (one_xyc, two_yxc))
    return (moment_one_new, moment_two_new, master_new.T, out.T)


def solution(mesh):
    n_dp, n_fsdp = mesh.shape["dp"], mesh.shape["fsdp"]

    def body(acts, grad_out, projection, moment_one, moment_two, master):
        args = (acts, grad_out, projection, moment_one, moment_two, master)
        fits = n_dp == 8 and n_fsdp == 4 and moment_one.shape[0] % 32 == 0 and master.shape[0] % 128 == 0
        if fits and grad_out.shape[1] % 64 == 0 and acts.shape[0] % 128 == 0:
            return kernel_body(*args, n_dp, n_fsdp)
        return plain_body(*args)

    in_specs = (
        P(("dp", "fsdp"), None),
        P("dp", "fsdp"),
        P(),
        P("dp", "fsdp"),
        P("dp", "fsdp"),
        P("dp", "fsdp"),
    )
    out_specs = (P("dp", "fsdp"), P("dp", "fsdp"), P("dp", "fsdp"), P(None, "fsdp"))
    return jax.shard_map(body, mesh=mesh, in_specs=in_specs, out_specs=out_specs, check_vma=False)
```

```python
import functools

import jax
import jax.numpy as jnp
from jax import lax
from jax.experimental import pallas as pl
from jax.experimental.pallas import tpu as pltpu
from jax.sharding import PartitionSpec as P

STEP = 1000


BETA_ONE = 0.9
BETA_TWO = 0.999
ADAM_EPS = 1e-08
LEARN_RATE = 0.01
CORRECT_ONE = 1.0 - BETA_ONE**STEP
CORRECT_TWO = 1.0 - BETA_TWO**STEP

VMEM = pl.BlockSpec(memory_space=pltpu.VMEM)
SMEM = pl.BlockSpec(memory_space=pltpu.SMEM)
ANY = pl.BlockSpec(memory_space=pl.ANY)


def adam(grad, moment_one, moment_two):
    moment_one_new = BETA_ONE * moment_one + (1.0 - BETA_ONE) * grad
    moment_two_new = BETA_TWO * moment_two + (1.0 - BETA_TWO) * grad * grad
    update = (
        moment_one_new / CORRECT_ONE / (jnp.sqrt(moment_two_new / CORRECT_TWO) + ADAM_EPS)
    ).astype(jnp.bfloat16)
    return moment_one_new, moment_two_new, update


def plain_body(acts, grad_out, projection, moment_one, moment_two, master):
    projected = jnp.dot(acts, projection, preferred_element_type=jnp.float32).astype(jnp.bfloat16)
    group_proj = lax.all_gather(projected, "fsdp", axis=0, tiled=True)
    partial_value = jnp.einsum(
        "tr,tc->rc", group_proj, grad_out, preferred_element_type=jnp.float32
    )
    partial_value = lax.optimization_barrier(partial_value.astype(jnp.bfloat16))
    grad = lax.psum_scatter(
        partial_value.astype(jnp.float32), "dp", scatter_dimension=0, tiled=True
    )
    moment_one_new, moment_two_new, update = adam(grad, moment_one, moment_two)
    slab_rows = master.shape[0]
    proj_slab = lax.dynamic_slice_in_dim(projection, lax.axis_index("dp") * slab_rows, slab_rows, 0)
    piece = lax.all_gather(update, "dp", axis=0, tiled=True)
    expanded = jnp.dot(proj_slab, piece, preferred_element_type=jnp.float32)
    master_new = master - LEARN_RATE * expanded
    weight_cols = lax.all_gather(master_new.astype(jnp.bfloat16), "dp", axis=0, tiled=True)
    return (moment_one_new, moment_two_new, master_new, weight_cols)


def send(value, axis, size, mask):
    return lax.ppermute(value, axis, [(i, i ^ mask) for i in range(size)])


def order(size):
    return (0, 6, 7, 2, 4, 3, 5, 1) if size == 8 else (0, *reversed(range(1, size)))


def partial_kernel(place, grad_t, *refs, n_fsdp, n_dp):
    pieces, outs, (tokens, result) = refs[:n_fsdp], refs[n_fsdp : n_fsdp + n_dp], refs[n_fsdp + n_dp :]
    count = pieces[0].shape[0]
    rows = outs[0].shape[0]
    for k, piece in zip(order(n_fsdp), pieces):
        tokens[pl.ds(pl.multiple_of((place[1] ^ k) * count, count), count), :] = piece[...]
    result[...] = lax.dot_general(
        tokens[...].T, grad_t[...], (((1,), (1,)), ((), ())), preferred_element_type=jnp.float32
    ).astype(jnp.bfloat16)
    for k, out in enumerate(outs):
        out[...] = result[pl.ds(pl.multiple_of((place[0] ^ k) * rows, rows), rows), :]


def adam_kernel(moment_one, moment_two, *refs, n_dp):
    pieces, (one_new, two_new, update) = refs[:n_dp], refs[n_dp:]
    grad = pieces[0][...].astype(jnp.float32)
    for k in range(1, n_dp):
        grad = grad + pieces[k][...].astype(jnp.float32)
    one, two, value = adam(grad, moment_one[...], moment_two[...])
    one_new[...] = one
    two_new[...] = two
    cols = value.shape[1]
    update[...] = jnp.zeros_like(update)
    update[:, :cols] = value


def expand(tall, slab, first, count):
    return lax.dot_general(
        tall[pl.ds(first, count), :], slab, (((1,), (1,)), ((), ())),
        preferred_element_type=jnp.float32,
    )


def weight_kernel(place, projection, master_t, *refs, n_in, spans, block):
    pieces, outs = refs[:n_in], refs[n_in:]
    if n_in > 1:
        tall, wide = outs[0], outs[-1]
        outs = outs[1:-1]
        rows = pieces[0].shape[0]
        for k, piece in zip(order(n_in), pieces):
            wide[pl.ds(pl.multiple_of((place[0] ^ k) * rows, rows), rows), :] = piece[...]
        tall[...] = wide[...].T
    else:
        tall = pieces[0]
    slab_rows = master_t.shape[1]
    slab = projection[pl.ds(pl.multiple_of(place[0] * slab_rows, slab_rows), slab_rows), :]
    for (first, count), out in zip(spans, outs):
        for at in range(0, count, block):
            master_new = master_t[pl.ds(first + at, block), :] - LEARN_RATE * expand(
                tall, slab, first + at, block
            )
            out[pl.ds(at, block), :] = master_new.astype(jnp.bfloat16)


def weights(place, projection, master_t, pieces, spans, block):
    slab_rows = master_t.shape[1]
    rank = projection.shape[1]
    wide = pieces[0].shape[1]
    out_shape = [jax.ShapeDtypeStruct((count, slab_rows), jnp.bfloat16) for _, count in spans]
    scratch = []
    if len(pieces) > 1:
        out_shape = [jax.ShapeDtypeStruct((wide, rank), jnp.bfloat16)] + out_shape
        scratch = [pltpu.VMEM((rank, wide), jnp.bfloat16)]
    size = sum(count for _, count in spans) * slab_rows
    return pl.pallas_call(
        functools.partial(weight_kernel, n_in=len(pieces), spans=spans, block=block),
        out_shape=out_shape,
        in_specs=[SMEM] + [VMEM] * (2 + len(pieces)),
        out_specs=[VMEM] * len(out_shape),
        scratch_shapes=scratch,
        compiler_params=pltpu.CompilerParams(vmem_limit_bytes=20 * 2**20),
        cost_estimate=pl.CostEstimate(flops=2 * size * rank, bytes_accessed=4 * size, transcendentals=0),
    )(place, projection, master_t, *pieces)


def master_kernel(place, slab, master_t, tall, out):
    block = master_t.shape[0]
    first = pl.multiple_of(pl.program_id(0) * block, block)
    out[...] = master_t[...] - LEARN_RATE * expand(tall, slab[...], first, block)


def new_master(place, projection, master_t, tall, block):
    cols, slab_rows = master_t.shape
    rank = projection.shape[1]
    return pl.pallas_call(
        master_kernel,
        out_shape=jax.ShapeDtypeStruct((cols, slab_rows), jnp.float32),
        grid_spec=pltpu.PrefetchScalarGridSpec(
            num_scalar_prefetch=1,
            grid=(cols // block,),
            in_specs=[
                pl.BlockSpec((slab_rows, rank), lambda i, s: (s[0], 0)),
                pl.BlockSpec((block, slab_rows), lambda i, s: (i, 0)),
                pl.BlockSpec(tall.shape, lambda i, s: (0, 0)),
            ],
            out_specs=pl.BlockSpec((block, slab_rows), lambda i, s: (i, 0)),
        ),
        compiler_params=pltpu.CompilerParams(vmem_limit_bytes=12 * 2**20),
        cost_estimate=pl.CostEstimate(
            flops=2 * cols * slab_rows * rank, bytes_accessed=8 * cols * slab_rows, transcendentals=0
        ),
    )(place, projection, master_t, tall)


def lay_kernel(place, *refs, spans, block, fresh):
    refs = refs if fresh else refs[1:]
    n_in = sum(len(masks) for _, _, masks in spans)
    pieces, out, (held, sems) = refs[:n_in], refs[n_in], refs[n_in + 1 :]
    copies = [None, None]
    at = 0
    base = 0
    for first, count, masks in spans:
        for start in range(0, count, block):
            slot = at % 2
            if copies[slot] is not None:
                copies[slot].wait()
            for mask, piece in zip(masks, pieces[base : base + len(masks)]):
                width = piece.shape[1]
                column = pl.multiple_of((place[0] ^ mask) * width, 128)
                held[slot, :, pl.ds(column, width)] = piece[pl.ds(start, block), :]
            copies[slot] = pltpu.make_async_copy(
                held.at[slot], out.at[pl.ds(first + start, block), :], sems.at[slot]
            )
            copies[slot].start()
            at += 1
        base += len(masks)
    for copy in copies:
        if copy is not None:
            copy.wait()


def lay(place, out, shape, spans, pieces, block):
    fresh = out is None
    held = [] if fresh else [out]
    size = sum(2 * 2 * piece.size for piece in pieces)
    return pl.pallas_call(
        functools.partial(lay_kernel, spans=spans, block=block, fresh=fresh),
        out_shape=jax.ShapeDtypeStruct(shape, jnp.bfloat16),
        in_specs=[SMEM] + [ANY] * len(held) + [VMEM] * len(pieces),
        out_specs=ANY,
        scratch_shapes=[
            pltpu.VMEM((2, block, shape[1]), jnp.bfloat16),
            pltpu.SemaphoreType.DMA((2,)),
        ],
        input_output_aliases={} if fresh else {1: 0},
        compiler_params=pltpu.CompilerParams(vmem_limit_bytes=20 * 2**20),
        cost_estimate=pl.CostEstimate(flops=0, bytes_accessed=size, transcendentals=0),
    )(place, *held, *pieces)


def kernel_body(acts, grad_out, projection, moment_one, moment_two, master, n_dp, n_fsdp):
    cols = grad_out.shape[1]
    rank = projection.shape[1]
    rows = moment_one.shape[0]
    slab_rows = master.shape[0]
    wide = -(-cols // 128) * 128
    place = jnp.stack([lax.axis_index("dp"), lax.axis_index("fsdp")]).astype(jnp.int32)
    master_t = master.T

    projected = jnp.dot(acts, projection, preferred_element_type=jnp.float32).astype(jnp.bfloat16)
    tokens = [projected if k == 0 else send(projected, "fsdp", n_fsdp, k) for k in order(n_fsdp)]
    parts = pl.pallas_call(
        functools.partial(partial_kernel, n_fsdp=n_fsdp, n_dp=n_dp),
        out_shape=[jax.ShapeDtypeStruct((rows, cols), jnp.bfloat16)] * n_dp,
        in_specs=[SMEM] + [VMEM] * (1 + n_fsdp),
        out_specs=[VMEM] * n_dp,
        scratch_shapes=[
            pltpu.VMEM((n_fsdp * projected.shape[0], rank), jnp.bfloat16),
            pltpu.VMEM((rank, cols), jnp.bfloat16),
        ],
        compiler_params=pltpu.CompilerParams(vmem_limit_bytes=16 * 2**20),
    )(place, grad_out.T, *tokens)
    parts = [parts[k] if k == 0 else send(parts[k], "dp", n_dp, k) for k in order(n_dp)]
    moment_one_new, moment_two_new, update = pl.pallas_call(
        functools.partial(adam_kernel, n_dp=n_dp),
        out_shape=[
            jax.ShapeDtypeStruct(moment_one.shape, jnp.float32),
            jax.ShapeDtypeStruct(moment_two.shape, jnp.float32),
            jax.ShapeDtypeStruct((rows, wide), jnp.bfloat16),
        ],
        in_specs=[VMEM] * (2 + n_dp),
        out_specs=[VMEM] * 3,
        compiler_params=pltpu.CompilerParams(vmem_limit_bytes=16 * 2**20),
    )(moment_one, moment_two, *parts)
    updates = {0: update}
    for k in (6, 2, 4, 1):
        updates[k] = send(update, "dp", n_dp, k)
    for k in (2, 4, 6):
        updates[k ^ 1] = send(updates[k], "dp", n_dp, 1)
    updates = [updates[k] for k in order(n_dp)]

    half = cols // 2
    block = cols // 12
    counts = (4 * block, 2 * block)
    chunks = len(counts)
    starts = [sum(counts[:at]) for at in range(chunks)]
    spans = [((first, count), (half + first, count)) for first, count in zip(starts, counts)]
    tall, *early = weights(place, projection, master_t, updates, spans[0], block)
    own = [early]
    for span in spans[1:]:
        own.append(weights(place, projection, master_t, [tall], span, block))
    master_new = new_master(place, projection, master_t, tall, cols // 4)

    def hop(value, mask):
        return send(value, "dp", n_dp, mask)

    pairs, relays, own_relays, out = [], [], [], None
    shape = (cols, n_dp * slab_rows)
    for step in range(3 * chunks):
        phase, at = divmod(step, chunks)
        if phase < 2:
            both = (own[at][phase], own[at][1 - phase])
        else:
            both = (pairs[at][1], pairs[at][0])
        earlier = []
        if step >= 2:
            earlier += pairs[step - 2]
        if step >= 3:
            earlier += relays[step - 3]
            if step - 3 < chunks:
                earlier += own_relays[step - 3]
        if step == 2:
            earlier.append(master_new)
        both = lax.optimization_barrier((*both, *earlier))[:2]
        pair = (hop(both[0], 2), hop(both[1], 4))
        pairs.append(pair)
        if step < chunks:
            held = lax.optimization_barrier((*own[step], *pair))[:2]
            own_relays.append([hop(value, 1) for value in held])
        held = pair if out is None else lax.optimization_barrier((*pair, out))[:2]
        relays.append([hop(value, 1) for value in held])
        if phase == 2:
            from_x, from_y = pairs[at], pairs[chunks + at]
            over_x, over_y = relays[at], relays[chunks + at]
            first = (own[at][0], own_relays[at][0], from_x[0], over_x[0], from_y[1], over_y[1], pair[1], relays[step][1])
            second = (own[at][1], own_relays[at][1], from_y[0], over_y[0], from_x[1], over_x[1], pair[0], relays[step][0])
            masks = tuple(range(n_dp))
            placed = [(*spans[at][0], masks), (*spans[at][1], masks)]
            out = lay(place, out, shape, placed, first + second, block)
    return (moment_one_new, moment_two_new, master_new.T, out.T)


def solution(mesh):
    n_dp, n_fsdp = mesh.shape["dp"], mesh.shape["fsdp"]

    def body(acts, grad_out, projection, moment_one, moment_two, master):
        args = (acts, grad_out, projection, moment_one, moment_two, master)
        fits = n_dp == 8 and n_fsdp == 4 and moment_one.shape[0] % 32 == 0 and master.shape[0] % 128 == 0
        if fits and grad_out.shape[1] % 64 == 0 and acts.shape[0] % 128 == 0:
            return kernel_body(*args, n_dp, n_fsdp)
        return plain_body(*args)

    in_specs = (
        P(("dp", "fsdp"), None),
        P("dp", "fsdp"),
        P(),
        P("dp", "fsdp"),
        P("dp", "fsdp"),
        P("dp", "fsdp"),
    )
    out_specs = (P("dp", "fsdp"), P("dp", "fsdp"), P("dp", "fsdp"), P(None, "fsdp"))
    return jax.shard_map(body, mesh=mesh, in_specs=in_specs, out_specs=out_specs, check_vma=False)
```

```python
import functools

import jax
import jax.numpy as jnp
from jax import lax
from jax.experimental import pallas as pl
from jax.experimental.pallas import tpu as pltpu
from jax.sharding import PartitionSpec as P

STEP = 1000


BETA_ONE = 0.9
BETA_TWO = 0.999
ADAM_EPS = 1e-08
LEARN_RATE = 0.01
CORRECT_ONE = 1.0 - BETA_ONE**STEP
CORRECT_TWO = 1.0 - BETA_TWO**STEP

VMEM = pl.BlockSpec(memory_space=pltpu.VMEM)
ANY = pl.BlockSpec(memory_space=pl.ANY)


def adam(grad, moment_one, moment_two):
    moment_one_new = BETA_ONE * moment_one + (1.0 - BETA_ONE) * grad
    moment_two_new = BETA_TWO * moment_two + (1.0 - BETA_TWO) * grad * grad
    update = (
        moment_one_new / CORRECT_ONE / (jnp.sqrt(moment_two_new / CORRECT_TWO) + ADAM_EPS)
    ).astype(jnp.bfloat16)
    return moment_one_new, moment_two_new, update


def plain_body(acts, grad_out, projection, moment_one, moment_two, master):
    projected = jnp.dot(acts, projection, preferred_element_type=jnp.float32).astype(jnp.bfloat16)
    group_proj = lax.all_gather(projected, "fsdp", axis=0, tiled=True)
    partial_value = jnp.einsum(
        "tr,tc->rc", group_proj, grad_out, preferred_element_type=jnp.float32
    )
    partial_value = lax.optimization_barrier(partial_value.astype(jnp.bfloat16))
    grad = lax.psum_scatter(
        partial_value.astype(jnp.float32), "dp", scatter_dimension=0, tiled=True
    )
    moment_one_new, moment_two_new, update = adam(grad, moment_one, moment_two)
    slab_rows = master.shape[0]
    proj_slab = lax.dynamic_slice_in_dim(projection, lax.axis_index("dp") * slab_rows, slab_rows, 0)
    piece = lax.all_gather(update, "dp", axis=0, tiled=True)
    expanded = jnp.dot(proj_slab, piece, preferred_element_type=jnp.float32)
    master_new = master - LEARN_RATE * expanded
    weight_cols = lax.all_gather(master_new.astype(jnp.bfloat16), "dp", axis=0, tiled=True)
    return (moment_one_new, moment_two_new, master_new, weight_cols)


def send(value, axis, size, mask):
    return lax.ppermute(value, axis, [(i, i ^ mask) for i in range(size)])


def order(size):
    return (0, *reversed(range(1, size)))


def partial_kernel(grad_t, *refs):
    pieces, out, tokens = refs[:-2], refs[-2], refs[-1]
    count = pieces[0].shape[0]
    me = lax.axis_index("fsdp")
    for k, piece in zip(order(len(pieces)), pieces):
        tokens[pl.ds(pl.multiple_of((me ^ k) * count, count), count), :] = piece[...]
    out[...] = lax.dot_general(
        tokens[...].T, grad_t[...], (((1,), (1,)), ((), ())), preferred_element_type=jnp.float32
    ).astype(jnp.bfloat16)


def adam_kernel(moment_one, moment_two, parts, one_new, two_new, update):
    rows, cols = moment_one.shape
    grad = parts[:rows, :].astype(jnp.float32)
    for first in range(rows, parts.shape[0], rows):
        grad = grad + parts[first : first + rows, :].astype(jnp.float32)
    one, two, value = adam(grad, moment_one[...], moment_two[...])
    one_new[...] = one
    two_new[...] = two
    update[...] = jnp.zeros_like(update)
    update[:, :cols] = value


def expand(tall, slab, first, count):
    return lax.dot_general(
        tall[pl.ds(first, count), :], slab, (((1,), (1,)), ((), ())),
        preferred_element_type=jnp.float32,
    )


def weight_kernel(projection, master_t, *refs, n_in, spans, block):
    pieces, outs = refs[:n_in], refs[n_in:]
    me = lax.axis_index("dp")
    if n_in > 1:
        tall, wide = outs[0], outs[-1]
        outs = outs[1:-1]
        rows = pieces[0].shape[0]
        for k, piece in enumerate(pieces):
            wide[pl.ds(pl.multiple_of((me ^ k) * rows, rows), rows), :] = piece[...]
        tall[...] = wide[...].T
    else:
        tall = pieces[0]
    slab_rows = master_t.shape[1]
    slab = projection[pl.ds(pl.multiple_of(me * slab_rows, slab_rows), slab_rows), :]
    for (first, count), out in zip(spans, outs):
        for at in range(0, count, block):
            master_new = master_t[pl.ds(first + at, block), :] - LEARN_RATE * expand(
                tall, slab, first + at, block
            )
            out[pl.ds(at, block), :] = master_new.astype(jnp.bfloat16)


def weights(projection, master_t, pieces, spans, block):
    slab_rows, rank = master_t.shape[1], projection.shape[1]
    wide = pieces[0].shape[1]
    out_shape = [jax.ShapeDtypeStruct((count, slab_rows), jnp.bfloat16) for _, count in spans]
    scratch = []
    if len(pieces) > 1:
        out_shape = [jax.ShapeDtypeStruct((wide, rank), jnp.bfloat16)] + out_shape
        scratch = [pltpu.VMEM((rank, wide), jnp.bfloat16)]
    size = sum(count for _, count in spans) * slab_rows
    return pl.pallas_call(
        functools.partial(weight_kernel, n_in=len(pieces), spans=spans, block=block),
        out_shape=out_shape,
        in_specs=[VMEM] * (2 + len(pieces)),
        out_specs=[VMEM] * len(out_shape),
        scratch_shapes=scratch,
        compiler_params=pltpu.CompilerParams(vmem_limit_bytes=20 * 2**20),
        cost_estimate=pl.CostEstimate(flops=2 * size * rank, bytes_accessed=4 * size, transcendentals=0),
    )(projection, master_t, *pieces)


def master_kernel(projection, master_t, tall, out):
    slab_rows = master_t.shape[1]
    first = pl.multiple_of(lax.axis_index("dp") * slab_rows, slab_rows)
    slab = projection[pl.ds(first, slab_rows), :]
    block = master_t.shape[0]
    first = pl.multiple_of(pl.program_id(0) * block, block)
    out[...] = master_t[...] - LEARN_RATE * expand(tall, slab, first, block)


def new_master(projection, master_t, tall, block):
    cols, slab_rows = master_t.shape
    rank = projection.shape[1]
    return pl.pallas_call(
        master_kernel,
        out_shape=jax.ShapeDtypeStruct((cols, slab_rows), jnp.float32),
        grid=(cols // block,),
        in_specs=[
            pl.BlockSpec(projection.shape, lambda i: (0, 0)),
            pl.BlockSpec((block, slab_rows), lambda i: (i, 0)),
            pl.BlockSpec(tall.shape, lambda i: (0, 0)),
        ],
        out_specs=pl.BlockSpec((block, slab_rows), lambda i: (i, 0)),
        compiler_params=pltpu.CompilerParams(vmem_limit_bytes=20 * 2**20),
        cost_estimate=pl.CostEstimate(
            flops=2 * cols * slab_rows * rank, bytes_accessed=8 * cols * slab_rows, transcendentals=0
        ),
    )(projection, master_t, tall)


def lay_kernel(*refs, spans, block, fresh):
    refs = refs if fresh else refs[1:]
    n_in = sum(len(masks) for _, _, masks in spans)
    pieces, out, (held, sems) = refs[:n_in], refs[n_in], refs[n_in + 1 :]
    copies = [None] * held.shape[0]
    me = lax.axis_index("dp")
    core = me & 1
    at = 0
    base = 0
    for first, count, masks in spans:
        for start in range(0, count, block):
            slot = at % len(copies)
            if copies[slot] is not None:
                copies[slot].wait()
            for mask, piece in zip(masks, pieces[base : base + len(masks)]):
                width = piece.shape[1]
                mask = jnp.where(core == 0, mask[0], mask[1])
                column = pl.multiple_of((me ^ mask) * width, 128)
                origin = start if piece.shape[0] == count else first + start
                held[slot, :, pl.ds(column, width)] = piece[pl.ds(origin, block), :]
            copies[slot] = pltpu.make_async_copy(
                held.at[slot], out.at[pl.ds(first + start, block), :], sems.at[slot]
            )
            copies[slot].start()
            at += 1
        base += len(masks)
    for copy in copies:
        if copy is not None:
            copy.wait()


def lay(out, shape, spans, pieces, block):
    fresh = out is None
    held = [] if fresh else [out]
    size = sum(2 * 2 * piece.size for piece in pieces)
    return pl.pallas_call(
        functools.partial(lay_kernel, spans=spans, block=block, fresh=fresh),
        out_shape=jax.ShapeDtypeStruct(shape, jnp.bfloat16),
        in_specs=[ANY] * len(held) + [VMEM] * len(pieces),
        out_specs=ANY,
        scratch_shapes=[
            pltpu.VMEM((4, block, shape[1]), jnp.bfloat16),
            pltpu.SemaphoreType.DMA((4,)),
        ],
        input_output_aliases={} if fresh else {0: 0},
        compiler_params=pltpu.CompilerParams(vmem_limit_bytes=20 * 2**20),
        cost_estimate=pl.CostEstimate(flops=0, bytes_accessed=size, transcendentals=0),
    )(*held, *pieces)


def kernel_body(acts, grad_out, projection, moment_one, moment_two, master, n_dp, n_fsdp):
    cols = grad_out.shape[1]
    rank = projection.shape[1]
    rows = moment_one.shape[0]
    slab_rows = master.shape[0]
    wide = -(-cols // 128) * 128
    master_t = master.T

    projected = jnp.dot(acts, projection, preferred_element_type=jnp.float32).astype(jnp.bfloat16)
    tokens = [projected if k == 0 else send(projected, "fsdp", n_fsdp, k) for k in order(n_fsdp)]
    parts = pl.pallas_call(
        partial_kernel,
        out_shape=jax.ShapeDtypeStruct((rank, cols), jnp.bfloat16),
        in_specs=[VMEM] * (1 + n_fsdp),
        out_specs=VMEM,
        scratch_shapes=[pltpu.VMEM((n_fsdp * projected.shape[0], rank), jnp.bfloat16)],
        compiler_params=pltpu.CompilerParams(vmem_limit_bytes=16 * 2**20),
    )(grad_out.T, *tokens)
    parts = lax.all_to_all(parts, "dp", split_axis=0, concat_axis=0, tiled=True)
    moment_one_new, moment_two_new, update = pl.pallas_call(
        adam_kernel,
        out_shape=[
            jax.ShapeDtypeStruct(moment_one.shape, jnp.float32),
            jax.ShapeDtypeStruct(moment_two.shape, jnp.float32),
            jax.ShapeDtypeStruct((rows, wide), jnp.bfloat16),
        ],
        in_specs=[VMEM] * 3,
        out_specs=[VMEM] * 3,
        compiler_params=pltpu.CompilerParams(vmem_limit_bytes=16 * 2**20),
    )(moment_one, moment_two, parts)

    def hop(value, mask):
        return send(value, "dp", n_dp, mask)

    updates = {0: update}
    for k in (6, 2, 4, 1):
        updates[k] = hop(update, k)
    for k in (2, 4, 6):
        updates[k ^ 1] = hop(updates[k], 1)
    updates = [updates[k] for k in range(n_dp)]

    def turn(value, which):
        masks = [(2, 4)[(i & 1) ^ which] for i in range(n_dp)]
        return lax.ppermute(value, "dp", [(i, i ^ masks[i]) for i in range(n_dp)])

    half = cols // 2
    block = cols // 18
    counts = (4 * block, 3 * block, 2 * block)
    chunks = len(counts)
    starts = [sum(counts[:at]) for at in range(chunks)]
    spans = [((first, count), (half + first, count)) for first, count in zip(starts, counts)]
    tall, *early = weights(projection, master_t, updates, spans[0], block)
    late = [span for both in spans[1:] for span in both]
    *late, whole = weights(projection, master_t, [tall], late + [(0, cols)], block)
    own = [early] + [late[2 * at : 2 * at + 2] for at in range(chunks - 1)]
    master_new = new_master(projection, master_t, tall, cols // 4)

    def after(value, earlier):
        return lax.optimization_barrier((value, *earlier))[0] if earlier else value

    got, over = [], []
    out = None
    shape = (cols, n_dp * slab_rows)
    whole_c = hop(whole, 1)
    for step in range(6 * chunks):
        phase, rest = divmod(step, 2 * chunks)
        at, part = divmod(rest, 2)
        if phase == 0:
            value, which = own[at][part], part
        elif phase == 1:
            value, which = own[at][1 - part], part
        else:
            value, which = got[2 * at + part], 1 - part
        earlier = got[step - 3 : step - 2] if step >= 3 else []
        if step == 3:
            earlier += [whole_c, master_new]
        if step >= 5 and part == 1:
            earlier += over[step - 5 : step - 3]
        got.append(turn(after(value, earlier), which))
        if part == 1:
            for which in (step - 1, step):
                over.append(hop(after(got[which], got[step - 1 :] + ([] if out is None else [out])), 1))
        if phase == 2 and part == 1:
            laid, placed = [], []
            for part, (first, count) in enumerate(spans[at]):
                one, two = 2 * at + part, 2 * chunks + 2 * at + 1 - part
                three = 4 * chunks + 2 * at + part
                laid += [whole, whole_c, got[one], over[one], got[two], over[two], got[three], over[three]]
                masks = ((0, 0), (1, 1), (2, 4), (5, 3), (4, 2), (3, 5), (6, 6), (7, 7))
                if part == 1:
                    masks = ((0, 0), (1, 1), (4, 2), (3, 5), (2, 4), (5, 3), (6, 6), (7, 7))
                placed.append((first, count, masks))
            out = lay(out, shape, placed, laid, block)
    return (moment_one_new, moment_two_new, master_new.T, out.T)


def solution(mesh):
    n_dp, n_fsdp = mesh.shape["dp"], mesh.shape["fsdp"]

    def body(acts, grad_out, projection, moment_one, moment_two, master):
        args = (acts, grad_out, projection, moment_one, moment_two, master)
        fits = n_dp == 8 and n_fsdp == 4 and moment_one.shape[0] % 32 == 0 and master.shape[0] % 128 == 0
        if fits and grad_out.shape[1] % 64 == 0 and acts.shape[0] % 128 == 0:
            return kernel_body(*args, n_dp, n_fsdp)
        return plain_body(*args)

    in_specs = (
        P(("dp", "fsdp"), None),
        P("dp", "fsdp"),
        P(),
        P("dp", "fsdp"),
        P("dp", "fsdp"),
        P("dp", "fsdp"),
    )
    out_specs = (P("dp", "fsdp"), P("dp", "fsdp"), P("dp", "fsdp"), P(None, "fsdp"))
    return jax.shard_map(body, mesh=mesh, in_specs=in_specs, out_specs=out_specs, check_vma=False)
```

```python
import functools

import jax
import jax.numpy as jnp
from jax import lax
from jax.experimental import pallas as pl
from jax.experimental.pallas import tpu as pltpu
from jax.sharding import PartitionSpec as P

STEP = 1000


BETA_ONE = 0.9
BETA_TWO = 0.999
ADAM_EPS = 1e-08
LEARN_RATE = 0.01
CORRECT_ONE = 1.0 - BETA_ONE**STEP
CORRECT_TWO = 1.0 - BETA_TWO**STEP

VMEM = pl.BlockSpec(memory_space=pltpu.VMEM)
ANY = pl.BlockSpec(memory_space=pl.ANY)


def adam(grad, moment_one, moment_two):
    moment_one_new = BETA_ONE * moment_one + (1.0 - BETA_ONE) * grad
    moment_two_new = BETA_TWO * moment_two + (1.0 - BETA_TWO) * grad * grad
    update = (
        moment_one_new / CORRECT_ONE / (jnp.sqrt(moment_two_new / CORRECT_TWO) + ADAM_EPS)
    ).astype(jnp.bfloat16)
    return moment_one_new, moment_two_new, update


def plain_body(acts, grad_out, projection, moment_one, moment_two, master):
    projected = jnp.dot(acts, projection, preferred_element_type=jnp.float32).astype(jnp.bfloat16)
    group_proj = lax.all_gather(projected, "fsdp", axis=0, tiled=True)
    partial_value = jnp.einsum(
        "tr,tc->rc", group_proj, grad_out, preferred_element_type=jnp.float32
    )
    partial_value = lax.optimization_barrier(partial_value.astype(jnp.bfloat16))
    grad = lax.psum_scatter(
        partial_value.astype(jnp.float32), "dp", scatter_dimension=0, tiled=True
    )
    moment_one_new, moment_two_new, update = adam(grad, moment_one, moment_two)
    slab_rows = master.shape[0]
    proj_slab = lax.dynamic_slice_in_dim(projection, lax.axis_index("dp") * slab_rows, slab_rows, 0)
    piece = lax.all_gather(update, "dp", axis=0, tiled=True)
    expanded = jnp.dot(proj_slab, piece, preferred_element_type=jnp.float32)
    master_new = master - LEARN_RATE * expanded
    weight_cols = lax.all_gather(master_new.astype(jnp.bfloat16), "dp", axis=0, tiled=True)
    return (moment_one_new, moment_two_new, master_new, weight_cols)


def send(value, axis, size, mask):
    return lax.ppermute(value, axis, [(i, i ^ mask) for i in range(size)])


def project_kernel(acts, projection, out, total):
    step = pl.program_id(0)
    part = jnp.dot(acts[...], projection[...], preferred_element_type=jnp.float32)

    @pl.when(step == 0)
    def _():
        total[...] = part

    @pl.when(step > 0)
    def _():
        total[...] += part

    @pl.when(step == pl.num_programs(0) - 1)
    def _():
        out[...] = total[...].astype(jnp.bfloat16)


def project(acts, projection, depth):
    tokens, width = acts.shape
    rank = projection.shape[1]
    return pl.pallas_call(
        project_kernel,
        out_shape=jax.ShapeDtypeStruct((tokens, rank), jnp.bfloat16),
        grid=(width // depth,),
        in_specs=[
            pl.BlockSpec((tokens, depth), lambda i: (0, i)),
            pl.BlockSpec((depth, rank), lambda i: (i, 0)),
        ],
        out_specs=VMEM,
        scratch_shapes=[pltpu.VMEM((tokens, rank), jnp.float32)],
        compiler_params=pltpu.CompilerParams(vmem_limit_bytes=56 * 2**20),
        cost_estimate=pl.CostEstimate(
            flops=2 * tokens * width * rank, bytes_accessed=2 * (tokens + rank) * width, transcendentals=0
        ),
    )(acts, projection)


def partial_kernel(grad_t, *refs, n_fsdp, n_dp):
    pieces, outs, (tokens, across) = refs[:n_fsdp], refs[n_fsdp : n_fsdp + n_dp], refs[n_fsdp + n_dp :]
    count = pieces[0].shape[0]
    rows = outs[0].shape[0]
    me = lax.axis_index("fsdp")
    for k, piece in enumerate(pieces):
        tokens[pl.ds(pl.multiple_of((me ^ k) * count, count), count), :] = piece[...]
    across[...] = tokens[...].T
    me = lax.axis_index("dp")
    left = jnp.concatenate(
        [across[pl.ds(pl.multiple_of((me ^ k) * rows, rows), rows), :] for k in range(n_dp)], axis=0
    )
    result = lax.dot_general(
        left, grad_t[...], (((1,), (1,)), ((), ())), preferred_element_type=jnp.float32
    ).astype(jnp.bfloat16)
    for k, out in enumerate(outs):
        out[...] = result[k * rows : (k + 1) * rows, :]


def adam_kernel(moment_one, moment_two, *refs):
    parts, (one_new, two_new, update) = refs[:-3], refs[-3:]
    grad = parts[0][...].astype(jnp.float32)
    for part in parts[1:]:
        grad = grad + part[...].astype(jnp.float32)
    one, two, value = adam(grad, moment_one[...], moment_two[...])
    one_new[...] = one
    two_new[...] = two
    cols = value.shape[1]
    update[...] = jnp.zeros_like(update)
    update[:, :cols] = value


def expand(tall, slab, first, count):
    return lax.dot_general(
        tall[pl.ds(first, count), :], slab, (((1,), (1,)), ((), ())),
        preferred_element_type=jnp.float32,
    )


def weight_kernel(projection, master_t, *refs, n_in, spans, block):
    pieces, outs = refs[:n_in], refs[n_in:]
    me = lax.axis_index("dp")
    if n_in > 1:
        tall, wide = outs[0], outs[-1]
        outs = outs[1:-1]
        rows = pieces[0].shape[0]
        for k, piece in enumerate(pieces):
            wide[pl.ds(pl.multiple_of((me ^ k) * rows, rows), rows), :] = piece[...]
        tall[...] = wide[...].T
    else:
        tall = pieces[0]
    slab_rows = master_t.shape[1]
    slab = projection[pl.ds(pl.multiple_of(me * slab_rows, slab_rows), slab_rows), :]
    for (first, count), out in zip(spans, outs):
        for at in range(0, count, block):
            master_new = master_t[pl.ds(first + at, block), :] - LEARN_RATE * expand(
                tall, slab, first + at, block
            )
            out[pl.ds(at, block), :] = master_new.astype(jnp.bfloat16)


def weights(projection, master_t, pieces, spans, block):
    slab_rows, rank = master_t.shape[1], projection.shape[1]
    wide = pieces[0].shape[1]
    out_shape = [jax.ShapeDtypeStruct((count, slab_rows), jnp.bfloat16) for _, count in spans]
    scratch = []
    if len(pieces) > 1:
        out_shape = [jax.ShapeDtypeStruct((wide, rank), jnp.bfloat16)] + out_shape
        scratch = [pltpu.VMEM((rank, wide), jnp.bfloat16)]
    size = sum(count for _, count in spans) * slab_rows
    return pl.pallas_call(
        functools.partial(weight_kernel, n_in=len(pieces), spans=spans, block=block),
        out_shape=out_shape,
        in_specs=[VMEM] * (2 + len(pieces)),
        out_specs=[VMEM] * len(out_shape),
        scratch_shapes=scratch,
        compiler_params=pltpu.CompilerParams(vmem_limit_bytes=20 * 2**20),
        cost_estimate=pl.CostEstimate(flops=2 * size * rank, bytes_accessed=4 * size, transcendentals=0),
    )(projection, master_t, *pieces)


def master_kernel(projection, master_t, tall, out):
    slab_rows = master_t.shape[1]
    first = pl.multiple_of(lax.axis_index("dp") * slab_rows, slab_rows)
    slab = projection[pl.ds(first, slab_rows), :]
    block = master_t.shape[0]
    first = pl.multiple_of(pl.program_id(0) * block, block)
    out[...] = master_t[...] - LEARN_RATE * expand(tall, slab, first, block)


def new_master(projection, master_t, tall, block):
    cols, slab_rows = master_t.shape
    rank = projection.shape[1]
    return pl.pallas_call(
        master_kernel,
        out_shape=jax.ShapeDtypeStruct((cols, slab_rows), jnp.float32),
        grid=(cols // block,),
        in_specs=[
            pl.BlockSpec(projection.shape, lambda i: (0, 0)),
            pl.BlockSpec((block, slab_rows), lambda i: (i, 0)),
            pl.BlockSpec(tall.shape, lambda i: (0, 0)),
        ],
        out_specs=pl.BlockSpec((block, slab_rows), lambda i: (i, 0)),
        compiler_params=pltpu.CompilerParams(vmem_limit_bytes=20 * 2**20),
        cost_estimate=pl.CostEstimate(
            flops=2 * cols * slab_rows * rank, bytes_accessed=8 * cols * slab_rows, transcendentals=0
        ),
    )(projection, master_t, tall)


def lay_kernel(*refs, spans, block, fresh):
    refs = refs if fresh else refs[1:]
    n_in = sum(len(masks) for _, _, masks in spans)
    pieces, out, (held, sems) = refs[:n_in], refs[n_in], refs[n_in + 1 :]
    copies = [None] * held.shape[0]
    me = lax.axis_index("dp")
    core = me & 1
    at = 0
    base = 0
    for first, count, masks in spans:
        for start in range(0, count, block):
            slot = at % len(copies)
            if copies[slot] is not None:
                copies[slot].wait()
            for mask, piece in zip(masks, pieces[base : base + len(masks)]):
                width = piece.shape[1]
                mask = jnp.where(core == 0, mask[0], mask[1])
                column = pl.multiple_of((me ^ mask) * width, 128)
                origin = start if piece.shape[0] == count else first + start
                held[slot, :, pl.ds(column, width)] = piece[pl.ds(origin, block), :]
            copies[slot] = pltpu.make_async_copy(
                held.at[slot], out.at[pl.ds(first + start, block), :], sems.at[slot]
            )
            copies[slot].start()
            at += 1
        base += len(masks)
    for copy in copies:
        if copy is not None:
            copy.wait()


def lay(out, shape, spans, pieces, block):
    fresh = out is None
    held = [] if fresh else [out]
    size = sum(2 * 2 * piece.size for piece in pieces)
    return pl.pallas_call(
        functools.partial(lay_kernel, spans=spans, block=block, fresh=fresh),
        out_shape=jax.ShapeDtypeStruct(shape, jnp.bfloat16),
        in_specs=[ANY] * len(held) + [VMEM] * len(pieces),
        out_specs=ANY,
        scratch_shapes=[
            pltpu.VMEM((4, block, shape[1]), jnp.bfloat16),
            pltpu.SemaphoreType.DMA((4,)),
        ],
        input_output_aliases={} if fresh else {0: 0},
        compiler_params=pltpu.CompilerParams(vmem_limit_bytes=20 * 2**20),
        cost_estimate=pl.CostEstimate(flops=0, bytes_accessed=size, transcendentals=0),
    )(*held, *pieces)


def kernel_body(acts, grad_out, projection, moment_one, moment_two, master, n_dp, n_fsdp):
    cols = grad_out.shape[1]
    rank = projection.shape[1]
    rows = moment_one.shape[0]
    slab_rows = master.shape[0]
    wide = -(-cols // 128) * 128
    master_t = master.T

    projected = project(acts, projection, acts.shape[1] // 5)
    tokens = [projected] + [send(projected, "fsdp", n_fsdp, k) for k in range(1, n_fsdp)]
    parts = pl.pallas_call(
        functools.partial(partial_kernel, n_fsdp=n_fsdp, n_dp=n_dp),
        out_shape=[jax.ShapeDtypeStruct((rows, cols), jnp.bfloat16)] * n_dp,
        in_specs=[VMEM] * (1 + n_fsdp),
        out_specs=[VMEM] * n_dp,
        scratch_shapes=[
            pltpu.VMEM((n_fsdp * projected.shape[0], rank), jnp.bfloat16),
            pltpu.VMEM((rank, n_fsdp * projected.shape[0]), jnp.bfloat16),
        ],
        compiler_params=pltpu.CompilerParams(vmem_limit_bytes=16 * 2**20),
    )(grad_out.T, *tokens)
    parts = [parts[k] if k == 0 else send(parts[k], "dp", n_dp, k) for k in (0, 2, 4, 6, 7, 3, 5, 1)]
    moment_one_new, moment_two_new, update = pl.pallas_call(
        adam_kernel,
        out_shape=[
            jax.ShapeDtypeStruct(moment_one.shape, jnp.float32),
            jax.ShapeDtypeStruct(moment_two.shape, jnp.float32),
            jax.ShapeDtypeStruct((rows, wide), jnp.bfloat16),
        ],
        in_specs=[VMEM] * (2 + n_dp),
        out_specs=[VMEM] * 3,
        compiler_params=pltpu.CompilerParams(vmem_limit_bytes=16 * 2**20),
    )(moment_one, moment_two, *parts)

    def hop(value, mask):
        return send(value, "dp", n_dp, mask)

    updates = {0: update}
    for k in (6, 2, 4, 1):
        updates[k] = hop(update, k)
    for k in (2, 4, 6):
        updates[k ^ 1] = hop(updates[k], 1)
    updates = [updates[k] for k in range(n_dp)]

    def turn(value, which):
        masks = [(2, 4)[(i & 1) ^ which] for i in range(n_dp)]
        return lax.ppermute(value, "dp", [(i, i ^ masks[i]) for i in range(n_dp)])

    half = cols // 2
    block = cols // 12
    counts = (3 * block, 3 * block)
    chunks = len(counts)
    starts = [sum(counts[:at]) for at in range(chunks)]
    spans = [((first, count), (half + first, count)) for first, count in zip(starts, counts)]
    tall, *early = weights(projection, master_t, updates, spans[0], block)
    late = [span for both in spans[1:] for span in both]
    late = weights(projection, master_t, [tall], late, block)
    own = [early] + [late[2 * at : 2 * at + 2] for at in range(chunks - 1)]
    master_new = new_master(projection, master_t, tall, cols // 4)

    def after(value, earlier):
        return lax.optimization_barrier((value, *earlier))[0] if earlier else value

    got, over = [], []
    out = None
    shape = (cols, n_dp * slab_rows)
    for step in range(6 * chunks):
        phase, rest = divmod(step, 2 * chunks)
        at, part = divmod(rest, 2)
        if phase == 0:
            value, which = own[at][part], part
        elif phase == 1:
            value, which = own[at][1 - part], part
        else:
            value, which = got[2 * at + part], 1 - part
        earlier = got[step - 2 : step - 1] if step >= 2 else []
        earlier += over[step - 4 : step - 3] if step >= 4 else []
        if step == 4:
            earlier.append(master_new)
        if step == 10:
            earlier.append(whole_c)
        got.append(turn(after(value, earlier), which))
        over.append(hop(after(got[step], [] if out is None else [out]), 1))
        if step == 0:
            (whole,) = weights(projection, master_t, [after(tall, got)], [(0, cols)], block)
            whole_c = hop(whole, 1)
        if phase == 2 and part == 1:
            laid, placed = [], []
            for part, (first, count) in enumerate(spans[at]):
                one, two = 2 * at + part, 2 * chunks + 2 * at + 1 - part
                three = 4 * chunks + 2 * at + part
                laid += [whole, whole_c, got[one], over[one], got[two], over[two], got[three], over[three]]
                masks = ((0, 0), (1, 1), (2, 4), (5, 3), (4, 2), (3, 5), (6, 6), (7, 7))
                if part == 1:
                    masks = ((0, 0), (1, 1), (4, 2), (3, 5), (2, 4), (5, 3), (6, 6), (7, 7))
                placed.append((first, count, masks))
            out = lay(out, shape, placed, laid, block // 2 if block % 32 == 0 else block)
    return (moment_one_new, moment_two_new, master_new.T, out.T)


def solution(mesh):
    n_dp, n_fsdp = mesh.shape["dp"], mesh.shape["fsdp"]

    def body(acts, grad_out, projection, moment_one, moment_two, master):
        args = (acts, grad_out, projection, moment_one, moment_two, master)
        fits = n_dp == 8 and n_fsdp == 4 and moment_one.shape[0] % 32 == 0 and master.shape[0] % 128 == 0
        if fits and grad_out.shape[1] % 64 == 0 and acts.shape[0] % 128 == 0:
            return kernel_body(*args, n_dp, n_fsdp)
        return plain_body(*args)

    in_specs = (
        P(("dp", "fsdp"), None),
        P("dp", "fsdp"),
        P(),
        P("dp", "fsdp"),
        P("dp", "fsdp"),
        P("dp", "fsdp"),
    )
    out_specs = (P("dp", "fsdp"), P("dp", "fsdp"), P("dp", "fsdp"), P(None, "fsdp"))
    return jax.shard_map(body, mesh=mesh, in_specs=in_specs, out_specs=out_specs, check_vma=False)
```

```python
import functools

import jax
import jax.numpy as jnp
from jax import lax
from jax.experimental import pallas as pl
from jax.experimental.pallas import tpu as pltpu
from jax.sharding import PartitionSpec as P

STEP = 1000


BETA_ONE = 0.9
BETA_TWO = 0.999
ADAM_EPS = 1e-08
LEARN_RATE = 0.01
CORRECT_ONE = 1.0 - BETA_ONE**STEP
CORRECT_TWO = 1.0 - BETA_TWO**STEP

VMEM = pl.BlockSpec(memory_space=pltpu.VMEM)
ANY = pl.BlockSpec(memory_space=pl.ANY)


TURN_MASKS = ((2, 4), (4, 2))
OWNER_MASKS = ((0, 0), (1, 1), (2, 4), (5, 3), (4, 2), (3, 5), (6, 6), (7, 7))


def chunk_sizes(cols):
    rest = -(-cols * 7 // 18 // 16) * 16
    return (cols - 2 * rest, rest, rest)


def adam(grad, moment_one, moment_two):
    moment_one_new = BETA_ONE * moment_one + (1.0 - BETA_ONE) * grad
    moment_two_new = BETA_TWO * moment_two + (1.0 - BETA_TWO) * grad * grad
    update = (
        moment_one_new / CORRECT_ONE / (jnp.sqrt(moment_two_new / CORRECT_TWO) + ADAM_EPS)
    ).astype(jnp.bfloat16)
    return moment_one_new, moment_two_new, update


def plain_body(acts, grad_out, projection, moment_one, moment_two, master):
    projected = jnp.dot(acts, projection, preferred_element_type=jnp.float32).astype(jnp.bfloat16)
    group_proj = lax.all_gather(projected, "fsdp", axis=0, tiled=True)
    partial_value = jnp.einsum(
        "tr,tc->rc", group_proj, grad_out, preferred_element_type=jnp.float32
    )
    partial_value = lax.optimization_barrier(partial_value.astype(jnp.bfloat16))
    grad = lax.psum_scatter(
        partial_value.astype(jnp.float32), "dp", scatter_dimension=0, tiled=True
    )
    moment_one_new, moment_two_new, update = adam(grad, moment_one, moment_two)
    slab_rows = master.shape[0]
    proj_slab = lax.dynamic_slice_in_dim(projection, lax.axis_index("dp") * slab_rows, slab_rows, 0)
    piece = lax.all_gather(update, "dp", axis=0, tiled=True)
    expanded = jnp.dot(proj_slab, piece, preferred_element_type=jnp.float32)
    master_new = master - LEARN_RATE * expanded
    weight_cols = lax.all_gather(master_new.astype(jnp.bfloat16), "dp", axis=0, tiled=True)
    return (moment_one_new, moment_two_new, master_new, weight_cols)


def send(value, axis, size, mask):
    return lax.ppermute(value, axis, [(i, i ^ mask) for i in range(size)])


def take_kernel(source, out, sem):
    copy = pltpu.make_async_copy(source.at[pl.ds(0, out.shape[0]), :], out, sem)
    copy.start()
    copy.wait()


def take(array, count):
    return pl.pallas_call(
        take_kernel,
        out_shape=jax.ShapeDtypeStruct((count, array.shape[1]), array.dtype),
        in_specs=[ANY],
        out_specs=VMEM,
        scratch_shapes=[pltpu.SemaphoreType.DMA],
        compiler_params=pltpu.CompilerParams(vmem_limit_bytes=60 * 2**20),
    )(array)


def partial_kernel(grad_t, *refs, n_fsdp, n_dp):
    pieces, outs, (tokens, across) = refs[:n_fsdp], refs[n_fsdp : n_fsdp + n_dp], refs[n_fsdp + n_dp :]
    count = pieces[0].shape[0]
    rows = outs[0].shape[0]
    me = lax.axis_index("fsdp")
    for k, piece in enumerate(pieces):
        tokens[pl.ds(pl.multiple_of((me ^ k) * count, count), count), :] = piece[...]
    across[...] = tokens[...].T
    me = lax.axis_index("dp")
    left = jnp.concatenate(
        [across[pl.ds(pl.multiple_of((me ^ k) * rows, rows), rows), :] for k in range(n_dp)], axis=0
    )
    result = lax.dot_general(
        left, grad_t[...], (((1,), (1,)), ((), ())), preferred_element_type=jnp.float32
    ).astype(jnp.bfloat16)
    for k, out in enumerate(outs):
        out[...] = result[k * rows : (k + 1) * rows, :]


def adam_kernel(moment_one, moment_two, *refs):
    parts, (one_new, two_new, update) = refs[:-3], refs[-3:]
    grad = parts[0][...].astype(jnp.float32)
    for part in parts[1:]:
        grad = grad + part[...].astype(jnp.float32)
    one, two, value = adam(grad, moment_one[...], moment_two[...])
    one_new[...] = one
    two_new[...] = two
    cols = value.shape[1]
    update[...] = jnp.zeros_like(update)
    update[:, :cols] = value


def expand(tall, slab, first, count):
    return lax.dot_general(
        tall[pl.ds(first, count), :], slab, (((1,), (1,)), ((), ())),
        preferred_element_type=jnp.float32,
    )


def weight_kernel(projection, master_t, *refs, n_in, masks, spans, block):
    pieces, outs = refs[:n_in], refs[n_in:]
    me = lax.axis_index("dp")
    if n_in > 1:
        tall, wide = outs[0], outs[-1]
        outs = outs[1:-1]
        rows = pieces[0].shape[0]
        for k, piece in enumerate(pieces):
            wide[pl.ds(pl.multiple_of((me ^ k) * rows, rows), rows), :] = piece[...]
        tall[...] = wide[...].T
    else:
        tall = pieces[0]
    slab_rows = master_t.shape[1]
    owner = me ^ jnp.where((me & 1) == 0, masks[0], masks[1])
    slab = projection[pl.ds(pl.multiple_of(owner * slab_rows, slab_rows), slab_rows), :]
    for (first, count), out in zip(spans, outs):
        for at in range(0, count, block):
            size = min(block, count - at)
            master_new = master_t[pl.ds(first + at, size), :] - LEARN_RATE * expand(
                tall, slab, first + at, size
            )
            out[pl.ds(at, size), :] = master_new.astype(jnp.bfloat16)


def weights(projection, master_t, pieces, spans, masks=(0, 0)):
    slab_rows, rank = master_t.shape[1], projection.shape[1]
    wide = pieces[0].shape[1]
    out_shape = [jax.ShapeDtypeStruct((count, slab_rows), jnp.bfloat16) for _, count in spans]
    scratch = []
    if len(pieces) > 1:
        out_shape = [jax.ShapeDtypeStruct((wide, rank), jnp.bfloat16)] + out_shape
        scratch = [pltpu.VMEM((rank, wide), jnp.bfloat16)]
    size = sum(count for _, count in spans) * slab_rows
    return pl.pallas_call(
        functools.partial(weight_kernel, n_in=len(pieces), masks=masks, spans=spans, block=144),
        out_shape=out_shape,
        in_specs=[VMEM] * (2 + len(pieces)),
        out_specs=[VMEM] * len(out_shape),
        scratch_shapes=scratch,
        compiler_params=pltpu.CompilerParams(vmem_limit_bytes=20 * 2**20),
        cost_estimate=pl.CostEstimate(flops=2 * size * rank, bytes_accessed=4 * size, transcendentals=0),
    )(projection, master_t, *pieces)


def master_kernel(projection, master_t, tall, out):
    slab_rows = master_t.shape[1]
    first = pl.multiple_of(lax.axis_index("dp") * slab_rows, slab_rows)
    slab = projection[pl.ds(first, slab_rows), :]
    block = master_t.shape[0]
    first = pl.multiple_of(pl.program_id(0) * block, block)
    out[...] = master_t[...] - LEARN_RATE * expand(tall, slab, first, block)


def new_master(projection, master_t, tall, block):
    cols, slab_rows = master_t.shape
    rank = projection.shape[1]
    return pl.pallas_call(
        master_kernel,
        out_shape=jax.ShapeDtypeStruct((cols, slab_rows), jnp.float32),
        grid=(cols // block,),
        in_specs=[
            pl.BlockSpec(projection.shape, lambda i: (0, 0)),
            pl.BlockSpec((block, slab_rows), lambda i: (i, 0)),
            pl.BlockSpec(tall.shape, lambda i: (0, 0)),
        ],
        out_specs=pl.BlockSpec((block, slab_rows), lambda i: (i, 0)),
        compiler_params=pltpu.CompilerParams(vmem_limit_bytes=20 * 2**20),
        cost_estimate=pl.CostEstimate(
            flops=2 * cols * slab_rows * rank, bytes_accessed=8 * cols * slab_rows, transcendentals=0
        ),
    )(projection, master_t, tall)


def lay_kernel(*refs, first, count, block, fresh):
    refs = refs if fresh else refs[1:]
    pieces, out, (held, sems) = refs[:-3], refs[-3], refs[-2:]
    copies = [None] * held.shape[0]
    me = lax.axis_index("dp")
    core = me & 1
    for at in range(0, count, block):
        slot = at // block % len(copies)
        size = min(block, count - at)
        if copies[slot] is not None:
            copies[slot].wait()
        for masks, piece in zip(OWNER_MASKS, pieces):
            width = piece.shape[1]
            column = pl.multiple_of((me ^ jnp.where(core == 0, masks[0], masks[1])) * width, 128)
            origin = at if piece.shape[0] == count else first + at
            held[slot, pl.ds(0, size), pl.ds(column, width)] = piece[pl.ds(origin, size), :]
        copies[slot] = pltpu.make_async_copy(
            held.at[slot, pl.ds(0, size), :], out.at[pl.ds(first + at, size), :], sems.at[slot]
        )
        copies[slot].start()
    for copy in copies:
        if copy is not None:
            copy.wait()


def lay(out, shape, span, pieces, block=96):
    fresh = out is None
    held = [] if fresh else [out]
    first, count = span
    return pl.pallas_call(
        functools.partial(lay_kernel, first=first, count=count, block=block, fresh=fresh),
        out_shape=jax.ShapeDtypeStruct(shape, jnp.bfloat16),
        in_specs=[ANY] * len(held) + [VMEM] * len(pieces),
        out_specs=ANY,
        scratch_shapes=[
            pltpu.VMEM((4, block, shape[1]), jnp.bfloat16),
            pltpu.SemaphoreType.DMA((4,)),
        ],
        input_output_aliases={} if fresh else {0: 0},
        compiler_params=pltpu.CompilerParams(vmem_limit_bytes=20 * 2**20),
        cost_estimate=pl.CostEstimate(flops=0, bytes_accessed=4 * count * shape[1], transcendentals=0),
    )(*held, *pieces)


def kernel_body(acts, grad_out, projection, moment_one, moment_two, master, n_dp, n_fsdp):
    cols = grad_out.shape[1]
    rank = projection.shape[1]
    rows = moment_one.shape[0]
    slab_rows = master.shape[0]
    wide = -(-cols // 128) * 128
    master_t = master.T

    def hop(value, mask):
        return send(value, "dp", n_dp, mask)

    def turn(value, which):
        masks = [TURN_MASKS[which][i & 1] for i in range(n_dp)]
        return lax.ppermute(value, "dp", [(i, i ^ masks[i]) for i in range(n_dp)])

    def after(value, earlier):
        return lax.optimization_barrier((value, *earlier))[0] if earlier else value

    counts = chunk_sizes(cols)
    chunks = len(counts)
    spans = [(sum(counts[:at]), count) for at, count in enumerate(counts)]
    taken = take(master_t, counts[0])
    ahead = turn(taken, 0)
    acts = after(acts, [taken])

    projected = jnp.dot(acts, projection, preferred_element_type=jnp.float32).astype(jnp.bfloat16)
    tokens = [projected] + [send(projected, "fsdp", n_fsdp, k) for k in range(1, n_fsdp)]
    parts = pl.pallas_call(
        functools.partial(partial_kernel, n_fsdp=n_fsdp, n_dp=n_dp),
        out_shape=[jax.ShapeDtypeStruct((rows, cols), jnp.bfloat16)] * n_dp,
        in_specs=[VMEM] * (1 + n_fsdp),
        out_specs=[VMEM] * n_dp,
        scratch_shapes=[
            pltpu.VMEM((n_fsdp * projected.shape[0], rank), jnp.bfloat16),
            pltpu.VMEM((rank, n_fsdp * projected.shape[0]), jnp.bfloat16),
        ],
        compiler_params=pltpu.CompilerParams(vmem_limit_bytes=16 * 2**20),
    )(grad_out.T, *tokens)
    parts = lax.optimization_barrier((*parts, ahead))[:-1]
    parts = [parts[k] if k == 0 else send(parts[k], "dp", n_dp, k) for k in (0, 2, 4, 6, 7, 3, 5, 1)]
    moment_one_new, moment_two_new, update = pl.pallas_call(
        adam_kernel,
        out_shape=[
            jax.ShapeDtypeStruct(moment_one.shape, jnp.float32),
            jax.ShapeDtypeStruct(moment_two.shape, jnp.float32),
            jax.ShapeDtypeStruct((rows, wide), jnp.bfloat16),
        ],
        in_specs=[VMEM] * (2 + n_dp),
        out_specs=[VMEM] * 3,
        compiler_params=pltpu.CompilerParams(vmem_limit_bytes=16 * 2**20),
    )(moment_one, moment_two, *parts)

    updates = {0: update}
    for k in (6, 2, 4, 1):
        updates[k] = hop(update, k)
    for k in (2, 4, 6):
        updates[k ^ 1] = hop(updates[k], 1)
    updates = [updates[k] for k in range(n_dp)]

    tall, *own = weights(projection, master_t, updates, spans[1:])
    own_last, whole = weights(projection, master_t, [tall], spans[:1] + [(0, cols)])
    own = [own_last] + own
    (ahead_got,) = weights(projection, ahead, [tall], spans[:1], TURN_MASKS[0])
    ahead_over = hop(ahead_got, 1)
    master_new = new_master(projection, master_t, tall, cols // 4)

    later = range(1, chunks)
    steps = [(0, at) for at in later] + [(1, at) for at in later] + [(2, at) for at in later] + [(1, 0), (2, 0)]
    got, over = {(0, 0): ahead_got}, {(0, 0): ahead_over}
    outs = [None]
    for step, (phase, at) in enumerate(steps):
        value = got[(0, at)] if phase == 2 else own[at]
        earlier = [got[steps[step - 2]]] if step >= 2 else []
        earlier += [over[steps[step - 4]]] if step >= 4 else []
        if step == 2:
            earlier.append(master_new)
        got[(phase, at)] = turn(after(value, earlier), min(phase, 1))
        held = outs[step - len(steps) + 3 : step - len(steps) + 4] if step >= len(steps) - 2 else []
        over[(phase, at)] = hop(after(got[(phase, at)], held), 1)
        if step == 1:
            whole_c = hop(after(whole, [got[steps[1]]]), 1)
        if phase == 2:
            pieces = [whole, whole_c]
            for which in range(3):
                pieces += [got[(which, at)], over[(which, at)]]
            outs.append(lay(outs[-1], (cols, n_dp * slab_rows), spans[at], pieces))
    return (moment_one_new, moment_two_new, master_new.T, outs[-1].T)


def solution(mesh):
    n_dp, n_fsdp = mesh.shape["dp"], mesh.shape["fsdp"]

    def body(acts, grad_out, projection, moment_one, moment_two, master):
        args = (acts, grad_out, projection, moment_one, moment_two, master)
        fits = n_dp == 8 and n_fsdp == 4 and moment_one.shape[0] % 32 == 0 and master.shape[0] % 128 == 0
        if fits and grad_out.shape[1] % 64 == 0 and acts.shape[0] % 128 == 0:
            return kernel_body(*args, n_dp, n_fsdp)
        return plain_body(*args)

    in_specs = (
        P(("dp", "fsdp"), None),
        P("dp", "fsdp"),
        P(),
        P("dp", "fsdp"),
        P("dp", "fsdp"),
        P("dp", "fsdp"),
    )
    out_specs = (P("dp", "fsdp"), P("dp", "fsdp"), P("dp", "fsdp"), P(None, "fsdp"))
    return jax.shard_map(body, mesh=mesh, in_specs=in_specs, out_specs=out_specs, check_vma=False)
```

```python
import functools

import jax
import jax.numpy as jnp
from jax import lax
from jax.experimental import pallas as pl
from jax.experimental.pallas import tpu as pltpu
from jax.sharding import PartitionSpec as P

STEP = 1000


BETA_ONE = 0.9
BETA_TWO = 0.999
ADAM_EPS = 1e-08
LEARN_RATE = 0.01
CORRECT_ONE = 1.0 - BETA_ONE**STEP
CORRECT_TWO = 1.0 - BETA_TWO**STEP

VMEM = pl.BlockSpec(memory_space=pltpu.VMEM)
ANY = pl.BlockSpec(memory_space=pl.ANY)


TURN_MASKS = ((2, 4), (4, 2))
OWNER_MASKS = ((0, 0), (1, 1), (2, 4), (5, 3), (4, 2), (3, 5), (6, 6), (7, 7))


def chunk_sizes(cols):
    rest = cols // 80 * 16
    return (cols - 4 * rest, rest, rest, rest, rest)


def adam(grad, moment_one, moment_two):
    moment_one_new = BETA_ONE * moment_one + (1.0 - BETA_ONE) * grad
    moment_two_new = BETA_TWO * moment_two + (1.0 - BETA_TWO) * grad * grad
    update = (
        moment_one_new / CORRECT_ONE / (jnp.sqrt(moment_two_new / CORRECT_TWO) + ADAM_EPS)
    ).astype(jnp.bfloat16)
    return moment_one_new, moment_two_new, update


def plain_body(acts, grad_out, projection, moment_one, moment_two, master):
    projected = jnp.dot(acts, projection, preferred_element_type=jnp.float32).astype(jnp.bfloat16)
    group_proj = lax.all_gather(projected, "fsdp", axis=0, tiled=True)
    partial_value = jnp.einsum(
        "tr,tc->rc", group_proj, grad_out, preferred_element_type=jnp.float32
    )
    partial_value = lax.optimization_barrier(partial_value.astype(jnp.bfloat16))
    grad = lax.psum_scatter(
        partial_value.astype(jnp.float32), "dp", scatter_dimension=0, tiled=True
    )
    moment_one_new, moment_two_new, update = adam(grad, moment_one, moment_two)
    slab_rows = master.shape[0]
    proj_slab = lax.dynamic_slice_in_dim(projection, lax.axis_index("dp") * slab_rows, slab_rows, 0)
    piece = lax.all_gather(update, "dp", axis=0, tiled=True)
    expanded = jnp.dot(proj_slab, piece, preferred_element_type=jnp.float32)
    master_new = master - LEARN_RATE * expanded
    weight_cols = lax.all_gather(master_new.astype(jnp.bfloat16), "dp", axis=0, tiled=True)
    return (moment_one_new, moment_two_new, master_new, weight_cols)


def send(value, axis, size, mask):
    return lax.ppermute(value, axis, [(i, i ^ mask) for i in range(size)])


def take_kernel(source, out, sems):
    count = out.shape[0] // sems.shape[0]
    copies = []
    for at in range(sems.shape[0]):
        rows = pl.ds(at * count, count)
        copies.append(pltpu.make_async_copy(source.at[rows, :], out.at[rows, :], sems.at[at]))
    for copy in copies:
        copy.start()
    for copy in copies:
        copy.wait()


def take(array, count):
    return pl.pallas_call(
        take_kernel,
        out_shape=jax.ShapeDtypeStruct((count, array.shape[1]), array.dtype),
        in_specs=[ANY],
        out_specs=VMEM,
        scratch_shapes=[pltpu.SemaphoreType.DMA((count // 16,))],
        compiler_params=pltpu.CompilerParams(vmem_limit_bytes=60 * 2**20),
    )(array)


def partial_kernel(grad_t, *refs, n_fsdp, n_dp):
    pieces, outs, (tokens, across) = refs[:n_fsdp], refs[n_fsdp : n_fsdp + n_dp], refs[n_fsdp + n_dp :]
    count = pieces[0].shape[0]
    rows = outs[0].shape[0]
    me = lax.axis_index("fsdp")
    for k, piece in enumerate(pieces):
        tokens[pl.ds(pl.multiple_of((me ^ k) * count, count), count), :] = piece[...]
    across[...] = tokens[...].T
    me = lax.axis_index("dp")
    left = jnp.concatenate(
        [across[pl.ds(pl.multiple_of((me ^ k) * rows, rows), rows), :] for k in range(n_dp)], axis=0
    )
    result = lax.dot_general(
        left, grad_t[...], (((1,), (1,)), ((), ())), preferred_element_type=jnp.float32
    ).astype(jnp.bfloat16)
    for k, out in enumerate(outs):
        out[...] = result[k * rows : (k + 1) * rows, :]


def adam_kernel(moment_one, moment_two, *refs):
    parts, (one_new, two_new, update) = refs[:-3], refs[-3:]
    grad = parts[0][...].astype(jnp.float32)
    for part in parts[1:]:
        grad = grad + part[...].astype(jnp.float32)
    one, two, value = adam(grad, moment_one[...], moment_two[...])
    one_new[...] = one
    two_new[...] = two
    cols = value.shape[1]
    update[...] = jnp.zeros_like(update)
    update[:, :cols] = value


def expand(tall, slab, first, count):
    return lax.dot_general(
        tall[pl.ds(first, count), :], slab, (((1,), (1,)), ((), ())),
        preferred_element_type=jnp.float32,
    )


def weight_kernel(projection, master_t, *refs, n_in, masks, spans, block):
    pieces, outs = refs[:n_in], refs[n_in:]
    me = lax.axis_index("dp")
    if n_in > 1:
        tall, wide = outs[0], outs[-1]
        outs = outs[1:-1]
        rows = pieces[0].shape[0]
        for piece_masks, piece in zip(OWNER_MASKS, pieces):
            owner = me ^ jnp.where((me & 1) == 0, piece_masks[0], piece_masks[1])
            wide[pl.ds(pl.multiple_of(owner * rows, rows), rows), :] = piece[...]
        tall[...] = wide[...].T
    else:
        tall = pieces[0]
    slab_rows = master_t.shape[1]
    owner = me ^ jnp.where((me & 1) == 0, masks[0], masks[1])
    slab = projection[pl.ds(pl.multiple_of(owner * slab_rows, slab_rows), slab_rows), :]
    for (first, count), out in zip(spans, outs):
        for at in range(0, count, block):
            size = min(block, count - at)
            master_new = master_t[pl.ds(first + at, size), :] - LEARN_RATE * expand(
                tall, slab, first + at, size
            )
            out[pl.ds(at, size), :] = master_new.astype(jnp.bfloat16)


def weights(projection, master_t, pieces, spans, masks=(0, 0)):
    slab_rows, rank = master_t.shape[1], projection.shape[1]
    wide = pieces[0].shape[1]
    out_shape = [jax.ShapeDtypeStruct((count, slab_rows), jnp.bfloat16) for _, count in spans]
    scratch = []
    if len(pieces) > 1:
        out_shape = [jax.ShapeDtypeStruct((wide, rank), jnp.bfloat16)] + out_shape
        scratch = [pltpu.VMEM((rank, wide), jnp.bfloat16)]
    size = sum(count for _, count in spans) * slab_rows
    return pl.pallas_call(
        functools.partial(weight_kernel, n_in=len(pieces), masks=masks, spans=spans, block=144),
        out_shape=out_shape,
        in_specs=[VMEM] * (2 + len(pieces)),
        out_specs=[VMEM] * len(out_shape),
        scratch_shapes=scratch,
        compiler_params=pltpu.CompilerParams(vmem_limit_bytes=20 * 2**20),
        cost_estimate=pl.CostEstimate(flops=2 * size * rank, bytes_accessed=4 * size, transcendentals=0),
    )(projection, master_t, *pieces)


def master_kernel(projection, master_t, tall, out):
    slab_rows = master_t.shape[1]
    first = pl.multiple_of(lax.axis_index("dp") * slab_rows, slab_rows)
    slab = projection[pl.ds(first, slab_rows), :]
    block = master_t.shape[0]
    first = pl.multiple_of(pl.program_id(0) * block, block)
    out[...] = master_t[...] - LEARN_RATE * expand(tall, slab, first, block)


def new_master(projection, master_t, tall, block):
    cols, slab_rows = master_t.shape
    rank = projection.shape[1]
    return pl.pallas_call(
        master_kernel,
        out_shape=jax.ShapeDtypeStruct((cols, slab_rows), jnp.float32),
        grid=(cols // block,),
        in_specs=[
            pl.BlockSpec(projection.shape, lambda i: (0, 0)),
            pl.BlockSpec((block, slab_rows), lambda i: (i, 0)),
            pl.BlockSpec(tall.shape, lambda i: (0, 0)),
        ],
        out_specs=pl.BlockSpec((block, slab_rows), lambda i: (i, 0)),
        compiler_params=pltpu.CompilerParams(vmem_limit_bytes=20 * 2**20),
        cost_estimate=pl.CostEstimate(
            flops=2 * cols * slab_rows * rank, bytes_accessed=8 * cols * slab_rows, transcendentals=0
        ),
    )(projection, master_t, tall)


def lay_kernel(*refs, first, count, block, fresh):
    refs = refs if fresh else refs[1:]
    pieces, out, (held, sems) = refs[:-3], refs[-3], refs[-2:]
    copies = [None] * held.shape[0]
    me = lax.axis_index("dp")
    core = me & 1
    for at in range(0, count, block):
        slot = at // block % len(copies)
        size = min(block, count - at)
        if copies[slot] is not None:
            copies[slot].wait()
        for masks, piece in zip(OWNER_MASKS, pieces):
            width = piece.shape[1]
            column = pl.multiple_of((me ^ jnp.where(core == 0, masks[0], masks[1])) * width, 128)
            origin = at if piece.shape[0] == count else first + at
            held[slot, pl.ds(0, size), pl.ds(column, width)] = piece[pl.ds(origin, size), :]
        copies[slot] = pltpu.make_async_copy(
            held.at[slot, pl.ds(0, size), :], out.at[pl.ds(first + at, size), :], sems.at[slot]
        )
        copies[slot].start()
    for copy in copies:
        if copy is not None:
            copy.wait()


def lay(out, shape, span, pieces, block=96):
    fresh = out is None
    held = [] if fresh else [out]
    first, count = span
    return pl.pallas_call(
        functools.partial(lay_kernel, first=first, count=count, block=block, fresh=fresh),
        out_shape=jax.ShapeDtypeStruct(shape, jnp.bfloat16),
        in_specs=[ANY] * len(held) + [VMEM] * len(pieces),
        out_specs=ANY,
        scratch_shapes=[
            pltpu.VMEM((4, block, shape[1]), jnp.bfloat16),
            pltpu.SemaphoreType.DMA((4,)),
        ],
        input_output_aliases={} if fresh else {0: 0},
        compiler_params=pltpu.CompilerParams(vmem_limit_bytes=20 * 2**20),
        cost_estimate=pl.CostEstimate(flops=0, bytes_accessed=4 * count * shape[1], transcendentals=0),
    )(*held, *pieces)


def kernel_body(acts, grad_out, projection, moment_one, moment_two, master, n_dp, n_fsdp):
    cols = grad_out.shape[1]
    rank = projection.shape[1]
    rows = moment_one.shape[0]
    slab_rows = master.shape[0]
    wide = -(-cols // 128) * 128
    master_t = master.T

    def hop(value, mask):
        return send(value, "dp", n_dp, mask)

    def turn(value, which):
        masks = [TURN_MASKS[which][i & 1] for i in range(n_dp)]
        return lax.ppermute(value, "dp", [(i, i ^ masks[i]) for i in range(n_dp)])

    def after(value, earlier):
        return lax.optimization_barrier((value, *earlier))[0] if earlier else value

    counts = chunk_sizes(cols)
    chunks = len(counts)
    spans = [(sum(counts[:at]), count) for at, count in enumerate(counts)]
    taken = take(master_t, counts[0])
    ahead = turn(taken, 0)
    acts = after(acts, [taken])

    projected = jnp.dot(acts, projection, preferred_element_type=jnp.float32).astype(jnp.bfloat16)
    tokens = [projected] + [send(projected, "fsdp", n_fsdp, k) for k in range(1, n_fsdp)]
    parts = pl.pallas_call(
        functools.partial(partial_kernel, n_fsdp=n_fsdp, n_dp=n_dp),
        out_shape=[jax.ShapeDtypeStruct((rows, cols), jnp.bfloat16)] * n_dp,
        in_specs=[VMEM] * (1 + n_fsdp),
        out_specs=[VMEM] * n_dp,
        scratch_shapes=[
            pltpu.VMEM((n_fsdp * projected.shape[0], rank), jnp.bfloat16),
            pltpu.VMEM((rank, n_fsdp * projected.shape[0]), jnp.bfloat16),
        ],
        compiler_params=pltpu.CompilerParams(vmem_limit_bytes=16 * 2**20),
    )(grad_out.T, *tokens)
    parts = lax.optimization_barrier((*parts, ahead))[:-1]
    parts = [parts[k] if k == 0 else send(parts[k], "dp", n_dp, k) for k in (0, 2, 4, 6, 7, 3, 5, 1)]
    moment_one_new, moment_two_new, update = pl.pallas_call(
        adam_kernel,
        out_shape=[
            jax.ShapeDtypeStruct(moment_one.shape, jnp.float32),
            jax.ShapeDtypeStruct(moment_two.shape, jnp.float32),
            jax.ShapeDtypeStruct((rows, wide), jnp.bfloat16),
        ],
        in_specs=[VMEM] * (2 + n_dp),
        out_specs=[VMEM] * 3,
        compiler_params=pltpu.CompilerParams(vmem_limit_bytes=16 * 2**20),
    )(moment_one, moment_two, *parts)

    brought = [turn(update, 0), turn(update, 1)]
    brought.append(turn(brought[0], 1))
    updates = []
    for value in [update] + brought:
        updates += [value, hop(value, 1)]

    tall, *own = weights(projection, master_t, updates, spans[1:])
    own_last, whole = weights(projection, master_t, [tall], spans[:1] + [(0, cols)])
    own = [own_last] + own
    (ahead_got,) = weights(projection, ahead, [tall], spans[:1], TURN_MASKS[0])
    ahead_over = hop(ahead_got, 1)
    master_new = new_master(projection, master_t, tall, cols // 4)

    later = range(1, chunks)
    steps = [(0, at) for at in later] + [(1, at) for at in later] + [(2, at) for at in later] + [(1, 0), (2, 0)]
    got, over = {(0, 0): ahead_got}, {(0, 0): ahead_over}
    outs = [None]
    for step, (phase, at) in enumerate(steps):
        value = got[(0, at)] if phase == 2 else own[at]
        earlier = [got[steps[step - 2]]] if step >= 2 else []
        earlier += [over[steps[step - 4]]] if step >= 4 else []
        if step == 2:
            earlier.append(master_new)
        got[(phase, at)] = turn(after(value, earlier), min(phase, 1))
        held = [outs[chunks + step - len(steps)]] if step >= len(steps) - 2 else []
        over[(phase, at)] = hop(after(got[(phase, at)], held), 1)
        if step == 1:
            whole_c = hop(after(whole, [got[steps[1]]]), 1)
        if phase == 2:
            pieces = [whole, whole_c]
            for which in range(3):
                pieces += [got[(which, at)], over[(which, at)]]
            outs.append(lay(outs[-1], (cols, n_dp * slab_rows), spans[at], pieces))
    return (moment_one_new, moment_two_new, master_new.T, outs[-1].T)


def solution(mesh):
    n_dp, n_fsdp = mesh.shape["dp"], mesh.shape["fsdp"]

    def body(acts, grad_out, projection, moment_one, moment_two, master):
        args = (acts, grad_out, projection, moment_one, moment_two, master)
        fits = n_dp == 8 and n_fsdp == 4 and moment_one.shape[0] % 32 == 0 and master.shape[0] % 128 == 0
        if fits and grad_out.shape[1] % 64 == 0 and acts.shape[0] % 128 == 0:
            return kernel_body(*args, n_dp, n_fsdp)
        return plain_body(*args)

    in_specs = (
        P(("dp", "fsdp"), None),
        P("dp", "fsdp"),
        P(),
        P("dp", "fsdp"),
        P("dp", "fsdp"),
        P("dp", "fsdp"),
    )
    out_specs = (P("dp", "fsdp"), P("dp", "fsdp"), P("dp", "fsdp"), P(None, "fsdp"))
    return jax.shard_map(body, mesh=mesh, in_specs=in_specs, out_specs=out_specs, check_vma=False)
```

```python
import functools

import jax
import jax.numpy as jnp
from jax import lax
from jax.experimental import pallas as pl
from jax.experimental.pallas import tpu as pltpu
from jax.sharding import PartitionSpec as P

STEP = 1000


BETA_ONE = 0.9
BETA_TWO = 0.999
ADAM_EPS = 1e-08
LEARN_RATE = 0.01
CORRECT_ONE = 1.0 - BETA_ONE**STEP
CORRECT_TWO = 1.0 - BETA_TWO**STEP

VMEM = pl.BlockSpec(memory_space=pltpu.VMEM)
ANY = pl.BlockSpec(memory_space=pl.ANY)


TURN_MASKS = ((2, 4), (4, 2))
UPDATE_MASKS = tuple((k, k) for k in range(8))
SWAP_MASKS = ((0, 0), (4, 2), (2, 4), (6, 6), (7, 7), (5, 3), (3, 5), (1, 1))
OWNER_MASKS = ((0, 0), (1, 1), (2, 4), (5, 3), (4, 2), (3, 5), (6, 6), (7, 7))


def chunk_sizes(cols):
    small = cols // 80 * 16
    part = -(-(cols - 2 * small) // 48) * 16
    return (small,), (small, part, part, cols - 2 * part - 2 * small, small)


def adam(grad, moment_one, moment_two):
    moment_one_new = BETA_ONE * moment_one + (1.0 - BETA_ONE) * grad
    moment_two_new = BETA_TWO * moment_two + (1.0 - BETA_TWO) * grad * grad
    update = (
        moment_one_new / CORRECT_ONE / (jnp.sqrt(moment_two_new / CORRECT_TWO) + ADAM_EPS)
    ).astype(jnp.bfloat16)
    return moment_one_new, moment_two_new, update


def plain_body(acts, grad_out, projection, moment_one, moment_two, master):
    projected = jnp.dot(acts, projection, preferred_element_type=jnp.float32).astype(jnp.bfloat16)
    group_proj = lax.all_gather(projected, "fsdp", axis=0, tiled=True)
    partial_value = jnp.einsum(
        "tr,tc->rc", group_proj, grad_out, preferred_element_type=jnp.float32
    )
    partial_value = lax.optimization_barrier(partial_value.astype(jnp.bfloat16))
    grad = lax.psum_scatter(
        partial_value.astype(jnp.float32), "dp", scatter_dimension=0, tiled=True
    )
    moment_one_new, moment_two_new, update = adam(grad, moment_one, moment_two)
    slab_rows = master.shape[0]
    proj_slab = lax.dynamic_slice_in_dim(projection, lax.axis_index("dp") * slab_rows, slab_rows, 0)
    piece = lax.all_gather(update, "dp", axis=0, tiled=True)
    expanded = jnp.dot(proj_slab, piece, preferred_element_type=jnp.float32)
    master_new = master - LEARN_RATE * expanded
    weight_cols = lax.all_gather(master_new.astype(jnp.bfloat16), "dp", axis=0, tiled=True)
    return (moment_one_new, moment_two_new, master_new, weight_cols)


def send(value, axis, size, mask):
    return lax.ppermute(value, axis, [(i, i ^ mask) for i in range(size)])


def other(me, masks):
    return me ^ jnp.where((me & 1) == 0, masks[0], masks[1])


def take_kernel(source, out, sems, *, first):
    count = out.shape[0] // sems.shape[0]
    copies = []
    for at in range(sems.shape[0]):
        part = source.at[pl.ds(first + at * count, count), :]
        copies.append(pltpu.make_async_copy(part, out.at[pl.ds(at * count, count), :], sems.at[at]))
    for copy in copies:
        copy.start()
    for copy in copies:
        copy.wait()


def take(array, first, count):
    return pl.pallas_call(
        functools.partial(take_kernel, first=first),
        out_shape=jax.ShapeDtypeStruct((count, array.shape[1]), array.dtype),
        in_specs=[ANY],
        out_specs=VMEM,
        scratch_shapes=[pltpu.SemaphoreType.DMA((count // 16,))],
        compiler_params=pltpu.CompilerParams(vmem_limit_bytes=60 * 2**20),
    )(array)


def partial_kernel(grad_t, *refs, n_fsdp, n_dp):
    pieces, outs, (tokens, across) = refs[:n_fsdp], refs[n_fsdp : n_fsdp + n_dp], refs[n_fsdp + n_dp :]
    count = pieces[0].shape[0]
    rows = outs[0].shape[0]
    me = lax.axis_index("fsdp")
    for k, piece in enumerate(pieces):
        tokens[pl.ds(pl.multiple_of((me ^ k) * count, count), count), :] = piece[...]
    across[...] = tokens[...].T
    me = lax.axis_index("dp")
    left = jnp.concatenate(
        [across[pl.ds(pl.multiple_of(other(me, masks) * rows, rows), rows), :] for masks in SWAP_MASKS], axis=0
    )
    result = lax.dot_general(
        left, grad_t[...], (((1,), (1,)), ((), ())), preferred_element_type=jnp.float32
    ).astype(jnp.bfloat16)
    for k, out in enumerate(outs):
        out[...] = result[k * rows : (k + 1) * rows, :]


def adam_kernel(moment_one, moment_two, *refs):
    parts, (one_new, two_new, update) = refs[:-3], refs[-3:]
    grad = parts[0][...].astype(jnp.float32)
    for part in parts[1:]:
        grad = grad + part[...].astype(jnp.float32)
    one, two, value = adam(grad, moment_one[...], moment_two[...])
    one_new[...] = one
    two_new[...] = two
    cols = value.shape[1]
    update[...] = jnp.zeros_like(update)
    update[:, :cols] = value


def expand(tall, slab, first, count):
    return lax.dot_general(
        tall[pl.ds(first, count), :], slab, (((1,), (1,)), ((), ())),
        preferred_element_type=jnp.float32,
    )


def weight_kernel(projection, master_t, *refs, n_in, spans, block):
    pieces, outs = refs[:n_in], refs[n_in:]
    me = lax.axis_index("dp")
    if n_in > 1:
        tall, wide = outs[0], outs[-1]
        outs = outs[1:-1]
        rows = pieces[0].shape[0]
        for k, piece in enumerate(pieces):
            wide[pl.ds(pl.multiple_of((me ^ k) * rows, rows), rows), :] = piece[...]
        tall[...] = wide[...].T
    else:
        tall = pieces[0]
    slab_rows = master_t.shape[1]
    slab = projection[pl.ds(pl.multiple_of(me * slab_rows, slab_rows), slab_rows), :]
    for (first, count), out in zip(spans, outs):
        for at in range(0, count, block):
            size = min(block, count - at)
            master_new = master_t[pl.ds(first + at, size), :] - LEARN_RATE * expand(
                tall, slab, first + at, size
            )
            out[pl.ds(at, size), :] = master_new.astype(jnp.bfloat16)


def weights(projection, master_t, pieces, spans):
    slab_rows, rank = master_t.shape[1], projection.shape[1]
    wide = pieces[0].shape[1]
    out_shape = [jax.ShapeDtypeStruct((count, slab_rows), jnp.bfloat16) for _, count in spans]
    scratch = []
    if len(pieces) > 1:
        out_shape = [jax.ShapeDtypeStruct((wide, rank), jnp.bfloat16)] + out_shape
        scratch = [pltpu.VMEM((rank, wide), jnp.bfloat16)]
    size = sum(count for _, count in spans) * slab_rows
    return pl.pallas_call(
        functools.partial(weight_kernel, n_in=len(pieces), spans=spans, block=144),
        out_shape=out_shape,
        in_specs=[VMEM] * (2 + len(pieces)),
        out_specs=[VMEM] * len(out_shape),
        scratch_shapes=scratch,
        compiler_params=pltpu.CompilerParams(vmem_limit_bytes=20 * 2**20),
        cost_estimate=pl.CostEstimate(flops=2 * size * rank, bytes_accessed=4 * size, transcendentals=0),
    )(projection, master_t, *pieces)


def ahead_kernel(projection, tall, *refs, block):
    parts, out = refs[:-1], refs[-1]
    slab_rows = out.shape[1]
    owner = other(lax.axis_index("dp"), TURN_MASKS[0])
    slab = projection[pl.ds(pl.multiple_of(owner * slab_rows, slab_rows), slab_rows), :]
    first = 0
    for part in parts:
        for at in range(0, part.shape[0], block):
            size = min(block, part.shape[0] - at)
            master_new = part[pl.ds(at, size), :] - LEARN_RATE * expand(tall, slab, first, size)
            out[pl.ds(first, size), :] = master_new.astype(jnp.bfloat16)
            first += size


def ahead_weights(projection, tall, parts):
    shape = (sum(part.shape[0] for part in parts), parts[0].shape[1])
    size = shape[0] * shape[1]
    return pl.pallas_call(
        functools.partial(ahead_kernel, block=144),
        out_shape=jax.ShapeDtypeStruct(shape, jnp.bfloat16),
        in_specs=[VMEM] * (2 + len(parts)),
        out_specs=VMEM,
        compiler_params=pltpu.CompilerParams(vmem_limit_bytes=20 * 2**20),
        cost_estimate=pl.CostEstimate(
            flops=2 * size * projection.shape[1], bytes_accessed=4 * size, transcendentals=0
        ),
    )(projection, tall, *parts)


def master_kernel(projection, master_t, tall, out):
    slab_rows = master_t.shape[1]
    first = pl.multiple_of(lax.axis_index("dp") * slab_rows, slab_rows)
    slab = projection[pl.ds(first, slab_rows), :]
    block = master_t.shape[0]
    first = pl.multiple_of(pl.program_id(0) * block, block)
    out[...] = master_t[...] - LEARN_RATE * expand(tall, slab, first, block)


def new_master(projection, master_t, tall, block):
    cols, slab_rows = master_t.shape
    rank = projection.shape[1]
    return pl.pallas_call(
        master_kernel,
        out_shape=jax.ShapeDtypeStruct((cols, slab_rows), jnp.float32),
        grid=(cols // block,),
        in_specs=[
            pl.BlockSpec(projection.shape, lambda i: (0, 0)),
            pl.BlockSpec((block, slab_rows), lambda i: (i, 0)),
            pl.BlockSpec(tall.shape, lambda i: (0, 0)),
        ],
        out_specs=pl.BlockSpec((block, slab_rows), lambda i: (i, 0)),
        compiler_params=pltpu.CompilerParams(vmem_limit_bytes=20 * 2**20),
        cost_estimate=pl.CostEstimate(
            flops=2 * cols * slab_rows * rank, bytes_accessed=8 * cols * slab_rows, transcendentals=0
        ),
    )(projection, master_t, tall)


def lay_kernel(*refs, first, count, block, fresh):
    refs = refs if fresh else refs[1:]
    pieces, out, (held, sems) = refs[:-3], refs[-3], refs[-2:]
    copies = [None] * held.shape[0]
    me = lax.axis_index("dp")
    for at in range(0, count, block):
        slot = at // block % len(copies)
        size = min(block, count - at)
        if copies[slot] is not None:
            copies[slot].wait()
        for masks, piece in zip(OWNER_MASKS, pieces):
            width = piece.shape[1]
            column = pl.multiple_of(other(me, masks) * width, 128)
            origin = at if piece.shape[0] == count else first + at
            held[slot, pl.ds(0, size), pl.ds(column, width)] = piece[pl.ds(origin, size), :]
        copies[slot] = pltpu.make_async_copy(
            held.at[slot, pl.ds(0, size), :], out.at[pl.ds(first + at, size), :], sems.at[slot]
        )
        copies[slot].start()
    for copy in copies:
        if copy is not None:
            copy.wait()


def lay(out, shape, span, pieces, block=96):
    fresh = out is None
    held = [] if fresh else [out]
    first, count = span
    return pl.pallas_call(
        functools.partial(lay_kernel, first=first, count=count, block=block, fresh=fresh),
        out_shape=jax.ShapeDtypeStruct(shape, jnp.bfloat16),
        in_specs=[ANY] * len(held) + [VMEM] * len(pieces),
        out_specs=ANY,
        scratch_shapes=[
            pltpu.VMEM((4, block, shape[1]), jnp.bfloat16),
            pltpu.SemaphoreType.DMA((4,)),
        ],
        input_output_aliases={} if fresh else {0: 0},
        compiler_params=pltpu.CompilerParams(vmem_limit_bytes=20 * 2**20),
        cost_estimate=pl.CostEstimate(flops=0, bytes_accessed=4 * count * shape[1], transcendentals=0),
    )(*held, *pieces)


def kernel_body(acts, grad_out, projection, moment_one, moment_two, master, n_dp, n_fsdp):
    cols = grad_out.shape[1]
    rank = projection.shape[1]
    rows = moment_one.shape[0]
    slab_rows = master.shape[0]
    wide = -(-cols // 128) * 128
    master_t = master.T

    def hop(value, mask):
        return send(value, "dp", n_dp, mask)

    def turn(value, masks):
        return lax.ppermute(value, "dp", [(i, i ^ masks[i & 1]) for i in range(n_dp)])

    def after(value, earlier):
        return lax.optimization_barrier((value, *earlier))[0] if earlier else value

    early, counts = chunk_sizes(cols)
    spans = [(sum(counts[:at]), count) for at, count in enumerate(counts)]
    taken = take(master_t, 0, early[0])
    ahead = [turn(taken, TURN_MASKS[0])]
    acts = after(acts, [taken])

    projected = jnp.dot(acts, projection, preferred_element_type=jnp.float32).astype(jnp.bfloat16)
    tokens = [projected] + [send(projected, "fsdp", n_fsdp, k) for k in range(1, n_fsdp)]
    parts = pl.pallas_call(
        functools.partial(partial_kernel, n_fsdp=n_fsdp, n_dp=n_dp),
        out_shape=[jax.ShapeDtypeStruct((rows, cols), jnp.bfloat16)] * n_dp,
        in_specs=[VMEM] * (1 + n_fsdp),
        out_specs=[VMEM] * n_dp,
        scratch_shapes=[
            pltpu.VMEM((n_fsdp * projected.shape[0], rank), jnp.bfloat16),
            pltpu.VMEM((rank, n_fsdp * projected.shape[0]), jnp.bfloat16),
        ],
        compiler_params=pltpu.CompilerParams(vmem_limit_bytes=16 * 2**20),
    )(grad_out.T, *tokens)
    parts = lax.optimization_barrier((*parts, *ahead))[:n_dp]
    parts = [part if masks == (0, 0) else turn(part, masks) for part, masks in zip(parts, SWAP_MASKS)]
    moment_one_new, moment_two_new, update = pl.pallas_call(
        adam_kernel,
        out_shape=[
            jax.ShapeDtypeStruct(moment_one.shape, jnp.float32),
            jax.ShapeDtypeStruct(moment_two.shape, jnp.float32),
            jax.ShapeDtypeStruct((rows, wide), jnp.bfloat16),
        ],
        in_specs=[VMEM] * (2 + n_dp),
        out_specs=[VMEM] * 3,
        compiler_params=pltpu.CompilerParams(vmem_limit_bytes=16 * 2**20),
    )(moment_one, moment_two, *parts)

    updates = {0: update}
    for k in (6, 2, 4, 1):
        updates[k] = hop(update, k)
    for k in (2, 4, 6):
        updates[k ^ 1] = hop(updates[k], 1)
    updates = [updates[k] for k in range(n_dp)]

    tall, *own = weights(projection, master_t, updates, spans[1:3])
    *late, own_first, whole = weights(projection, master_t, [tall], spans[3:] + spans[:1] + [(0, cols)])
    own = [own_first] + own + late
    got = {(0, 0): ahead_weights(projection, tall, ahead)}
    over = {(0, 0): hop(got[(0, 0)], 1)}
    master_new = new_master(projection, master_t, tall, cols // 4)

    later = range(1, len(counts))
    steps = [(phase, at) for phase in range(3) for at in later] + [(1, 0), (2, 0)]
    outs = [None]
    for step, (phase, at) in enumerate(steps):
        value = got[(0, at)] if phase == 2 else own[at]
        earlier = [got[steps[step - 2]]] if step >= 2 else []
        earlier += [over[steps[step - 4]]] if step >= 4 else []
        if step == 2:
            earlier.append(master_new)
        got[(phase, at)] = turn(after(value, earlier), TURN_MASKS[min(phase, 1)])
        held = [outs[len(counts) + step - len(steps)]] if step >= len(steps) - 2 else []
        over[(phase, at)] = hop(after(got[(phase, at)], held), 1)
        if step == 1:
            whole_c = hop(after(whole, [got[steps[1]]]), 1)
        if phase == 2:
            pieces = [whole, whole_c]
            for which in range(3):
                pieces += [got[(which, at)], over[(which, at)]]
            outs.append(lay(outs[-1], (cols, n_dp * slab_rows), spans[at], pieces))
    return (moment_one_new, moment_two_new, master_new.T, outs[-1].T)


def solution(mesh):
    n_dp, n_fsdp = mesh.shape["dp"], mesh.shape["fsdp"]

    def body(acts, grad_out, projection, moment_one, moment_two, master):
        args = (acts, grad_out, projection, moment_one, moment_two, master)
        fits = n_dp == 8 and n_fsdp == 4 and moment_one.shape[0] % 32 == 0 and master.shape[0] % 128 == 0
        if fits and grad_out.shape[1] % 64 == 0 and acts.shape[0] % 128 == 0:
            return kernel_body(*args, n_dp, n_fsdp)
        return plain_body(*args)

    in_specs = (
        P(("dp", "fsdp"), None),
        P("dp", "fsdp"),
        P(),
        P("dp", "fsdp"),
        P("dp", "fsdp"),
        P("dp", "fsdp"),
    )
    out_specs = (P("dp", "fsdp"), P("dp", "fsdp"), P("dp", "fsdp"), P(None, "fsdp"))
    return jax.shard_map(body, mesh=mesh, in_specs=in_specs, out_specs=out_specs, check_vma=False)
```

```python
import functools

import jax
import jax.numpy as jnp
from jax import lax
from jax.experimental import pallas as pl
from jax.experimental.pallas import tpu as pltpu
from jax.sharding import PartitionSpec as P

STEP = 1000


BETA_ONE = 0.9
BETA_TWO = 0.999
ADAM_EPS = 1e-08
LEARN_RATE = 0.01
CORRECT_ONE = 1.0 - BETA_ONE**STEP
CORRECT_TWO = 1.0 - BETA_TWO**STEP

VMEM = pl.BlockSpec(memory_space=pltpu.VMEM)
ANY = pl.BlockSpec(memory_space=pl.ANY)


TURN_MASKS = ((2, 4), (4, 2))
UPDATE_MASKS = tuple((k, k) for k in range(8))
SWAP_MASKS = ((0, 0), (4, 2), (2, 4), (6, 6), (7, 7), (5, 3), (3, 5), (1, 1))
OWNER_MASKS = ((0, 0), (1, 1), (2, 4), (5, 3), (4, 2), (3, 5), (6, 6), (7, 7))


def chunk_sizes(cols):
    ahead = (cols // 120 * 16, cols // 112 * 16)
    rest = cols - sum(ahead)
    part = -(-rest // 64) * 16
    return ahead, (sum(ahead), part, part, part, rest - 3 * part)


def adam(grad, moment_one, moment_two):
    moment_one_new = BETA_ONE * moment_one + (1.0 - BETA_ONE) * grad
    moment_two_new = BETA_TWO * moment_two + (1.0 - BETA_TWO) * grad * grad
    update = (
        moment_one_new / CORRECT_ONE / (jnp.sqrt(moment_two_new / CORRECT_TWO) + ADAM_EPS)
    ).astype(jnp.bfloat16)
    return moment_one_new, moment_two_new, update


def plain_body(acts, grad_out, projection, moment_one, moment_two, master):
    projected = jnp.dot(acts, projection, preferred_element_type=jnp.float32).astype(jnp.bfloat16)
    group_proj = lax.all_gather(projected, "fsdp", axis=0, tiled=True)
    partial_value = jnp.einsum(
        "tr,tc->rc", group_proj, grad_out, preferred_element_type=jnp.float32
    )
    partial_value = lax.optimization_barrier(partial_value.astype(jnp.bfloat16))
    grad = lax.psum_scatter(
        partial_value.astype(jnp.float32), "dp", scatter_dimension=0, tiled=True
    )
    moment_one_new, moment_two_new, update = adam(grad, moment_one, moment_two)
    slab_rows = master.shape[0]
    proj_slab = lax.dynamic_slice_in_dim(projection, lax.axis_index("dp") * slab_rows, slab_rows, 0)
    piece = lax.all_gather(update, "dp", axis=0, tiled=True)
    expanded = jnp.dot(proj_slab, piece, preferred_element_type=jnp.float32)
    master_new = master - LEARN_RATE * expanded
    weight_cols = lax.all_gather(master_new.astype(jnp.bfloat16), "dp", axis=0, tiled=True)
    return (moment_one_new, moment_two_new, master_new, weight_cols)


def send(value, axis, size, mask):
    return lax.ppermute(value, axis, [(i, i ^ mask) for i in range(size)])


def other(me, masks):
    return me ^ jnp.where((me & 1) == 0, masks[0], masks[1])


def take_kernel(source, out, sems, *, first):
    count = out.shape[0] // sems.shape[0]
    copies = []
    for at in range(sems.shape[0]):
        part = source.at[pl.ds(first + at * count, count), :]
        copies.append(pltpu.make_async_copy(part, out.at[pl.ds(at * count, count), :], sems.at[at]))
    for copy in copies:
        copy.start()
    for copy in copies:
        copy.wait()


def take(array, first, count, limit):
    return pl.pallas_call(
        functools.partial(take_kernel, first=first),
        out_shape=jax.ShapeDtypeStruct((count, array.shape[1]), array.dtype),
        in_specs=[ANY],
        out_specs=VMEM,
        scratch_shapes=[pltpu.SemaphoreType.DMA((count // 16,))],
        compiler_params=pltpu.CompilerParams(vmem_limit_bytes=limit * 2**20),
    )(array)


def partial_kernel(grad_t, *refs, n_fsdp, n_dp):
    pieces, outs, (tokens, across) = refs[:n_fsdp], refs[n_fsdp : n_fsdp + n_dp], refs[n_fsdp + n_dp :]
    count = pieces[0].shape[0]
    rows = outs[0].shape[0]
    me = lax.axis_index("fsdp")
    for k, piece in enumerate(pieces):
        tokens[pl.ds(pl.multiple_of((me ^ k) * count, count), count), :] = piece[...]
    across[...] = tokens[...].T
    me = lax.axis_index("dp")
    left = jnp.concatenate(
        [across[pl.ds(pl.multiple_of(other(me, masks) * rows, rows), rows), :] for masks in SWAP_MASKS], axis=0
    )
    result = lax.dot_general(
        left, grad_t[...], (((1,), (1,)), ((), ())), preferred_element_type=jnp.float32
    ).astype(jnp.bfloat16)
    for k, out in enumerate(outs):
        out[...] = result[k * rows : (k + 1) * rows, :]


def adam_kernel(moment_one, moment_two, *refs):
    parts, (one_new, two_new, update) = refs[:-3], refs[-3:]
    grad = parts[0][...].astype(jnp.float32)
    for part in parts[1:]:
        grad = grad + part[...].astype(jnp.float32)
    one, two, value = adam(grad, moment_one[...], moment_two[...])
    one_new[...] = one
    two_new[...] = two
    cols = value.shape[1]
    update[...] = jnp.zeros_like(update)
    update[:, :cols] = value


def expand(tall, slab, first, count):
    return lax.dot_general(
        tall[pl.ds(first, count), :], slab, (((1,), (1,)), ((), ())),
        preferred_element_type=jnp.float32,
    )


def weight_kernel(projection, master_t, *refs, n_in, spans, block):
    pieces, outs = refs[:n_in], refs[n_in:]
    me = lax.axis_index("dp")
    if n_in > 1:
        tall, wide = outs[0], outs[-1]
        outs = outs[1:-1]
        rows = pieces[0].shape[0]
        for k, piece in enumerate(pieces):
            wide[pl.ds(pl.multiple_of((me ^ k) * rows, rows), rows), :] = piece[...]
        tall[...] = wide[...].T
    else:
        tall = pieces[0]
    slab_rows = master_t.shape[1]
    slab = projection[pl.ds(pl.multiple_of(me * slab_rows, slab_rows), slab_rows), :]
    for (first, count), out in zip(spans, outs):
        for at in range(0, count, block):
            size = min(block, count - at)
            master_new = master_t[pl.ds(first + at, size), :] - LEARN_RATE * expand(
                tall, slab, first + at, size
            )
            out[pl.ds(at, size), :] = master_new.astype(jnp.bfloat16)


def weights(projection, master_t, pieces, spans):
    slab_rows, rank = master_t.shape[1], projection.shape[1]
    wide = pieces[0].shape[1]
    out_shape = [jax.ShapeDtypeStruct((count, slab_rows), jnp.bfloat16) for _, count in spans]
    scratch = []
    if len(pieces) > 1:
        out_shape = [jax.ShapeDtypeStruct((wide, rank), jnp.bfloat16)] + out_shape
        scratch = [pltpu.VMEM((rank, wide), jnp.bfloat16)]
    size = sum(count for _, count in spans) * slab_rows
    return pl.pallas_call(
        functools.partial(weight_kernel, n_in=len(pieces), spans=spans, block=144),
        out_shape=out_shape,
        in_specs=[VMEM] * (2 + len(pieces)),
        out_specs=[VMEM] * len(out_shape),
        scratch_shapes=scratch,
        compiler_params=pltpu.CompilerParams(vmem_limit_bytes=20 * 2**20),
        cost_estimate=pl.CostEstimate(flops=2 * size * rank, bytes_accessed=4 * size, transcendentals=0),
    )(projection, master_t, *pieces)


def ahead_kernel(projection, tall, *refs, block):
    parts, out = refs[:-1], refs[-1]
    slab_rows = out.shape[1]
    owner = other(lax.axis_index("dp"), TURN_MASKS[0])
    slab = projection[pl.ds(pl.multiple_of(owner * slab_rows, slab_rows), slab_rows), :]
    first = 0
    for part in parts:
        for at in range(0, part.shape[0], block):
            size = min(block, part.shape[0] - at)
            master_new = part[pl.ds(at, size), :] - LEARN_RATE * expand(tall, slab, first, size)
            out[pl.ds(first, size), :] = master_new.astype(jnp.bfloat16)
            first += size


def ahead_weights(projection, tall, parts):
    shape = (sum(part.shape[0] for part in parts), parts[0].shape[1])
    size = shape[0] * shape[1]
    return pl.pallas_call(
        functools.partial(ahead_kernel, block=144),
        out_shape=jax.ShapeDtypeStruct(shape, jnp.bfloat16),
        in_specs=[VMEM] * (2 + len(parts)),
        out_specs=VMEM,
        compiler_params=pltpu.CompilerParams(vmem_limit_bytes=20 * 2**20),
        cost_estimate=pl.CostEstimate(
            flops=2 * size * projection.shape[1], bytes_accessed=4 * size, transcendentals=0
        ),
    )(projection, tall, *parts)


def master_kernel(projection, master_t, tall, out):
    slab_rows = master_t.shape[1]
    first = pl.multiple_of(lax.axis_index("dp") * slab_rows, slab_rows)
    slab = projection[pl.ds(first, slab_rows), :]
    block = master_t.shape[0]
    first = pl.multiple_of(pl.program_id(0) * block, block)
    out[...] = master_t[...] - LEARN_RATE * expand(tall, slab, first, block)


def new_master(projection, master_t, tall, block):
    cols, slab_rows = master_t.shape
    rank = projection.shape[1]
    return pl.pallas_call(
        master_kernel,
        out_shape=jax.ShapeDtypeStruct((cols, slab_rows), jnp.float32),
        grid=(cols // block,),
        in_specs=[
            pl.BlockSpec(projection.shape, lambda i: (0, 0)),
            pl.BlockSpec((block, slab_rows), lambda i: (i, 0)),
            pl.BlockSpec(tall.shape, lambda i: (0, 0)),
        ],
        out_specs=pl.BlockSpec((block, slab_rows), lambda i: (i, 0)),
        compiler_params=pltpu.CompilerParams(vmem_limit_bytes=20 * 2**20),
        cost_estimate=pl.CostEstimate(
            flops=2 * cols * slab_rows * rank, bytes_accessed=8 * cols * slab_rows, transcendentals=0
        ),
    )(projection, master_t, tall)


def lay_kernel(*refs, first, count, block, fresh):
    refs = refs if fresh else refs[1:]
    pieces, out, (held, sems) = refs[:-3], refs[-3], refs[-2:]
    copies = [None] * held.shape[0]
    me = lax.axis_index("dp")
    for at in range(0, count, block):
        slot = at // block % len(copies)
        size = min(block, count - at)
        if copies[slot] is not None:
            copies[slot].wait()
        for masks, piece in zip(OWNER_MASKS, pieces):
            width = piece.shape[1]
            column = pl.multiple_of(other(me, masks) * width, 128)
            origin = at if piece.shape[0] == count else first + at
            held[slot, pl.ds(0, size), pl.ds(column, width)] = piece[pl.ds(origin, size), :]
        copies[slot] = pltpu.make_async_copy(
            held.at[slot, pl.ds(0, size), :], out.at[pl.ds(first + at, size), :], sems.at[slot]
        )
        copies[slot].start()
    for copy in copies:
        if copy is not None:
            copy.wait()


def lay(out, shape, span, pieces, block=96):
    fresh = out is None
    held = [] if fresh else [out]
    first, count = span
    return pl.pallas_call(
        functools.partial(lay_kernel, first=first, count=count, block=block, fresh=fresh),
        out_shape=jax.ShapeDtypeStruct(shape, jnp.bfloat16),
        in_specs=[ANY] * len(held) + [VMEM] * len(pieces),
        out_specs=ANY,
        scratch_shapes=[
            pltpu.VMEM((4, block, shape[1]), jnp.bfloat16),
            pltpu.SemaphoreType.DMA((4,)),
        ],
        input_output_aliases={} if fresh else {0: 0},
        compiler_params=pltpu.CompilerParams(vmem_limit_bytes=20 * 2**20),
        cost_estimate=pl.CostEstimate(flops=0, bytes_accessed=4 * count * shape[1], transcendentals=0),
    )(*held, *pieces)


def kernel_body(acts, grad_out, projection, moment_one, moment_two, master, n_dp, n_fsdp):
    cols = grad_out.shape[1]
    rank = projection.shape[1]
    rows = moment_one.shape[0]
    slab_rows = master.shape[0]
    wide = -(-cols // 128) * 128
    master_t = master.T

    def hop(value, mask):
        return send(value, "dp", n_dp, mask)

    def turn(value, masks):
        return lax.ppermute(value, "dp", [(i, i ^ masks[i & 1]) for i in range(n_dp)])

    def after(value, earlier):
        return lax.optimization_barrier((value, *earlier))[0] if earlier else value

    early, counts = chunk_sizes(cols)
    spans = [(sum(counts[:at]), count) for at, count in enumerate(counts)]
    taken = take(master_t, 0, early[0], 60)
    ahead = [turn(taken, TURN_MASKS[0])]
    acts = after(acts, [taken])

    projected = jnp.dot(acts, projection, preferred_element_type=jnp.float32).astype(jnp.bfloat16)
    tokens = [projected] + [send(projected, "fsdp", n_fsdp, k) for k in range(1, n_fsdp)]
    parts = pl.pallas_call(
        functools.partial(partial_kernel, n_fsdp=n_fsdp, n_dp=n_dp),
        out_shape=[jax.ShapeDtypeStruct((rows, cols), jnp.bfloat16)] * n_dp,
        in_specs=[VMEM] * (1 + n_fsdp),
        out_specs=[VMEM] * n_dp,
        scratch_shapes=[
            pltpu.VMEM((n_fsdp * projected.shape[0], rank), jnp.bfloat16),
            pltpu.VMEM((rank, n_fsdp * projected.shape[0]), jnp.bfloat16),
        ],
        compiler_params=pltpu.CompilerParams(vmem_limit_bytes=16 * 2**20),
    )(grad_out.T, *tokens)
    parts = lax.optimization_barrier((*parts, *ahead))[:n_dp]
    parts = [part if masks == (0, 0) else turn(part, masks) for part, masks in zip(parts, SWAP_MASKS)]
    moment_one_new, moment_two_new, update = pl.pallas_call(
        adam_kernel,
        out_shape=[
            jax.ShapeDtypeStruct(moment_one.shape, jnp.float32),
            jax.ShapeDtypeStruct(moment_two.shape, jnp.float32),
            jax.ShapeDtypeStruct((rows, wide), jnp.bfloat16),
        ],
        in_specs=[VMEM] * (2 + n_dp),
        out_specs=[VMEM] * 3,
        compiler_params=pltpu.CompilerParams(vmem_limit_bytes=16 * 2**20),
    )(moment_one, moment_two, *parts)

    updates = {0: update}
    for k in (6, 2, 4, 1):
        updates[k] = hop(update, k)
    for k in (2, 4, 6):
        updates[k ^ 1] = hop(updates[k], 1)
    second = take(after(master_t, [update]), *early, 8)
    ahead.append(turn(after(second, [updates[k] for k in (2, 4, 6)]), TURN_MASKS[0]))
    updates = [updates[k] for k in range(n_dp)]

    tall, *own = weights(projection, master_t, updates, spans[1:3])
    *late, own_first, whole = weights(projection, master_t, [tall], spans[3:] + spans[:1] + [(0, cols)])
    own = [own_first] + own + late
    got = {(0, 0): ahead_weights(projection, tall, ahead)}
    over = {(0, 0): hop(got[(0, 0)], 1)}
    master_new = new_master(projection, master_t, tall, cols // 4)

    later = range(1, len(counts))
    steps = [(phase, at) for phase in range(3) for at in later] + [(1, 0), (2, 0)]
    outs = [None]
    for step, (phase, at) in enumerate(steps):
        value = got[(0, at)] if phase == 2 else own[at]
        earlier = [got[steps[step - 2]]] if step >= 2 else []
        earlier += [over[steps[step - 4]]] if step >= 4 else []
        if step == 2:
            earlier.append(master_new)
        if step == 3:
            earlier.append(ahead[1])
        got[(phase, at)] = turn(after(value, earlier), TURN_MASKS[min(phase, 1)])
        held = [outs[len(counts) + step - len(steps)]] if step >= len(steps) - 2 else []
        over[(phase, at)] = hop(after(got[(phase, at)], held), 1)
        if step == 1:
            whole_c = hop(after(whole, [got[steps[1]]]), 1)
        if phase == 2:
            pieces = [whole, whole_c]
            for which in range(3):
                pieces += [got[(which, at)], over[(which, at)]]
            outs.append(lay(outs[-1], (cols, n_dp * slab_rows), spans[at], pieces))
    return (moment_one_new, moment_two_new, master_new.T, outs[-1].T)


def solution(mesh):
    n_dp, n_fsdp = mesh.shape["dp"], mesh.shape["fsdp"]

    def body(acts, grad_out, projection, moment_one, moment_two, master):
        args = (acts, grad_out, projection, moment_one, moment_two, master)
        fits = n_dp == 8 and n_fsdp == 4 and moment_one.shape[0] % 32 == 0 and master.shape[0] % 128 == 0
        if fits and grad_out.shape[1] % 64 == 0 and acts.shape[0] % 128 == 0:
            return kernel_body(*args, n_dp, n_fsdp)
        return plain_body(*args)

    in_specs = (
        P(("dp", "fsdp"), None),
        P("dp", "fsdp"),
        P(),
        P("dp", "fsdp"),
        P("dp", "fsdp"),
        P("dp", "fsdp"),
    )
    out_specs = (P("dp", "fsdp"), P("dp", "fsdp"), P("dp", "fsdp"), P(None, "fsdp"))
    return jax.shard_map(body, mesh=mesh, in_specs=in_specs, out_specs=out_specs, check_vma=False)
```

```python
import functools

import jax
import jax.numpy as jnp
from jax import lax
from jax.experimental import pallas as pl
from jax.experimental.pallas import tpu as pltpu
from jax.sharding import PartitionSpec as P

STEP = 1000


BETA_ONE = 0.9
BETA_TWO = 0.999
ADAM_EPS = 1e-08
LEARN_RATE = 0.01
CORRECT_ONE = 1.0 - BETA_ONE**STEP
CORRECT_TWO = 1.0 - BETA_TWO**STEP

VMEM = pl.BlockSpec(memory_space=pltpu.VMEM)
ANY = pl.BlockSpec(memory_space=pl.ANY)


TURN_MASKS = ((2, 4), (4, 2))
SWAP_MASKS = ((0, 0), (4, 2), (2, 4), (6, 6), (7, 7), (5, 3), (3, 5), (1, 1))
OWNER_MASKS = ((0, 0), (1, 1), (2, 4), (5, 3), (4, 2), (3, 5), (6, 6), (7, 7))


def chunk_sizes(cols):
    small = cols // 80 * 16
    part = -(-(cols - 2 * small) // 48) * 16
    return (small,), (small, part, part, cols - 2 * part - 2 * small, small)


def adam(grad, moment_one, moment_two):
    moment_one_new = BETA_ONE * moment_one + (1.0 - BETA_ONE) * grad
    moment_two_new = BETA_TWO * moment_two + (1.0 - BETA_TWO) * grad * grad
    update = (
        moment_one_new / CORRECT_ONE / (jnp.sqrt(moment_two_new / CORRECT_TWO) + ADAM_EPS)
    ).astype(jnp.bfloat16)
    return moment_one_new, moment_two_new, update


def plain_body(acts, grad_out, projection, moment_one, moment_two, master):
    projected = jnp.dot(acts, projection, preferred_element_type=jnp.float32).astype(jnp.bfloat16)
    group_proj = lax.all_gather(projected, "fsdp", axis=0, tiled=True)
    partial_value = jnp.einsum(
        "tr,tc->rc", group_proj, grad_out, preferred_element_type=jnp.float32
    )
    partial_value = lax.optimization_barrier(partial_value.astype(jnp.bfloat16))
    grad = lax.psum_scatter(
        partial_value.astype(jnp.float32), "dp", scatter_dimension=0, tiled=True
    )
    moment_one_new, moment_two_new, update = adam(grad, moment_one, moment_two)
    slab_rows = master.shape[0]
    proj_slab = lax.dynamic_slice_in_dim(projection, lax.axis_index("dp") * slab_rows, slab_rows, 0)
    piece = lax.all_gather(update, "dp", axis=0, tiled=True)
    expanded = jnp.dot(proj_slab, piece, preferred_element_type=jnp.float32)
    master_new = master - LEARN_RATE * expanded
    weight_cols = lax.all_gather(master_new.astype(jnp.bfloat16), "dp", axis=0, tiled=True)
    return (moment_one_new, moment_two_new, master_new, weight_cols)


def send(value, axis, size, mask):
    return lax.ppermute(value, axis, [(i, i ^ mask) for i in range(size)])


def other(me, masks):
    return me ^ jnp.where((me & 1) == 0, masks[0], masks[1])


def partial_kernel(grad_t, *refs, n_fsdp, n_dp):
    pieces, outs, (tokens, across) = refs[:n_fsdp], refs[n_fsdp : n_fsdp + n_dp], refs[n_fsdp + n_dp :]
    count = pieces[0].shape[0]
    rows = outs[0].shape[0]
    me = lax.axis_index("fsdp")
    for k, piece in enumerate(pieces):
        tokens[pl.ds(pl.multiple_of((me ^ k) * count, count), count), :] = piece[...]
    across[...] = tokens[...].T
    me = lax.axis_index("dp")
    left = jnp.concatenate(
        [across[pl.ds(pl.multiple_of(other(me, masks) * rows, rows), rows), :] for masks in SWAP_MASKS], axis=0
    )
    result = lax.dot_general(
        left, grad_t[...], (((1,), (1,)), ((), ())), preferred_element_type=jnp.float32
    ).astype(jnp.bfloat16)
    for k, out in enumerate(outs):
        out[...] = result[k * rows : (k + 1) * rows, :]


def adam_kernel(moment_one, moment_two, *refs):
    parts, (one_new, two_new, update) = refs[:-3], refs[-3:]
    grad = parts[0][...].astype(jnp.float32)
    for part in parts[1:]:
        grad = grad + part[...].astype(jnp.float32)
    one, two, value = adam(grad, moment_one[...], moment_two[...])
    one_new[...] = one
    two_new[...] = two
    cols = value.shape[1]
    update[...] = jnp.zeros_like(update)
    update[:, :cols] = value


def expand(tall, slab, first, count):
    return lax.dot_general(
        tall[pl.ds(first, count), :], slab, (((1,), (1,)), ((), ())),
        preferred_element_type=jnp.float32,
    )


def weight_kernel(projection, master_t, *refs, n_in, spans, block):
    pieces, outs = refs[:n_in], refs[n_in:]
    me = lax.axis_index("dp")
    if n_in > 1:
        tall, wide = outs[0], outs[-1]
        outs = outs[1:-1]
        rows = pieces[0].shape[0]
        for masks, piece in zip(OWNER_MASKS, pieces):
            wide[pl.ds(pl.multiple_of(other(me, masks) * rows, rows), rows), :] = piece[...]
        tall[...] = wide[...].T
    else:
        tall = pieces[0]
    slab_rows = master_t.shape[1]
    slab = projection[pl.ds(pl.multiple_of(me * slab_rows, slab_rows), slab_rows), :]
    for (first, count), out in zip(spans, outs):
        for at in range(0, count, block):
            size = min(block, count - at)
            master_new = master_t[pl.ds(first + at, size), :] - LEARN_RATE * expand(
                tall, slab, first + at, size
            )
            out[pl.ds(at, size), :] = master_new.astype(jnp.bfloat16)


def weights(projection, master_t, pieces, spans):
    slab_rows, rank = master_t.shape[1], projection.shape[1]
    wide = pieces[0].shape[1]
    out_shape = [jax.ShapeDtypeStruct((count, slab_rows), jnp.bfloat16) for _, count in spans]
    scratch = []
    if len(pieces) > 1:
        out_shape = [jax.ShapeDtypeStruct((wide, rank), jnp.bfloat16)] + out_shape
        scratch = [pltpu.VMEM((rank, wide), jnp.bfloat16)]
    size = sum(count for _, count in spans) * slab_rows
    return pl.pallas_call(
        functools.partial(weight_kernel, n_in=len(pieces), spans=spans, block=144),
        out_shape=out_shape,
        in_specs=[VMEM] * (2 + len(pieces)),
        out_specs=[VMEM] * len(out_shape),
        scratch_shapes=scratch,
        compiler_params=pltpu.CompilerParams(vmem_limit_bytes=20 * 2**20),
        cost_estimate=pl.CostEstimate(flops=2 * size * rank, bytes_accessed=4 * size, transcendentals=0),
    )(projection, master_t, *pieces)


def ahead_kernel(projection, tall, *refs, block):
    parts, out = refs[:-1], refs[-1]
    slab_rows = out.shape[1]
    owner = other(lax.axis_index("dp"), TURN_MASKS[0])
    slab = projection[pl.ds(pl.multiple_of(owner * slab_rows, slab_rows), slab_rows), :]
    first = 0
    for part in parts:
        for at in range(0, part.shape[0], block):
            size = min(block, part.shape[0] - at)
            master_new = part[pl.ds(at, size), :] - LEARN_RATE * expand(tall, slab, first, size)
            out[pl.ds(first, size), :] = master_new.astype(jnp.bfloat16)
            first += size


def ahead_weights(projection, tall, parts):
    shape = (sum(part.shape[0] for part in parts), parts[0].shape[1])
    size = shape[0] * shape[1]
    return pl.pallas_call(
        functools.partial(ahead_kernel, block=144),
        out_shape=jax.ShapeDtypeStruct(shape, jnp.bfloat16),
        in_specs=[VMEM] * (2 + len(parts)),
        out_specs=VMEM,
        compiler_params=pltpu.CompilerParams(vmem_limit_bytes=20 * 2**20),
        cost_estimate=pl.CostEstimate(
            flops=2 * size * projection.shape[1], bytes_accessed=4 * size, transcendentals=0
        ),
    )(projection, tall, *parts)


def master_kernel(projection, master_t, tall, out):
    slab_rows = master_t.shape[1]
    first = pl.multiple_of(lax.axis_index("dp") * slab_rows, slab_rows)
    slab = projection[pl.ds(first, slab_rows), :]
    block = master_t.shape[0]
    first = pl.multiple_of(pl.program_id(0) * block, block)
    out[...] = master_t[...] - LEARN_RATE * expand(tall, slab, first, block)


def new_master(projection, master_t, tall, block):
    cols, slab_rows = master_t.shape
    rank = projection.shape[1]
    return pl.pallas_call(
        master_kernel,
        out_shape=jax.ShapeDtypeStruct((cols, slab_rows), jnp.float32),
        grid=(cols // block,),
        in_specs=[
            pl.BlockSpec(projection.shape, lambda i: (0, 0)),
            pl.BlockSpec((block, slab_rows), lambda i: (i, 0)),
            pl.BlockSpec(tall.shape, lambda i: (0, 0)),
        ],
        out_specs=pl.BlockSpec((block, slab_rows), lambda i: (i, 0)),
        compiler_params=pltpu.CompilerParams(vmem_limit_bytes=20 * 2**20),
        cost_estimate=pl.CostEstimate(
            flops=2 * cols * slab_rows * rank, bytes_accessed=8 * cols * slab_rows, transcendentals=0
        ),
    )(projection, master_t, tall)


def lay_kernel(*refs, first, count, block, fresh):
    refs = refs if fresh else refs[1:]
    pieces, out, (held, sems) = refs[:-3], refs[-3], refs[-2:]
    copies = [None] * held.shape[0]
    me = lax.axis_index("dp")
    for at in range(0, count, block):
        slot = at // block % len(copies)
        size = min(block, count - at)
        if copies[slot] is not None:
            copies[slot].wait()
        for masks, piece in zip(OWNER_MASKS, pieces):
            width = piece.shape[1]
            column = pl.multiple_of(other(me, masks) * width, 128)
            origin = at if piece.shape[0] == count else first + at
            held[slot, pl.ds(0, size), pl.ds(column, width)] = piece[pl.ds(origin, size), :]
        copies[slot] = pltpu.make_async_copy(
            held.at[slot, pl.ds(0, size), :], out.at[pl.ds(first + at, size), :], sems.at[slot]
        )
        copies[slot].start()
    for copy in copies:
        if copy is not None:
            copy.wait()


def lay(out, shape, span, pieces, block=96):
    fresh = out is None
    held = [] if fresh else [out]
    first, count = span
    return pl.pallas_call(
        functools.partial(lay_kernel, first=first, count=count, block=block, fresh=fresh),
        out_shape=jax.ShapeDtypeStruct(shape, jnp.bfloat16),
        in_specs=[ANY] * len(held) + [VMEM] * len(pieces),
        out_specs=ANY,
        scratch_shapes=[
            pltpu.VMEM((4, block, shape[1]), jnp.bfloat16),
            pltpu.SemaphoreType.DMA((4,)),
        ],
        input_output_aliases={} if fresh else {0: 0},
        compiler_params=pltpu.CompilerParams(vmem_limit_bytes=20 * 2**20),
        cost_estimate=pl.CostEstimate(flops=0, bytes_accessed=4 * count * shape[1], transcendentals=0),
    )(*held, *pieces)


def kernel_body(acts, grad_out, projection, moment_one, moment_two, master, n_dp, n_fsdp):
    cols = grad_out.shape[1]
    rank = projection.shape[1]
    rows = moment_one.shape[0]
    slab_rows = master.shape[0]
    wide = -(-cols // 128) * 128
    master_t = master.T

    def hop(value, mask):
        return send(value, "dp", n_dp, mask)

    def turn(value, masks):
        return lax.ppermute(value, "dp", [(i, i ^ masks[i & 1]) for i in range(n_dp)])

    def after(value, earlier):
        return lax.optimization_barrier((value, *earlier))[0] if earlier else value

    early, counts = chunk_sizes(cols)
    spans = [(sum(counts[:at]), count) for at, count in enumerate(counts)]
    taken = lax.slice_in_dim(master_t, 0, early[0], axis=0)
    ahead = [turn(taken, TURN_MASKS[0])]
    acts = after(acts, [taken])

    projected = jnp.dot(acts, projection, preferred_element_type=jnp.float32).astype(jnp.bfloat16)
    tokens = [projected] + [send(projected, "fsdp", n_fsdp, k) for k in range(1, n_fsdp)]
    parts = pl.pallas_call(
        functools.partial(partial_kernel, n_fsdp=n_fsdp, n_dp=n_dp),
        out_shape=[jax.ShapeDtypeStruct((rows, cols), jnp.bfloat16)] * n_dp,
        in_specs=[VMEM] * (1 + n_fsdp),
        out_specs=[VMEM] * n_dp,
        scratch_shapes=[
            pltpu.VMEM((n_fsdp * projected.shape[0], rank), jnp.bfloat16),
            pltpu.VMEM((rank, n_fsdp * projected.shape[0]), jnp.bfloat16),
        ],
        compiler_params=pltpu.CompilerParams(vmem_limit_bytes=16 * 2**20),
    )(grad_out.T, *tokens)
    parts = lax.optimization_barrier((*parts, *ahead))[:n_dp]
    parts = [part if masks == (0, 0) else turn(part, masks) for part, masks in zip(parts, SWAP_MASKS)]
    moment_one_new, moment_two_new, update = pl.pallas_call(
        adam_kernel,
        out_shape=[
            jax.ShapeDtypeStruct(moment_one.shape, jnp.float32),
            jax.ShapeDtypeStruct(moment_two.shape, jnp.float32),
            jax.ShapeDtypeStruct((rows, wide), jnp.bfloat16),
        ],
        in_specs=[VMEM] * (2 + n_dp),
        out_specs=[VMEM] * 3,
        compiler_params=pltpu.CompilerParams(vmem_limit_bytes=16 * 2**20),
    )(moment_one, moment_two, *parts)

    updates = {(0, 0): update, (1, 1): hop(update, 1)}
    for masks, relayed in (((6, 6), (7, 7)), ((2, 4), (5, 3)), ((4, 2), (3, 5))):
        updates[masks] = turn(update, masks)
        updates[relayed] = hop(updates[masks], 1)
    updates = [updates[masks] for masks in OWNER_MASKS]

    tall, *own = weights(projection, master_t, updates, spans[1:3])
    *late, own_first, whole = weights(projection, master_t, [tall], spans[3:] + spans[:1] + [(0, cols)])
    own = [own_first] + own + late
    got = {(0, 0): ahead_weights(projection, tall, ahead)}
    over = {(0, 0): hop(got[(0, 0)], 1)}
    master_new = new_master(projection, master_t, tall, cols // 4)

    later = range(1, len(counts))
    steps = [(phase, at) for phase in range(3) for at in later] + [(1, 0), (2, 0)]
    outs = [None]
    for step, (phase, at) in enumerate(steps):
        value = got[(0, at)] if phase == 2 else own[at]
        earlier = [got[steps[step - 2]]] if step >= 2 else []
        earlier += [over[steps[step - 4]]] if step >= 4 else []
        if step == 2:
            earlier.append(master_new)
        got[(phase, at)] = turn(after(value, earlier), TURN_MASKS[min(phase, 1)])
        held = [outs[len(counts) + step - len(steps)]] if step >= len(steps) - 2 else []
        over[(phase, at)] = hop(after(got[(phase, at)], held), 1)
        if step == 1:
            whole_c = hop(after(whole, [got[steps[1]]]), 1)
        if phase == 2:
            pieces = [whole, whole_c]
            for which in range(3):
                pieces += [got[(which, at)], over[(which, at)]]
            outs.append(lay(outs[-1], (cols, n_dp * slab_rows), spans[at], pieces))
    return (moment_one_new, moment_two_new, master_new.T, outs[-1].T)


def solution(mesh):
    n_dp, n_fsdp = mesh.shape["dp"], mesh.shape["fsdp"]

    def body(acts, grad_out, projection, moment_one, moment_two, master):
        args = (acts, grad_out, projection, moment_one, moment_two, master)
        fits = n_dp == 8 and n_fsdp == 4 and moment_one.shape[0] % 32 == 0 and master.shape[0] % 128 == 0
        if fits and grad_out.shape[1] % 64 == 0 and acts.shape[0] % 128 == 0:
            return kernel_body(*args, n_dp, n_fsdp)
        return plain_body(*args)

    in_specs = (
        P(("dp", "fsdp"), None),
        P("dp", "fsdp"),
        P(),
        P("dp", "fsdp"),
        P("dp", "fsdp"),
        P("dp", "fsdp"),
    )
    out_specs = (P("dp", "fsdp"), P("dp", "fsdp"), P("dp", "fsdp"), P(None, "fsdp"))
    return jax.shard_map(body, mesh=mesh, in_specs=in_specs, out_specs=out_specs, check_vma=False)
```

```python
import functools

import jax
import jax.numpy as jnp
from jax import lax
from jax.experimental import pallas as pl
from jax.experimental.pallas import tpu as pltpu
from jax.sharding import PartitionSpec as P

STEP = 1000


BETA_ONE = 0.9
BETA_TWO = 0.999
ADAM_EPS = 1e-08
LEARN_RATE = 0.01
CORRECT_ONE = 1.0 - BETA_ONE**STEP
CORRECT_TWO = 1.0 - BETA_TWO**STEP

VMEM = pl.BlockSpec(memory_space=pltpu.VMEM)
ANY = pl.BlockSpec(memory_space=pl.ANY)


TURN_MASKS = ((2, 4), (4, 2))
UPDATE_MASKS = tuple((k, k) for k in range(8))
SWAP_MASKS = ((0, 0), (4, 2), (2, 4), (6, 6), (7, 7), (5, 3), (3, 5), (1, 1))
OWNER_MASKS = ((0, 0), (1, 1), (2, 4), (5, 3), (4, 2), (3, 5), (6, 6), (7, 7))


def chunk_sizes(cols):
    small = cols // 80 * 16
    part = -(-(cols - 2 * small) // 48) * 16
    return (small,), (small, part, part, cols - 2 * part - 2 * small, small)


def adam(grad, moment_one, moment_two):
    moment_one_new = BETA_ONE * moment_one + (1.0 - BETA_ONE) * grad
    moment_two_new = BETA_TWO * moment_two + (1.0 - BETA_TWO) * grad * grad
    update = (
        moment_one_new / CORRECT_ONE / (jnp.sqrt(moment_two_new / CORRECT_TWO) + ADAM_EPS)
    ).astype(jnp.bfloat16)
    return moment_one_new, moment_two_new, update


def plain_body(acts, grad_out, projection, moment_one, moment_two, master):
    projected = jnp.dot(acts, projection, preferred_element_type=jnp.float32).astype(jnp.bfloat16)
    group_proj = lax.all_gather(projected, "fsdp", axis=0, tiled=True)
    partial_value = jnp.einsum(
        "tr,tc->rc", group_proj, grad_out, preferred_element_type=jnp.float32
    )
    partial_value = lax.optimization_barrier(partial_value.astype(jnp.bfloat16))
    grad = lax.psum_scatter(
        partial_value.astype(jnp.float32), "dp", scatter_dimension=0, tiled=True
    )
    moment_one_new, moment_two_new, update = adam(grad, moment_one, moment_two)
    slab_rows = master.shape[0]
    proj_slab = lax.dynamic_slice_in_dim(projection, lax.axis_index("dp") * slab_rows, slab_rows, 0)
    piece = lax.all_gather(update, "dp", axis=0, tiled=True)
    expanded = jnp.dot(proj_slab, piece, preferred_element_type=jnp.float32)
    master_new = master - LEARN_RATE * expanded
    weight_cols = lax.all_gather(master_new.astype(jnp.bfloat16), "dp", axis=0, tiled=True)
    return (moment_one_new, moment_two_new, master_new, weight_cols)


def send(value, axis, size, mask):
    return lax.ppermute(value, axis, [(i, i ^ mask) for i in range(size)])


def other(me, masks):
    return me ^ jnp.where((me & 1) == 0, masks[0], masks[1])


def take_kernel(source, out, sems, *, first):
    count = out.shape[0] // sems.shape[0]
    copies = []
    for at in range(sems.shape[0]):
        part = source.at[pl.ds(first + at * count, count), :]
        copies.append(pltpu.make_async_copy(part, out.at[pl.ds(at * count, count), :], sems.at[at]))
    for copy in copies:
        copy.start()
    for copy in copies:
        copy.wait()


def take(array, first, count):
    return pl.pallas_call(
        functools.partial(take_kernel, first=first),
        out_shape=jax.ShapeDtypeStruct((count, array.shape[1]), array.dtype),
        in_specs=[ANY],
        out_specs=ANY,
        scratch_shapes=[pltpu.SemaphoreType.DMA((count // 16,))],
        compiler_params=pltpu.CompilerParams(vmem_limit_bytes=60 * 2**20),
    )(array)


def partial_kernel(grad_t, *refs, n_fsdp, n_dp):
    pieces, outs, (tokens, across) = refs[:n_fsdp], refs[n_fsdp : n_fsdp + n_dp], refs[n_fsdp + n_dp :]
    count = pieces[0].shape[0]
    rows = outs[0].shape[0]
    me = lax.axis_index("fsdp")
    for k, piece in enumerate(pieces):
        tokens[pl.ds(pl.multiple_of((me ^ k) * count, count), count), :] = piece[...]
    across[...] = tokens[...].T
    me = lax.axis_index("dp")
    left = jnp.concatenate(
        [across[pl.ds(pl.multiple_of(other(me, masks) * rows, rows), rows), :] for masks in SWAP_MASKS], axis=0
    )
    result = lax.dot_general(
        left, grad_t[...], (((1,), (1,)), ((), ())), preferred_element_type=jnp.float32
    ).astype(jnp.bfloat16)
    for k, out in enumerate(outs):
        out[...] = result[k * rows : (k + 1) * rows, :]


def adam_kernel(moment_one, moment_two, *refs):
    parts, (one_new, two_new, update) = refs[:-3], refs[-3:]
    grad = parts[0][...].astype(jnp.float32)
    for part in parts[1:]:
        grad = grad + part[...].astype(jnp.float32)
    one, two, value = adam(grad, moment_one[...], moment_two[...])
    one_new[...] = one
    two_new[...] = two
    cols = value.shape[1]
    update[...] = jnp.zeros_like(update)
    update[:, :cols] = value


def expand(tall, slab, first, count):
    return lax.dot_general(
        tall[pl.ds(first, count), :], slab, (((1,), (1,)), ((), ())),
        preferred_element_type=jnp.float32,
    )


def weight_kernel(projection, master_t, *refs, n_in, spans, block):
    pieces, outs = refs[:n_in], refs[n_in:]
    me = lax.axis_index("dp")
    if n_in > 1:
        tall, wide = outs[0], outs[-1]
        outs = outs[1:-1]
        rows = pieces[0].shape[0]
        for k, piece in enumerate(pieces):
            wide[pl.ds(pl.multiple_of((me ^ k) * rows, rows), rows), :] = piece[...]
        tall[...] = wide[...].T
    else:
        tall = pieces[0]
    slab_rows = master_t.shape[1]
    slab = projection[pl.ds(pl.multiple_of(me * slab_rows, slab_rows), slab_rows), :]
    for (first, count), out in zip(spans, outs):
        for at in range(0, count, block):
            size = min(block, count - at)
            master_new = master_t[pl.ds(first + at, size), :] - LEARN_RATE * expand(
                tall, slab, first + at, size
            )
            out[pl.ds(at, size), :] = master_new.astype(jnp.bfloat16)


def weights(projection, master_t, pieces, spans):
    slab_rows, rank = master_t.shape[1], projection.shape[1]
    wide = pieces[0].shape[1]
    out_shape = [jax.ShapeDtypeStruct((count, slab_rows), jnp.bfloat16) for _, count in spans]
    scratch = []
    if len(pieces) > 1:
        out_shape = [jax.ShapeDtypeStruct((wide, rank), jnp.bfloat16)] + out_shape
        scratch = [pltpu.VMEM((rank, wide), jnp.bfloat16)]
    size = sum(count for _, count in spans) * slab_rows
    return pl.pallas_call(
        functools.partial(weight_kernel, n_in=len(pieces), spans=spans, block=144),
        out_shape=out_shape,
        in_specs=[VMEM] * (2 + len(pieces)),
        out_specs=[VMEM] * len(out_shape),
        scratch_shapes=scratch,
        compiler_params=pltpu.CompilerParams(vmem_limit_bytes=20 * 2**20),
        cost_estimate=pl.CostEstimate(flops=2 * size * rank, bytes_accessed=4 * size, transcendentals=0),
    )(projection, master_t, *pieces)


def ahead_kernel(projection, tall, *refs, block):
    parts, out = refs[:-1], refs[-1]
    slab_rows = out.shape[1]
    owner = other(lax.axis_index("dp"), TURN_MASKS[0])
    slab = projection[pl.ds(pl.multiple_of(owner * slab_rows, slab_rows), slab_rows), :]
    first = 0
    for part in parts:
        for at in range(0, part.shape[0], block):
            size = min(block, part.shape[0] - at)
            master_new = part[pl.ds(at, size), :] - LEARN_RATE * expand(tall, slab, first, size)
            out[pl.ds(first, size), :] = master_new.astype(jnp.bfloat16)
            first += size


def ahead_weights(projection, tall, parts):
    shape = (sum(part.shape[0] for part in parts), parts[0].shape[1])
    size = shape[0] * shape[1]
    return pl.pallas_call(
        functools.partial(ahead_kernel, block=144),
        out_shape=jax.ShapeDtypeStruct(shape, jnp.bfloat16),
        in_specs=[VMEM] * (2 + len(parts)),
        out_specs=VMEM,
        compiler_params=pltpu.CompilerParams(vmem_limit_bytes=20 * 2**20),
        cost_estimate=pl.CostEstimate(
            flops=2 * size * projection.shape[1], bytes_accessed=4 * size, transcendentals=0
        ),
    )(projection, tall, *parts)


def master_kernel(projection, master_t, tall, out):
    slab_rows = master_t.shape[1]
    first = pl.multiple_of(lax.axis_index("dp") * slab_rows, slab_rows)
    slab = projection[pl.ds(first, slab_rows), :]
    block = master_t.shape[0]
    first = pl.multiple_of(pl.program_id(0) * block, block)
    out[...] = master_t[...] - LEARN_RATE * expand(tall, slab, first, block)


def new_master(projection, master_t, tall, block):
    cols, slab_rows = master_t.shape
    rank = projection.shape[1]
    return pl.pallas_call(
        master_kernel,
        out_shape=jax.ShapeDtypeStruct((cols, slab_rows), jnp.float32),
        grid=(cols // block,),
        in_specs=[
            pl.BlockSpec(projection.shape, lambda i: (0, 0)),
            pl.BlockSpec((block, slab_rows), lambda i: (i, 0)),
            pl.BlockSpec(tall.shape, lambda i: (0, 0)),
        ],
        out_specs=pl.BlockSpec((block, slab_rows), lambda i: (i, 0)),
        compiler_params=pltpu.CompilerParams(vmem_limit_bytes=20 * 2**20),
        cost_estimate=pl.CostEstimate(
            flops=2 * cols * slab_rows * rank, bytes_accessed=8 * cols * slab_rows, transcendentals=0
        ),
    )(projection, master_t, tall)


def lay_kernel(*refs, first, count, block, fresh):
    refs = refs if fresh else refs[1:]
    pieces, out, (held, sems) = refs[:-3], refs[-3], refs[-2:]
    copies = [None] * held.shape[0]
    me = lax.axis_index("dp")
    for at in range(0, count, block):
        slot = at // block % len(copies)
        size = min(block, count - at)
        if copies[slot] is not None:
            copies[slot].wait()
        for masks, piece in zip(OWNER_MASKS, pieces):
            width = piece.shape[1]
            column = pl.multiple_of(other(me, masks) * width, 128)
            origin = at if piece.shape[0] == count else first + at
            held[slot, pl.ds(0, size), pl.ds(column, width)] = piece[pl.ds(origin, size), :]
        copies[slot] = pltpu.make_async_copy(
            held.at[slot, pl.ds(0, size), :], out.at[pl.ds(first + at, size), :], sems.at[slot]
        )
        copies[slot].start()
    for copy in copies:
        if copy is not None:
            copy.wait()


def lay(out, shape, span, pieces, block=96):
    fresh = out is None
    held = [] if fresh else [out]
    first, count = span
    return pl.pallas_call(
        functools.partial(lay_kernel, first=first, count=count, block=block, fresh=fresh),
        out_shape=jax.ShapeDtypeStruct(shape, jnp.bfloat16),
        in_specs=[ANY] * len(held) + [VMEM] * len(pieces),
        out_specs=ANY,
        scratch_shapes=[
            pltpu.VMEM((4, block, shape[1]), jnp.bfloat16),
            pltpu.SemaphoreType.DMA((4,)),
        ],
        input_output_aliases={} if fresh else {0: 0},
        compiler_params=pltpu.CompilerParams(vmem_limit_bytes=20 * 2**20),
        cost_estimate=pl.CostEstimate(flops=0, bytes_accessed=4 * count * shape[1], transcendentals=0),
    )(*held, *pieces)


def kernel_body(acts, grad_out, projection, moment_one, moment_two, master, n_dp, n_fsdp):
    cols = grad_out.shape[1]
    rank = projection.shape[1]
    rows = moment_one.shape[0]
    slab_rows = master.shape[0]
    wide = -(-cols // 128) * 128
    master_t = master.T

    def hop(value, mask):
        return send(value, "dp", n_dp, mask)

    def turn(value, masks):
        return lax.ppermute(value, "dp", [(i, i ^ masks[i & 1]) for i in range(n_dp)])

    def after(value, earlier):
        return lax.optimization_barrier((value, *earlier))[0] if earlier else value

    early, counts = chunk_sizes(cols)
    spans = [(sum(counts[:at]), count) for at, count in enumerate(counts)]
    taken = take(master_t, 0, early[0])
    ahead = [turn(taken, TURN_MASKS[0])]
    acts = after(acts, [taken])

    projected = jnp.dot(acts, projection, preferred_element_type=jnp.float32).astype(jnp.bfloat16)
    tokens = [projected] + [send(projected, "fsdp", n_fsdp, k) for k in range(1, n_fsdp)]
    parts = pl.pallas_call(
        functools.partial(partial_kernel, n_fsdp=n_fsdp, n_dp=n_dp),
        out_shape=[jax.ShapeDtypeStruct((rows, cols), jnp.bfloat16)] * n_dp,
        in_specs=[VMEM] * (1 + n_fsdp),
        out_specs=[VMEM] * n_dp,
        scratch_shapes=[
            pltpu.VMEM((n_fsdp * projected.shape[0], rank), jnp.bfloat16),
            pltpu.VMEM((rank, n_fsdp * projected.shape[0]), jnp.bfloat16),
        ],
        compiler_params=pltpu.CompilerParams(vmem_limit_bytes=16 * 2**20),
    )(grad_out.T, *tokens)
    parts = lax.optimization_barrier((*parts, *ahead))[:n_dp]
    parts = [part if masks == (0, 0) else turn(part, masks) for part, masks in zip(parts, SWAP_MASKS)]
    moment_one_new, moment_two_new, update = pl.pallas_call(
        adam_kernel,
        out_shape=[
            jax.ShapeDtypeStruct(moment_one.shape, jnp.float32),
            jax.ShapeDtypeStruct(moment_two.shape, jnp.float32),
            jax.ShapeDtypeStruct((rows, wide), jnp.bfloat16),
        ],
        in_specs=[VMEM] * (2 + n_dp),
        out_specs=[VMEM] * 3,
        compiler_params=pltpu.CompilerParams(vmem_limit_bytes=16 * 2**20),
    )(moment_one, moment_two, *parts)

    updates = {0: update}
    for k in (6, 2, 4, 1):
        updates[k] = hop(update, k)
    for k in (2, 4, 6):
        updates[k ^ 1] = hop(updates[k], 1)
    updates = [updates[k] for k in range(n_dp)]

    tall, *own = weights(projection, master_t, updates, spans[1:3])
    *late, own_first, whole = weights(projection, master_t, [tall], spans[3:] + spans[:1] + [(0, cols)])
    own = [own_first] + own + late
    got = {(0, 0): ahead_weights(projection, tall, ahead)}
    over = {(0, 0): hop(got[(0, 0)], 1)}
    master_new = new_master(projection, master_t, tall, cols // 4)

    later = range(1, len(counts))
    steps = [(phase, at) for phase in range(3) for at in later] + [(1, 0), (2, 0)]
    outs = [None]
    for step, (phase, at) in enumerate(steps):
        value = got[(0, at)] if phase == 2 else own[at]
        earlier = [got[steps[step - 2]]] if step >= 2 else []
        earlier += [over[steps[step - 4]]] if step >= 4 else []
        if step == 2:
            earlier.append(master_new)
        got[(phase, at)] = turn(after(value, earlier), TURN_MASKS[min(phase, 1)])
        held = [outs[len(counts) + step - len(steps)]] if step >= len(steps) - 2 else []
        over[(phase, at)] = hop(after(got[(phase, at)], held), 1)
        if step == 1:
            whole_c = hop(after(whole, [got[steps[1]]]), 1)
        if phase == 2:
            pieces = [whole, whole_c]
            for which in range(3):
                pieces += [got[(which, at)], over[(which, at)]]
            outs.append(lay(outs[-1], (cols, n_dp * slab_rows), spans[at], pieces))
    return (moment_one_new, moment_two_new, master_new.T, outs[-1].T)


def solution(mesh):
    n_dp, n_fsdp = mesh.shape["dp"], mesh.shape["fsdp"]

    def body(acts, grad_out, projection, moment_one, moment_two, master):
        args = (acts, grad_out, projection, moment_one, moment_two, master)
        fits = n_dp == 8 and n_fsdp == 4 and moment_one.shape[0] % 32 == 0 and master.shape[0] % 128 == 0
        if fits and grad_out.shape[1] % 64 == 0 and acts.shape[0] % 128 == 0:
            return kernel_body(*args, n_dp, n_fsdp)
        return plain_body(*args)

    in_specs = (
        P(("dp", "fsdp"), None),
        P("dp", "fsdp"),
        P(),
        P("dp", "fsdp"),
        P("dp", "fsdp"),
        P("dp", "fsdp"),
    )
    out_specs = (P("dp", "fsdp"), P("dp", "fsdp"), P("dp", "fsdp"), P(None, "fsdp"))
    return jax.shard_map(body, mesh=mesh, in_specs=in_specs, out_specs=out_specs, check_vma=False)
```

```python
import functools

import jax
import jax.numpy as jnp
from jax import lax
from jax.experimental import pallas as pl
from jax.experimental.pallas import tpu as pltpu
from jax.sharding import PartitionSpec as P

STEP = 1000


BETA_ONE = 0.9
BETA_TWO = 0.999
ADAM_EPS = 1e-08
LEARN_RATE = 0.01
CORRECT_ONE = 1.0 - BETA_ONE**STEP
CORRECT_TWO = 1.0 - BETA_TWO**STEP

VMEM = pl.BlockSpec(memory_space=pltpu.VMEM)
ANY = pl.BlockSpec(memory_space=pl.ANY)


TURN_MASKS = ((2, 4), (4, 2))
UPDATE_MASKS = tuple((k, k) for k in range(8))
SWAP_MASKS = ((0, 0), (4, 2), (2, 4), (6, 6), (7, 7), (5, 3), (3, 5), (1, 1))
OWNER_MASKS = ((0, 0), (1, 1), (2, 4), (5, 3), (4, 2), (3, 5), (6, 6), (7, 7))


def chunk_sizes(cols):
    small = cols // 80 * 16
    part = -(-(cols - 2 * small) // 48) * 16
    return (small,), (small, part, part, cols - 2 * part - 2 * small, small)


def adam(grad, moment_one, moment_two):
    moment_one_new = BETA_ONE * moment_one + (1.0 - BETA_ONE) * grad
    moment_two_new = BETA_TWO * moment_two + (1.0 - BETA_TWO) * grad * grad
    update = (
        moment_one_new / CORRECT_ONE / (jnp.sqrt(moment_two_new / CORRECT_TWO) + ADAM_EPS)
    ).astype(jnp.bfloat16)
    return moment_one_new, moment_two_new, update


def plain_body(acts, grad_out, projection, moment_one, moment_two, master):
    projected = jnp.dot(acts, projection, preferred_element_type=jnp.float32).astype(jnp.bfloat16)
    group_proj = lax.all_gather(projected, "fsdp", axis=0, tiled=True)
    partial_value = jnp.einsum(
        "tr,tc->rc", group_proj, grad_out, preferred_element_type=jnp.float32
    )
    partial_value = lax.optimization_barrier(partial_value.astype(jnp.bfloat16))
    grad = lax.psum_scatter(
        partial_value.astype(jnp.float32), "dp", scatter_dimension=0, tiled=True
    )
    moment_one_new, moment_two_new, update = adam(grad, moment_one, moment_two)
    slab_rows = master.shape[0]
    proj_slab = lax.dynamic_slice_in_dim(projection, lax.axis_index("dp") * slab_rows, slab_rows, 0)
    piece = lax.all_gather(update, "dp", axis=0, tiled=True)
    expanded = jnp.dot(proj_slab, piece, preferred_element_type=jnp.float32)
    master_new = master - LEARN_RATE * expanded
    weight_cols = lax.all_gather(master_new.astype(jnp.bfloat16), "dp", axis=0, tiled=True)
    return (moment_one_new, moment_two_new, master_new, weight_cols)


def send(value, axis, size, mask):
    return lax.ppermute(value, axis, [(i, i ^ mask) for i in range(size)])


def other(me, masks):
    return me ^ jnp.where((me & 1) == 0, masks[0], masks[1])


def take_kernel(source, out, sems, *, first):
    count = out.shape[0] // sems.shape[0]
    copies = []
    for at in range(sems.shape[0]):
        part = source.at[pl.ds(first + at * count, count), :]
        copies.append(pltpu.make_async_copy(part, out.at[pl.ds(at * count, count), :], sems.at[at]))
    for copy in copies:
        copy.start()
    for copy in copies:
        copy.wait()


def take(array, first, count):
    return pl.pallas_call(
        functools.partial(take_kernel, first=first),
        out_shape=jax.ShapeDtypeStruct((count, array.shape[1]), array.dtype),
        in_specs=[ANY],
        out_specs=VMEM,
        scratch_shapes=[pltpu.SemaphoreType.DMA((count // 16,))],
        compiler_params=pltpu.CompilerParams(vmem_limit_bytes=60 * 2**20),
    )(array)


def partial_kernel(grad_t, *refs, n_fsdp, n_dp):
    pieces, outs, (tokens, across) = refs[:n_fsdp], refs[n_fsdp : n_fsdp + n_dp], refs[n_fsdp + n_dp :]
    count = pieces[0].shape[0]
    rows = outs[0].shape[0]
    me = lax.axis_index("fsdp")
    for k, piece in enumerate(pieces):
        tokens[pl.ds(pl.multiple_of((me ^ k) * count, count), count), :] = piece[...]
    across[...] = tokens[...].T
    me = lax.axis_index("dp")
    left = jnp.concatenate(
        [across[pl.ds(pl.multiple_of(other(me, masks) * rows, rows), rows), :] for masks in SWAP_MASKS], axis=0
    )
    result = lax.dot_general(
        left, grad_t[...], (((1,), (1,)), ((), ())), preferred_element_type=jnp.float32
    ).astype(jnp.bfloat16)
    for k, out in enumerate(outs):
        out[...] = result[k * rows : (k + 1) * rows, :]


def adam_kernel(moment_one, moment_two, *refs):
    parts, (one_new, two_new, update) = refs[:-3], refs[-3:]
    grad = parts[0][...].astype(jnp.float32)
    for part in parts[1:]:
        grad = grad + part[...].astype(jnp.float32)
    one, two, value = adam(grad, moment_one[...], moment_two[...])
    one_new[...] = one
    two_new[...] = two
    cols = value.shape[1]
    update[...] = jnp.zeros_like(update)
    update[:, :cols] = value


def expand(tall, slab, first, count):
    return lax.dot_general(
        tall[pl.ds(first, count), :], slab, (((1,), (1,)), ((), ())),
        preferred_element_type=jnp.float32,
    )


def weight_kernel(projection, master_t, *refs, n_in, spans, block):
    pieces, outs = refs[:n_in], refs[n_in:]
    me = lax.axis_index("dp")
    if n_in > 1:
        tall, wide = outs[0], outs[-1]
        outs = outs[1:-1]
        rows = pieces[0].shape[0]
        for k, piece in enumerate(pieces):
            wide[pl.ds(pl.multiple_of((me ^ k) * rows, rows), rows), :] = piece[...]
        tall[...] = wide[...].T
    else:
        tall = pieces[0]
    slab_rows = master_t.shape[1]
    slab = projection[pl.ds(pl.multiple_of(me * slab_rows, slab_rows), slab_rows), :]
    for (first, count), out in zip(spans, outs):
        for at in range(0, count, block):
            size = min(block, count - at)
            master_new = master_t[pl.ds(first + at, size), :] - LEARN_RATE * expand(
                tall, slab, first + at, size
            )
            out[pl.ds(at, size), :] = master_new.astype(jnp.bfloat16)


def weights(projection, master_t, pieces, spans):
    slab_rows, rank = master_t.shape[1], projection.shape[1]
    wide = pieces[0].shape[1]
    out_shape = [jax.ShapeDtypeStruct((count, slab_rows), jnp.bfloat16) for _, count in spans]
    scratch = []
    if len(pieces) > 1:
        out_shape = [jax.ShapeDtypeStruct((wide, rank), jnp.bfloat16)] + out_shape
        scratch = [pltpu.VMEM((rank, wide), jnp.bfloat16)]
    size = sum(count for _, count in spans) * slab_rows
    return pl.pallas_call(
        functools.partial(weight_kernel, n_in=len(pieces), spans=spans, block=144),
        out_shape=out_shape,
        in_specs=[VMEM] * (2 + len(pieces)),
        out_specs=[VMEM] * len(out_shape),
        scratch_shapes=scratch,
        compiler_params=pltpu.CompilerParams(vmem_limit_bytes=20 * 2**20),
        cost_estimate=pl.CostEstimate(flops=2 * size * rank, bytes_accessed=4 * size, transcendentals=0),
    )(projection, master_t, *pieces)


def ahead_kernel(projection, tall, *refs, block):
    parts, out = refs[:-1], refs[-1]
    slab_rows = out.shape[1]
    owner = other(lax.axis_index("dp"), TURN_MASKS[0])
    slab = projection[pl.ds(pl.multiple_of(owner * slab_rows, slab_rows), slab_rows), :]
    first = 0
    for part in parts:
        for at in range(0, part.shape[0], block):
            size = min(block, part.shape[0] - at)
            master_new = part[pl.ds(at, size), :] - LEARN_RATE * expand(tall, slab, first, size)
            out[pl.ds(first, size), :] = master_new.astype(jnp.bfloat16)
            first += size


def ahead_weights(projection, tall, parts):
    shape = (sum(part.shape[0] for part in parts), parts[0].shape[1])
    size = shape[0] * shape[1]
    return pl.pallas_call(
        functools.partial(ahead_kernel, block=144),
        out_shape=jax.ShapeDtypeStruct(shape, jnp.bfloat16),
        in_specs=[VMEM] * (2 + len(parts)),
        out_specs=VMEM,
        compiler_params=pltpu.CompilerParams(vmem_limit_bytes=20 * 2**20),
        cost_estimate=pl.CostEstimate(
            flops=2 * size * projection.shape[1], bytes_accessed=4 * size, transcendentals=0
        ),
    )(projection, tall, *parts)


def master_kernel(projection, master_t, tall, out):
    slab_rows = master_t.shape[1]
    first = pl.multiple_of(lax.axis_index("dp") * slab_rows, slab_rows)
    slab = projection[pl.ds(first, slab_rows), :]
    block = master_t.shape[0]
    first = pl.multiple_of(pl.program_id(0) * block, block)
    out[...] = master_t[...] - LEARN_RATE * expand(tall, slab, first, block)


def new_master(projection, master_t, tall, block):
    cols, slab_rows = master_t.shape
    rank = projection.shape[1]
    return pl.pallas_call(
        master_kernel,
        out_shape=jax.ShapeDtypeStruct((cols, slab_rows), jnp.float32),
        grid=(cols // block,),
        in_specs=[
            pl.BlockSpec(projection.shape, lambda i: (0, 0)),
            pl.BlockSpec((block, slab_rows), lambda i: (i, 0)),
            pl.BlockSpec(tall.shape, lambda i: (0, 0)),
        ],
        out_specs=pl.BlockSpec((block, slab_rows), lambda i: (i, 0)),
        compiler_params=pltpu.CompilerParams(vmem_limit_bytes=20 * 2**20),
        cost_estimate=pl.CostEstimate(
            flops=2 * cols * slab_rows * rank, bytes_accessed=8 * cols * slab_rows, transcendentals=0
        ),
    )(projection, master_t, tall)


def lay_kernel(*refs, first, count, kinds, fresh):
    refs = refs if fresh else refs[1:]
    pieces, out, sems = refs[:-2], refs[-2], refs[-1]
    me = lax.axis_index("dp")
    copies = []
    for at, (kind, piece) in enumerate(zip(kinds, pieces)):
        width = piece.shape[1]
        column = pl.multiple_of(other(me, OWNER_MASKS[kind]) * width, 128)
        part = piece if piece.shape[0] == count else piece.at[pl.ds(first, count), :]
        target = out.at[pl.ds(first, count), pl.ds(column, width)]
        copies.append(pltpu.make_async_copy(part, target, sems.at[at]))
    for copy in copies:
        copy.start()
    for copy in copies:
        copy.wait()


def lay(out, shape, span, kinds, pieces):
    fresh = out is None
    held = [] if fresh else [out]
    first, count = span
    return pl.pallas_call(
        functools.partial(lay_kernel, first=first, count=count, kinds=kinds, fresh=fresh),
        out_shape=jax.ShapeDtypeStruct(shape, jnp.bfloat16),
        in_specs=[ANY] * len(held) + [VMEM] * len(pieces),
        out_specs=ANY,
        scratch_shapes=[pltpu.SemaphoreType.DMA((len(pieces),))],
        input_output_aliases={} if fresh else {0: 0},
        compiler_params=pltpu.CompilerParams(vmem_limit_bytes=20 * 2**20),
        cost_estimate=pl.CostEstimate(
            flops=0, bytes_accessed=4 * count * pieces[0].shape[1] * len(pieces), transcendentals=0
        ),
    )(*held, *pieces)


def kernel_body(acts, grad_out, projection, moment_one, moment_two, master, n_dp, n_fsdp):
    cols = grad_out.shape[1]
    rank = projection.shape[1]
    rows = moment_one.shape[0]
    slab_rows = master.shape[0]
    wide = -(-cols // 128) * 128
    master_t = master.T

    def hop(value, mask):
        return send(value, "dp", n_dp, mask)

    def turn(value, masks):
        return lax.ppermute(value, "dp", [(i, i ^ masks[i & 1]) for i in range(n_dp)])

    def after(value, earlier):
        return lax.optimization_barrier((value, *earlier))[0] if earlier else value

    early, counts = chunk_sizes(cols)
    spans = [(sum(counts[:at]), count) for at, count in enumerate(counts)]
    taken = take(master_t, 0, early[0])
    ahead = [turn(taken, TURN_MASKS[0])]
    acts = after(acts, [taken])

    projected = jnp.dot(acts, projection, preferred_element_type=jnp.float32).astype(jnp.bfloat16)
    tokens = [projected] + [send(projected, "fsdp", n_fsdp, k) for k in range(1, n_fsdp)]
    parts = pl.pallas_call(
        functools.partial(partial_kernel, n_fsdp=n_fsdp, n_dp=n_dp),
        out_shape=[jax.ShapeDtypeStruct((rows, cols), jnp.bfloat16)] * n_dp,
        in_specs=[VMEM] * (1 + n_fsdp),
        out_specs=[VMEM] * n_dp,
        scratch_shapes=[
            pltpu.VMEM((n_fsdp * projected.shape[0], rank), jnp.bfloat16),
            pltpu.VMEM((rank, n_fsdp * projected.shape[0]), jnp.bfloat16),
        ],
        compiler_params=pltpu.CompilerParams(vmem_limit_bytes=16 * 2**20),
    )(grad_out.T, *tokens)
    parts = lax.optimization_barrier((*parts, *ahead))[:n_dp]
    parts = [part if masks == (0, 0) else turn(part, masks) for part, masks in zip(parts, SWAP_MASKS)]
    moment_one_new, moment_two_new, update = pl.pallas_call(
        adam_kernel,
        out_shape=[
            jax.ShapeDtypeStruct(moment_one.shape, jnp.float32),
            jax.ShapeDtypeStruct(moment_two.shape, jnp.float32),
            jax.ShapeDtypeStruct((rows, wide), jnp.bfloat16),
        ],
        in_specs=[VMEM] * (2 + n_dp),
        out_specs=[VMEM] * 3,
        compiler_params=pltpu.CompilerParams(vmem_limit_bytes=16 * 2**20),
    )(moment_one, moment_two, *parts)

    updates = {0: update}
    for k in (6, 2, 4, 1):
        updates[k] = hop(update, k)
    for k in (2, 4, 6):
        updates[k ^ 1] = hop(updates[k], 1)
    updates = [updates[k] for k in range(n_dp)]

    tall, *own = weights(projection, master_t, updates, spans[1:3])
    *late, own_first, whole = weights(projection, master_t, [tall], spans[3:] + spans[:1] + [(0, cols)])
    own = [own_first] + own + late
    got = {(0, 0): ahead_weights(projection, tall, ahead)}
    over = {(0, 0): hop(got[(0, 0)], 1)}
    master_new = new_master(projection, master_t, tall, cols // 4)

    later = range(1, len(counts))
    steps = [(phase, at) for phase in range(3) for at in later] + [(1, 0), (2, 0)]
    outs = [None]
    for step, (phase, at) in enumerate(steps):
        value = got[(0, at)] if phase == 2 else own[at]
        earlier = [got[steps[step - 2]]] if step >= 2 else []
        earlier += [over[steps[step - 4]]] if step >= 4 else []
        if step == 2:
            earlier.append(master_new)
        got[(phase, at)] = turn(after(value, earlier), TURN_MASKS[min(phase, 1)])
        held = [outs[len(counts) + step - len(steps)]] if step >= len(steps) - 2 else []
        over[(phase, at)] = hop(after(got[(phase, at)], held), 1)
        if step == 1:
            whole_c = hop(after(whole, [got[steps[1]]]), 1)
        if phase == 2:
            pieces = [whole, whole_c]
            for which in range(3):
                pieces += [got[(which, at)], over[(which, at)]]
            kinds = tuple(range(len(pieces)))
            shape = (cols, n_dp * slab_rows)
            if step < len(steps) - 1:
                outs.append(lay(outs[-1], shape, spans[at], kinds, pieces))
            else:
                outs.append(lay(outs[-1], shape, spans[at], kinds[:-1], pieces[:-1]))
                outs.append(lay(outs[-1], shape, spans[at], kinds[-1:], pieces[-1:]))
    return (moment_one_new, moment_two_new, master_new.T, outs[-1].T)


def solution(mesh):
    n_dp, n_fsdp = mesh.shape["dp"], mesh.shape["fsdp"]

    def body(acts, grad_out, projection, moment_one, moment_two, master):
        args = (acts, grad_out, projection, moment_one, moment_two, master)
        fits = n_dp == 8 and n_fsdp == 4 and moment_one.shape[0] % 32 == 0 and master.shape[0] % 128 == 0
        if fits and grad_out.shape[1] % 64 == 0 and acts.shape[0] % 128 == 0:
            return kernel_body(*args, n_dp, n_fsdp)
        return plain_body(*args)

    in_specs = (
        P(("dp", "fsdp"), None),
        P("dp", "fsdp"),
        P(),
        P("dp", "fsdp"),
        P("dp", "fsdp"),
        P("dp", "fsdp"),
    )
    out_specs = (P("dp", "fsdp"), P("dp", "fsdp"), P("dp", "fsdp"), P(None, "fsdp"))
    return jax.shard_map(body, mesh=mesh, in_specs=in_specs, out_specs=out_specs, check_vma=False)
```

```python
import functools

import jax
import jax.numpy as jnp
from jax import lax
from jax.experimental import pallas as pl
from jax.experimental.pallas import tpu as pltpu
from jax.sharding import PartitionSpec as P

STEP = 1000


BETA_ONE = 0.9
BETA_TWO = 0.999
ADAM_EPS = 1e-08
LEARN_RATE = 0.01
CORRECT_ONE = 1.0 - BETA_ONE**STEP
CORRECT_TWO = 1.0 - BETA_TWO**STEP

VMEM = pl.BlockSpec(memory_space=pltpu.VMEM)
ANY = pl.BlockSpec(memory_space=pl.ANY)


TURN_MASKS = ((2, 4), (4, 2))
UPDATE_MASKS = tuple((k, k) for k in range(8))
SWAP_MASKS = ((0, 0), (4, 2), (2, 4), (6, 6), (7, 7), (5, 3), (3, 5), (1, 1))
OWNER_MASKS = ((0, 0), (1, 1), (2, 4), (5, 3), (4, 2), (3, 5), (6, 6), (7, 7))


def chunk_sizes(cols):
    small = cols // 80 * 16
    part = -(-(cols - 2 * small) // 48) * 16
    return (small,), (small, part, part, cols - 2 * part - 2 * small, small)


def adam(grad, moment_one, moment_two):
    moment_one_new = BETA_ONE * moment_one + (1.0 - BETA_ONE) * grad
    moment_two_new = BETA_TWO * moment_two + (1.0 - BETA_TWO) * grad * grad
    update = (
        moment_one_new / CORRECT_ONE / (jnp.sqrt(moment_two_new / CORRECT_TWO) + ADAM_EPS)
    ).astype(jnp.bfloat16)
    return moment_one_new, moment_two_new, update


def plain_body(acts, grad_out, projection, moment_one, moment_two, master):
    projected = jnp.dot(acts, projection, preferred_element_type=jnp.float32).astype(jnp.bfloat16)
    group_proj = lax.all_gather(projected, "fsdp", axis=0, tiled=True)
    partial_value = jnp.einsum(
        "tr,tc->rc", group_proj, grad_out, preferred_element_type=jnp.float32
    )
    partial_value = lax.optimization_barrier(partial_value.astype(jnp.bfloat16))
    grad = lax.psum_scatter(
        partial_value.astype(jnp.float32), "dp", scatter_dimension=0, tiled=True
    )
    moment_one_new, moment_two_new, update = adam(grad, moment_one, moment_two)
    slab_rows = master.shape[0]
    proj_slab = lax.dynamic_slice_in_dim(projection, lax.axis_index("dp") * slab_rows, slab_rows, 0)
    piece = lax.all_gather(update, "dp", axis=0, tiled=True)
    expanded = jnp.dot(proj_slab, piece, preferred_element_type=jnp.float32)
    master_new = master - LEARN_RATE * expanded
    weight_cols = lax.all_gather(master_new.astype(jnp.bfloat16), "dp", axis=0, tiled=True)
    return (moment_one_new, moment_two_new, master_new, weight_cols)


def send(value, axis, size, mask):
    return lax.ppermute(value, axis, [(i, i ^ mask) for i in range(size)])


def other(me, masks):
    return me ^ jnp.where((me & 1) == 0, masks[0], masks[1])


def take_kernel(source, out, sems, *, first):
    count = out.shape[0] // sems.shape[0]
    copies = []
    for at in range(sems.shape[0]):
        part = source.at[pl.ds(first + at * count, count), :]
        copies.append(pltpu.make_async_copy(part, out.at[pl.ds(at * count, count), :], sems.at[at]))
    for copy in copies:
        copy.start()
    for copy in copies:
        copy.wait()


def take(array, first, count):
    return pl.pallas_call(
        functools.partial(take_kernel, first=first),
        out_shape=jax.ShapeDtypeStruct((count, array.shape[1]), array.dtype),
        in_specs=[ANY],
        out_specs=VMEM,
        scratch_shapes=[pltpu.SemaphoreType.DMA((count // 16,))],
        compiler_params=pltpu.CompilerParams(vmem_limit_bytes=60 * 2**20),
    )(array)


def partial_kernel(grad_t, *refs, n_fsdp, n_dp):
    pieces, outs, (tokens, across) = refs[:n_fsdp], refs[n_fsdp : n_fsdp + n_dp], refs[n_fsdp + n_dp :]
    count = pieces[0].shape[0]
    rows = outs[0].shape[0]
    me = lax.axis_index("fsdp")
    for k, piece in enumerate(pieces):
        tokens[pl.ds(pl.multiple_of((me ^ k) * count, count), count), :] = piece[...]
    across[...] = tokens[...].T
    me = lax.axis_index("dp")
    left = jnp.concatenate(
        [across[pl.ds(pl.multiple_of(other(me, masks) * rows, rows), rows), :] for masks in SWAP_MASKS], axis=0
    )
    result = lax.dot_general(
        left, grad_t[...], (((1,), (1,)), ((), ())), preferred_element_type=jnp.float32
    ).astype(jnp.bfloat16)
    for k, out in enumerate(outs):
        out[...] = result[k * rows : (k + 1) * rows, :]


def adam_kernel(moment_one, moment_two, *refs):
    parts, (one_new, two_new, update) = refs[:-3], refs[-3:]
    grad = parts[0][...].astype(jnp.float32)
    for part in parts[1:]:
        grad = grad + part[...].astype(jnp.float32)
    one, two, value = adam(grad, moment_one[...], moment_two[...])
    one_new[...] = one
    two_new[...] = two
    cols = value.shape[1]
    update[...] = jnp.zeros_like(update)
    update[:, :cols] = value


def expand(tall, slab, first, count):
    return lax.dot_general(
        tall[pl.ds(first, count), :], slab, (((1,), (1,)), ((), ())),
        preferred_element_type=jnp.float32,
    )


def weight_kernel(projection, master_t, *refs, n_in, spans, block):
    pieces, outs = refs[:n_in], refs[n_in:]
    me = lax.axis_index("dp")
    if n_in > 1:
        tall, wide = outs[0], outs[-1]
        outs = outs[1:-1]
        rows = pieces[0].shape[0]
        for k, piece in enumerate(pieces):
            wide[pl.ds(pl.multiple_of((me ^ k) * rows, rows), rows), :] = piece[...]
        tall[...] = wide[...].T
    else:
        tall = pieces[0]
    slab_rows = master_t.shape[1]
    slab = projection[pl.ds(pl.multiple_of(me * slab_rows, slab_rows), slab_rows), :]
    for (first, count), out in zip(spans, outs):
        for at in range(0, count, block):
            size = min(block, count - at)
            master_new = master_t[pl.ds(first + at, size), :] - LEARN_RATE * expand(
                tall, slab, first + at, size
            )
            out[pl.ds(at, size), :] = master_new.astype(jnp.bfloat16)


def weights(projection, master_t, pieces, spans):
    slab_rows, rank = master_t.shape[1], projection.shape[1]
    wide = pieces[0].shape[1]
    out_shape = [jax.ShapeDtypeStruct((count, slab_rows), jnp.bfloat16) for _, count in spans]
    scratch = []
    if len(pieces) > 1:
        out_shape = [jax.ShapeDtypeStruct((wide, rank), jnp.bfloat16)] + out_shape
        scratch = [pltpu.VMEM((rank, wide), jnp.bfloat16)]
    size = sum(count for _, count in spans) * slab_rows
    return pl.pallas_call(
        functools.partial(weight_kernel, n_in=len(pieces), spans=spans, block=144),
        out_shape=out_shape,
        in_specs=[VMEM] * (2 + len(pieces)),
        out_specs=[VMEM] * len(out_shape),
        scratch_shapes=scratch,
        compiler_params=pltpu.CompilerParams(vmem_limit_bytes=20 * 2**20),
        cost_estimate=pl.CostEstimate(flops=2 * size * rank, bytes_accessed=4 * size, transcendentals=0),
    )(projection, master_t, *pieces)


def ahead_kernel(projection, tall, *refs, block):
    parts, out = refs[:-1], refs[-1]
    slab_rows = out.shape[1]
    owner = other(lax.axis_index("dp"), TURN_MASKS[0])
    slab = projection[pl.ds(pl.multiple_of(owner * slab_rows, slab_rows), slab_rows), :]
    first = 0
    for part in parts:
        for at in range(0, part.shape[0], block):
            size = min(block, part.shape[0] - at)
            master_new = part[pl.ds(at, size), :] - LEARN_RATE * expand(tall, slab, first, size)
            out[pl.ds(first, size), :] = master_new.astype(jnp.bfloat16)
            first += size


def ahead_weights(projection, tall, parts):
    shape = (sum(part.shape[0] for part in parts), parts[0].shape[1])
    size = shape[0] * shape[1]
    return pl.pallas_call(
        functools.partial(ahead_kernel, block=144),
        out_shape=jax.ShapeDtypeStruct(shape, jnp.bfloat16),
        in_specs=[VMEM] * (2 + len(parts)),
        out_specs=VMEM,
        compiler_params=pltpu.CompilerParams(vmem_limit_bytes=20 * 2**20),
        cost_estimate=pl.CostEstimate(
            flops=2 * size * projection.shape[1], bytes_accessed=4 * size, transcendentals=0
        ),
    )(projection, tall, *parts)


def master_kernel(projection, master_t, tall, out):
    slab_rows = master_t.shape[1]
    first = pl.multiple_of(lax.axis_index("dp") * slab_rows, slab_rows)
    slab = projection[pl.ds(first, slab_rows), :]
    block = master_t.shape[0]
    first = pl.multiple_of(pl.program_id(0) * block, block)
    out[...] = master_t[...] - LEARN_RATE * expand(tall, slab, first, block)


def new_master(projection, master_t, tall, block):
    cols, slab_rows = master_t.shape
    rank = projection.shape[1]
    return pl.pallas_call(
        master_kernel,
        out_shape=jax.ShapeDtypeStruct((cols, slab_rows), jnp.float32),
        grid=(cols // block,),
        in_specs=[
            pl.BlockSpec(projection.shape, lambda i: (0, 0)),
            pl.BlockSpec((block, slab_rows), lambda i: (i, 0)),
            pl.BlockSpec(tall.shape, lambda i: (0, 0)),
        ],
        out_specs=pl.BlockSpec((block, slab_rows), lambda i: (i, 0)),
        compiler_params=pltpu.CompilerParams(vmem_limit_bytes=20 * 2**20),
        cost_estimate=pl.CostEstimate(
            flops=2 * cols * slab_rows * rank, bytes_accessed=8 * cols * slab_rows, transcendentals=0
        ),
    )(projection, master_t, tall)


def lay_kernel(*refs, places, fresh):
    refs = refs if fresh else refs[1:]
    pieces, out, sems = refs[:-2], refs[-2], refs[-1]
    me = lax.axis_index("dp")
    copies = []
    for at, (index, first, count, kind) in enumerate(places):
        piece = pieces[index]
        width = piece.shape[1]
        column = pl.multiple_of(other(me, OWNER_MASKS[kind]) * width, 128)
        part = piece if piece.shape[0] == count else piece.at[pl.ds(first, count), :]
        target = out.at[pl.ds(first, count), pl.ds(column, width)]
        copies.append(pltpu.make_async_copy(part, target, sems.at[at]))
    for copy in copies:
        copy.start()
    for copy in copies:
        copy.wait()


def lay(out, shape, parts):
    fresh = out is None
    held = [] if fresh else [out]
    pieces = []
    places = []
    for first, count, kind, piece in parts:
        known = [at for at, other_piece in enumerate(pieces) if other_piece is piece]
        if not known:
            pieces.append(piece)
        places.append((known[0] if known else len(pieces) - 1, first, count, kind))
    size = sum(count for _, _, count, _ in places) * pieces[0].shape[1]
    return pl.pallas_call(
        functools.partial(lay_kernel, places=tuple(places), fresh=fresh),
        out_shape=jax.ShapeDtypeStruct(shape, jnp.bfloat16),
        in_specs=[ANY] * len(held) + [VMEM] * len(pieces),
        out_specs=ANY,
        scratch_shapes=[pltpu.SemaphoreType.DMA((len(places),))],
        input_output_aliases={} if fresh else {0: 0},
        compiler_params=pltpu.CompilerParams(vmem_limit_bytes=20 * 2**20),
        cost_estimate=pl.CostEstimate(flops=0, bytes_accessed=4 * size, transcendentals=0),
    )(*held, *pieces)


def kernel_body(acts, grad_out, projection, moment_one, moment_two, master, n_dp, n_fsdp):
    cols = grad_out.shape[1]
    rank = projection.shape[1]
    rows = moment_one.shape[0]
    slab_rows = master.shape[0]
    wide = -(-cols // 128) * 128
    master_t = master.T

    def hop(value, mask):
        return send(value, "dp", n_dp, mask)

    def turn(value, masks):
        return lax.ppermute(value, "dp", [(i, i ^ masks[i & 1]) for i in range(n_dp)])

    def after(value, earlier):
        return lax.optimization_barrier((value, *earlier))[0] if earlier else value

    early, counts = chunk_sizes(cols)
    spans = [(sum(counts[:at]), count) for at, count in enumerate(counts)]
    taken = take(master_t, 0, early[0])
    ahead = [turn(taken, TURN_MASKS[0])]
    acts = after(acts, [taken])

    projected = jnp.dot(acts, projection, preferred_element_type=jnp.float32).astype(jnp.bfloat16)
    tokens = [projected] + [send(projected, "fsdp", n_fsdp, k) for k in range(1, n_fsdp)]
    parts = pl.pallas_call(
        functools.partial(partial_kernel, n_fsdp=n_fsdp, n_dp=n_dp),
        out_shape=[jax.ShapeDtypeStruct((rows, cols), jnp.bfloat16)] * n_dp,
        in_specs=[VMEM] * (1 + n_fsdp),
        out_specs=[VMEM] * n_dp,
        scratch_shapes=[
            pltpu.VMEM((n_fsdp * projected.shape[0], rank), jnp.bfloat16),
            pltpu.VMEM((rank, n_fsdp * projected.shape[0]), jnp.bfloat16),
        ],
        compiler_params=pltpu.CompilerParams(vmem_limit_bytes=16 * 2**20),
    )(grad_out.T, *tokens)
    parts = lax.optimization_barrier((*parts, *ahead))[:n_dp]
    parts = [part if masks == (0, 0) else turn(part, masks) for part, masks in zip(parts, SWAP_MASKS)]
    moment_one_new, moment_two_new, update = pl.pallas_call(
        adam_kernel,
        out_shape=[
            jax.ShapeDtypeStruct(moment_one.shape, jnp.float32),
            jax.ShapeDtypeStruct(moment_two.shape, jnp.float32),
            jax.ShapeDtypeStruct((rows, wide), jnp.bfloat16),
        ],
        in_specs=[VMEM] * (2 + n_dp),
        out_specs=[VMEM] * 3,
        compiler_params=pltpu.CompilerParams(vmem_limit_bytes=16 * 2**20),
    )(moment_one, moment_two, *parts)

    updates = {0: update}
    for k in (6, 2, 4, 1):
        updates[k] = hop(update, k)
    for k in (2, 4, 6):
        updates[k ^ 1] = hop(updates[k], 1)
    updates = [updates[k] for k in range(n_dp)]

    tall, *own = weights(projection, master_t, updates, spans[1:3])
    *late, own_first, whole = weights(projection, master_t, [tall], spans[3:] + spans[:1] + [(0, cols)])
    own = [own_first] + own + late
    got = {(0, 0): ahead_weights(projection, tall, ahead)}
    over = {(0, 0): hop(got[(0, 0)], 1)}
    master_new = new_master(projection, master_t, tall, cols // 4)

    later = range(1, len(counts))
    steps = [(phase, at) for phase in range(3) for at in later] + [(1, 0), (2, 0)]
    outs = [None]
    shape = (cols, n_dp * slab_rows)

    def parts_of(at):
        pieces = [whole, whole_c]
        for which in range(3):
            pieces += [got[(which, at)], over[(which, at)]]
        return [(*spans[at], kind, piece) for kind, piece in enumerate(pieces)]

    for step, (phase, at) in enumerate(steps):
        value = got[(0, at)] if phase == 2 else own[at]
        earlier = [got[steps[step - 2]]] if step >= 2 else []
        earlier += [over[steps[step - 4]]] if step >= 4 else []
        if step == 2:
            earlier.append(master_new)
        got[(phase, at)] = turn(after(value, earlier), TURN_MASKS[min(phase, 1)])
        held = [outs[step - len(steps) + 3]] if step >= len(steps) - 2 else []
        over[(phase, at)] = hop(after(got[(phase, at)], held), 1)
        if step == 1:
            whole_c = hop(after(whole, [got[steps[1]]]), 1)
        if phase == 2 and at in (2, 4):
            outs.append(lay(outs[-1], shape, parts_of(at - 1) + parts_of(at)))
    parts = parts_of(0)
    outs.append(lay(outs[-1], shape, parts[:-1]))
    outs.append(lay(outs[-1], shape, parts[-1:]))
    return (moment_one_new, moment_two_new, master_new.T, outs[-1].T)


def solution(mesh):
    n_dp, n_fsdp = mesh.shape["dp"], mesh.shape["fsdp"]

    def body(acts, grad_out, projection, moment_one, moment_two, master):
        args = (acts, grad_out, projection, moment_one, moment_two, master)
        fits = n_dp == 8 and n_fsdp == 4 and moment_one.shape[0] % 32 == 0 and master.shape[0] % 128 == 0
        if fits and grad_out.shape[1] % 64 == 0 and acts.shape[0] % 128 == 0:
            return kernel_body(*args, n_dp, n_fsdp)
        return plain_body(*args)

    in_specs = (
        P(("dp", "fsdp"), None),
        P("dp", "fsdp"),
        P(),
        P("dp", "fsdp"),
        P("dp", "fsdp"),
        P("dp", "fsdp"),
    )
    out_specs = (P("dp", "fsdp"), P("dp", "fsdp"), P("dp", "fsdp"), P(None, "fsdp"))
    return jax.shard_map(body, mesh=mesh, in_specs=in_specs, out_specs=out_specs, check_vma=False)
```

```python
import functools

import jax
import jax.numpy as jnp
from jax import lax
from jax.experimental import pallas as pl
from jax.experimental.pallas import tpu as pltpu
from jax.sharding import PartitionSpec as P

STEP = 1000


BETA_ONE = 0.9
BETA_TWO = 0.999
ADAM_EPS = 1e-08
LEARN_RATE = 0.01
CORRECT_ONE = 1.0 - BETA_ONE**STEP
CORRECT_TWO = 1.0 - BETA_TWO**STEP

VMEM = pl.BlockSpec(memory_space=pltpu.VMEM)
ANY = pl.BlockSpec(memory_space=pl.ANY)


TURN_MASKS = ((2, 4), (4, 2))
UPDATE_MASKS = tuple((k, k) for k in range(8))
SWAP_MASKS = ((0, 0), (4, 2), (2, 4), (6, 6), (7, 7), (5, 3), (3, 5), (1, 1))
OWNER_MASKS = ((0, 0), (1, 1), (2, 4), (5, 3), (4, 2), (3, 5), (6, 6), (7, 7))


def chunk_sizes(cols):
    small = cols // 80 * 16
    part = -(-(cols - 2 * small) // 48) * 16
    return (small,), (small, part, part, cols - 2 * part - 2 * small, small)


def adam(grad, moment_one, moment_two):
    moment_one_new = BETA_ONE * moment_one + (1.0 - BETA_ONE) * grad
    moment_two_new = BETA_TWO * moment_two + (1.0 - BETA_TWO) * grad * grad
    update = (
        moment_one_new / CORRECT_ONE / (jnp.sqrt(moment_two_new / CORRECT_TWO) + ADAM_EPS)
    ).astype(jnp.bfloat16)
    return moment_one_new, moment_two_new, update


def plain_body(acts, grad_out, projection, moment_one, moment_two, master):
    projected = jnp.dot(acts, projection, preferred_element_type=jnp.float32).astype(jnp.bfloat16)
    group_proj = lax.all_gather(projected, "fsdp", axis=0, tiled=True)
    partial_value = jnp.einsum(
        "tr,tc->rc", group_proj, grad_out, preferred_element_type=jnp.float32
    )
    partial_value = lax.optimization_barrier(partial_value.astype(jnp.bfloat16))
    grad = lax.psum_scatter(
        partial_value.astype(jnp.float32), "dp", scatter_dimension=0, tiled=True
    )
    moment_one_new, moment_two_new, update = adam(grad, moment_one, moment_two)
    slab_rows = master.shape[0]
    proj_slab = lax.dynamic_slice_in_dim(projection, lax.axis_index("dp") * slab_rows, slab_rows, 0)
    piece = lax.all_gather(update, "dp", axis=0, tiled=True)
    expanded = jnp.dot(proj_slab, piece, preferred_element_type=jnp.float32)
    master_new = master - LEARN_RATE * expanded
    weight_cols = lax.all_gather(master_new.astype(jnp.bfloat16), "dp", axis=0, tiled=True)
    return (moment_one_new, moment_two_new, master_new, weight_cols)


def send(value, axis, size, mask):
    return lax.ppermute(value, axis, [(i, i ^ mask) for i in range(size)])


def other(me, masks):
    return me ^ jnp.where((me & 1) == 0, masks[0], masks[1])


def take_kernel(source, out, held, sems):
    count = held.shape[1]
    ways = []
    for at in range(held.shape[0]):
        rows = pl.ds(at * count, count)
        ways.append((
            pltpu.make_async_copy(source.at[rows, :], held.at[at], sems.at[0, at]),
            pltpu.make_async_copy(held.at[at], out.at[rows, :], sems.at[1, at]),
        ))
    for into, _ in ways:
        into.start()
    for into, back in ways:
        into.wait()
        back.start()
    for _, back in ways:
        back.wait()


def take(array, count):
    parts = count // 48 if count % 48 == 0 else 1
    return pl.pallas_call(
        take_kernel,
        out_shape=jax.ShapeDtypeStruct((count, array.shape[1]), array.dtype),
        in_specs=[ANY],
        out_specs=ANY,
        scratch_shapes=[
            pltpu.VMEM((parts, count // parts, array.shape[1]), array.dtype),
            pltpu.SemaphoreType.DMA((2, parts)),
        ],
        compiler_params=pltpu.CompilerParams(vmem_limit_bytes=60 * 2**20),
    )(array)


def partial_kernel(grad_t, *refs, n_fsdp, n_dp):
    pieces, outs, (tokens, across) = refs[:n_fsdp], refs[n_fsdp : n_fsdp + n_dp], refs[n_fsdp + n_dp :]
    count = pieces[0].shape[0]
    rows = outs[0].shape[0]
    me = lax.axis_index("fsdp")
    for k, piece in enumerate(pieces):
        tokens[pl.ds(pl.multiple_of((me ^ k) * count, count), count), :] = piece[...]
    across[...] = tokens[...].T
    me = lax.axis_index("dp")
    left = jnp.concatenate(
        [across[pl.ds(pl.multiple_of(other(me, masks) * rows, rows), rows), :] for masks in SWAP_MASKS], axis=0
    )
    result = lax.dot_general(
        left, grad_t[...], (((1,), (1,)), ((), ())), preferred_element_type=jnp.float32
    ).astype(jnp.bfloat16)
    for k, out in enumerate(outs):
        out[...] = result[k * rows : (k + 1) * rows, :]


def adam_kernel(moment_one, moment_two, *refs):
    parts, (one_new, two_new, update) = refs[:-3], refs[-3:]
    grad = parts[0][...].astype(jnp.float32)
    for part in parts[1:]:
        grad = grad + part[...].astype(jnp.float32)
    one, two, value = adam(grad, moment_one[...], moment_two[...])
    one_new[...] = one
    two_new[...] = two
    cols = value.shape[1]
    update[...] = jnp.zeros_like(update)
    update[:, :cols] = value


def expand(tall, slab, first, count):
    return lax.dot_general(
        tall[pl.ds(first, count), :], slab, (((1,), (1,)), ((), ())),
        preferred_element_type=jnp.float32,
    )


def weight_kernel(projection, master_t, *refs, n_in, spans, block):
    pieces, outs = refs[:n_in], refs[n_in:]
    me = lax.axis_index("dp")
    if n_in > 1:
        tall, wide = outs[0], outs[-1]
        outs = outs[1:-1]
        rows = pieces[0].shape[0]
        for k, piece in enumerate(pieces):
            wide[pl.ds(pl.multiple_of((me ^ k) * rows, rows), rows), :] = piece[...]
        tall[...] = wide[...].T
    else:
        tall = pieces[0]
    slab_rows = master_t.shape[1]
    slab = projection[pl.ds(pl.multiple_of(me * slab_rows, slab_rows), slab_rows), :]
    for (first, count), out in zip(spans, outs):
        for at in range(0, count, block):
            size = min(block, count - at)
            master_new = master_t[pl.ds(first + at, size), :] - LEARN_RATE * expand(
                tall, slab, first + at, size
            )
            out[pl.ds(at, size), :] = master_new.astype(jnp.bfloat16)


def weights(projection, master_t, pieces, spans):
    slab_rows, rank = master_t.shape[1], projection.shape[1]
    wide = pieces[0].shape[1]
    out_shape = [jax.ShapeDtypeStruct((count, slab_rows), jnp.bfloat16) for _, count in spans]
    scratch = []
    if len(pieces) > 1:
        out_shape = [jax.ShapeDtypeStruct((wide, rank), jnp.bfloat16)] + out_shape
        scratch = [pltpu.VMEM((rank, wide), jnp.bfloat16)]
    size = sum(count for _, count in spans) * slab_rows
    return pl.pallas_call(
        functools.partial(weight_kernel, n_in=len(pieces), spans=spans, block=144),
        out_shape=out_shape,
        in_specs=[VMEM] * (2 + len(pieces)),
        out_specs=[VMEM] * len(out_shape),
        scratch_shapes=scratch,
        compiler_params=pltpu.CompilerParams(vmem_limit_bytes=20 * 2**20),
        cost_estimate=pl.CostEstimate(flops=2 * size * rank, bytes_accessed=4 * size, transcendentals=0),
    )(projection, master_t, *pieces)


def ahead_kernel(projection, tall, *refs, block):
    parts, out = refs[:-1], refs[-1]
    slab_rows = out.shape[1]
    owner = other(lax.axis_index("dp"), TURN_MASKS[0])
    slab = projection[pl.ds(pl.multiple_of(owner * slab_rows, slab_rows), slab_rows), :]
    first = 0
    for part in parts:
        for at in range(0, part.shape[0], block):
            size = min(block, part.shape[0] - at)
            master_new = part[pl.ds(at, size), :] - LEARN_RATE * expand(tall, slab, first, size)
            out[pl.ds(first, size), :] = master_new.astype(jnp.bfloat16)
            first += size


def ahead_weights(projection, tall, parts):
    shape = (sum(part.shape[0] for part in parts), parts[0].shape[1])
    size = shape[0] * shape[1]
    return pl.pallas_call(
        functools.partial(ahead_kernel, block=144),
        out_shape=jax.ShapeDtypeStruct(shape, jnp.bfloat16),
        in_specs=[VMEM] * (2 + len(parts)),
        out_specs=VMEM,
        compiler_params=pltpu.CompilerParams(vmem_limit_bytes=20 * 2**20),
        cost_estimate=pl.CostEstimate(
            flops=2 * size * projection.shape[1], bytes_accessed=4 * size, transcendentals=0
        ),
    )(projection, tall, *parts)


def master_kernel(projection, master_t, tall, out):
    slab_rows = master_t.shape[1]
    first = pl.multiple_of(lax.axis_index("dp") * slab_rows, slab_rows)
    slab = projection[pl.ds(first, slab_rows), :]
    block = master_t.shape[0]
    first = pl.multiple_of(pl.program_id(0) * block, block)
    out[...] = master_t[...] - LEARN_RATE * expand(tall, slab, first, block)


def new_master(projection, master_t, tall, block):
    cols, slab_rows = master_t.shape
    rank = projection.shape[1]
    return pl.pallas_call(
        master_kernel,
        out_shape=jax.ShapeDtypeStruct((cols, slab_rows), jnp.float32),
        grid=(cols // block,),
        in_specs=[
            pl.BlockSpec(projection.shape, lambda i: (0, 0)),
            pl.BlockSpec((block, slab_rows), lambda i: (i, 0)),
            pl.BlockSpec(tall.shape, lambda i: (0, 0)),
        ],
        out_specs=pl.BlockSpec((block, slab_rows), lambda i: (i, 0)),
        compiler_params=pltpu.CompilerParams(vmem_limit_bytes=20 * 2**20),
        cost_estimate=pl.CostEstimate(
            flops=2 * cols * slab_rows * rank, bytes_accessed=8 * cols * slab_rows, transcendentals=0
        ),
    )(projection, master_t, tall)


def lay_kernel(*refs, places, fresh):
    refs = refs if fresh else refs[1:]
    pieces, out, sems = refs[:-2], refs[-2], refs[-1]
    me = lax.axis_index("dp")
    copies = []
    for at, (index, first, count, kind) in enumerate(places):
        piece = pieces[index]
        width = piece.shape[1]
        column = pl.multiple_of(other(me, OWNER_MASKS[kind]) * width, 128)
        part = piece if piece.shape[0] == count else piece.at[pl.ds(first, count), :]
        target = out.at[pl.ds(first, count), pl.ds(column, width)]
        copies.append(pltpu.make_async_copy(part, target, sems.at[at]))
    for copy in copies:
        copy.start()
    for copy in copies:
        copy.wait()


def lay(out, shape, parts):
    fresh = out is None
    held = [] if fresh else [out]
    pieces = []
    places = []
    for first, count, kind, piece in parts:
        known = [at for at, other_piece in enumerate(pieces) if other_piece is piece]
        if not known:
            pieces.append(piece)
        places.append((known[0] if known else len(pieces) - 1, first, count, kind))
    size = sum(count for _, _, count, _ in places) * pieces[0].shape[1]
    return pl.pallas_call(
        functools.partial(lay_kernel, places=tuple(places), fresh=fresh),
        out_shape=jax.ShapeDtypeStruct(shape, jnp.bfloat16),
        in_specs=[ANY] * len(held) + [VMEM] * len(pieces),
        out_specs=ANY,
        scratch_shapes=[pltpu.SemaphoreType.DMA((len(places),))],
        input_output_aliases={} if fresh else {0: 0},
        compiler_params=pltpu.CompilerParams(vmem_limit_bytes=20 * 2**20),
        cost_estimate=pl.CostEstimate(flops=0, bytes_accessed=4 * size, transcendentals=0),
    )(*held, *pieces)


def kernel_body(acts, grad_out, projection, moment_one, moment_two, master, n_dp, n_fsdp):
    cols = grad_out.shape[1]
    rank = projection.shape[1]
    rows = moment_one.shape[0]
    slab_rows = master.shape[0]
    wide = -(-cols // 128) * 128
    master_t = master.T

    def hop(value, mask):
        return send(value, "dp", n_dp, mask)

    def turn(value, masks):
        return lax.ppermute(value, "dp", [(i, i ^ masks[i & 1]) for i in range(n_dp)])

    def after(value, earlier):
        return lax.optimization_barrier((value, *earlier))[0] if earlier else value

    early, counts = chunk_sizes(cols)
    spans = [(sum(counts[:at]), count) for at, count in enumerate(counts)]
    taken = take(master_t, early[0])
    ahead = [turn(taken, TURN_MASKS[0])]
    acts = after(acts, [taken])

    projected = jnp.dot(acts, projection, preferred_element_type=jnp.float32).astype(jnp.bfloat16)
    tokens = [projected] + [send(projected, "fsdp", n_fsdp, k) for k in range(1, n_fsdp)]
    parts = pl.pallas_call(
        functools.partial(partial_kernel, n_fsdp=n_fsdp, n_dp=n_dp),
        out_shape=[jax.ShapeDtypeStruct((rows, cols), jnp.bfloat16)] * n_dp,
        in_specs=[VMEM] * (1 + n_fsdp),
        out_specs=[VMEM] * n_dp,
        scratch_shapes=[
            pltpu.VMEM((n_fsdp * projected.shape[0], rank), jnp.bfloat16),
            pltpu.VMEM((rank, n_fsdp * projected.shape[0]), jnp.bfloat16),
        ],
        compiler_params=pltpu.CompilerParams(vmem_limit_bytes=16 * 2**20),
    )(grad_out.T, *tokens)
    parts = lax.optimization_barrier((*parts, *ahead))[:n_dp]
    parts = [part if masks == (0, 0) else turn(part, masks) for part, masks in zip(parts, SWAP_MASKS)]
    moment_one_new, moment_two_new, update = pl.pallas_call(
        adam_kernel,
        out_shape=[
            jax.ShapeDtypeStruct(moment_one.shape, jnp.float32),
            jax.ShapeDtypeStruct(moment_two.shape, jnp.float32),
            jax.ShapeDtypeStruct((rows, wide), jnp.bfloat16),
        ],
        in_specs=[VMEM] * (2 + n_dp),
        out_specs=[VMEM] * 3,
        compiler_params=pltpu.CompilerParams(vmem_limit_bytes=16 * 2**20),
    )(moment_one, moment_two, *parts)

    updates = {0: update}
    for k in (6, 2, 4, 1):
        updates[k] = hop(update, k)
    for k in (2, 4, 6):
        updates[k ^ 1] = hop(updates[k], 1)
    updates = [updates[k] for k in range(n_dp)]

    tall, *own = weights(projection, master_t, updates, spans[1:3])
    *late, own_first, whole = weights(projection, master_t, [tall], spans[3:] + spans[:1] + [(0, cols)])
    own = [own_first] + own + late
    got = {(0, 0): ahead_weights(projection, tall, ahead)}
    over = {(0, 0): hop(got[(0, 0)], 1)}
    master_new = new_master(projection, master_t, tall, cols // 4)

    later = range(1, len(counts))
    steps = [(phase, at) for phase in range(3) for at in later] + [(1, 0), (2, 0)]
    outs = [None]
    shape = (cols, n_dp * slab_rows)

    def parts_of(at):
        pieces = [whole, whole_c]
        for which in range(3):
            pieces += [table[(which, at)] for table in (got, over) if (which, at) in table]
        return [(*spans[at], kind, piece) for kind, piece in enumerate(pieces)]

    for step, (phase, at) in enumerate(steps):
        value = got[(0, at)] if phase == 2 else own[at]
        earlier = [got[steps[step - 2]]] if step >= 2 else []
        earlier += [over[steps[step - 4]]] if step >= 4 else []
        if step == 2:
            earlier.append(master_new)
        got[(phase, at)] = turn(after(value, earlier), TURN_MASKS[min(phase, 1)])
        held = [outs[step - len(steps) + 3]] if step >= len(steps) - 2 else []
        over[(phase, at)] = hop(after(got[(phase, at)], held), 1)
        if step == 1:
            whole_c = hop(after(whole, [got[steps[1]]]), 1)
        if phase == 2 and at in (2, 4):
            outs.append(lay(outs[-1], shape, parts_of(at - 1) + parts_of(at) + parts_of(0)[at - 2 : at]))
    parts = parts_of(0)
    outs.append(lay(outs[-1], shape, parts[4:-1]))
    outs.append(lay(outs[-1], shape, parts[-1:]))
    return (moment_one_new, moment_two_new, master_new.T, outs[-1].T)


def solution(mesh):
    n_dp, n_fsdp = mesh.shape["dp"], mesh.shape["fsdp"]

    def body(acts, grad_out, projection, moment_one, moment_two, master):
        args = (acts, grad_out, projection, moment_one, moment_two, master)
        fits = n_dp == 8 and n_fsdp == 4 and moment_one.shape[0] % 32 == 0 and master.shape[0] % 128 == 0
        if fits and grad_out.shape[1] % 64 == 0 and acts.shape[0] % 128 == 0:
            return kernel_body(*args, n_dp, n_fsdp)
        return plain_body(*args)

    in_specs = (
        P(("dp", "fsdp"), None),
        P("dp", "fsdp"),
        P(),
        P("dp", "fsdp"),
        P("dp", "fsdp"),
        P("dp", "fsdp"),
    )
    out_specs = (P("dp", "fsdp"), P("dp", "fsdp"), P("dp", "fsdp"), P(None, "fsdp"))
    return jax.shard_map(body, mesh=mesh, in_specs=in_specs, out_specs=out_specs, check_vma=False)
```

```python
import functools

import jax
import jax.numpy as jnp
from jax import lax
from jax.experimental import pallas as pl
from jax.experimental.pallas import tpu as pltpu
from jax.sharding import PartitionSpec as P

STEP = 1000


BETA_ONE = 0.9
BETA_TWO = 0.999
ADAM_EPS = 1e-08
LEARN_RATE = 0.01
CORRECT_ONE = 1.0 - BETA_ONE**STEP
CORRECT_TWO = 1.0 - BETA_TWO**STEP

VMEM = pl.BlockSpec(memory_space=pltpu.VMEM)
ANY = pl.BlockSpec(memory_space=pl.ANY)


TURN_MASKS = ((2, 4), (4, 2))
UPDATE_MASKS = tuple((k, k) for k in range(8))
SWAP_MASKS = ((0, 0), (6, 6), (7, 7), (4, 2), (2, 4), (5, 3), (3, 5), (1, 1))
OWNER_MASKS = ((0, 0), (1, 1), (2, 4), (5, 3), (4, 2), (3, 5), (6, 6), (7, 7))


def chunk_sizes(cols):
    small = cols // 80 * 16
    part = -(-(cols - 2 * small) // 48) * 16
    return (small,), (small, part, part, cols - 2 * part - 2 * small, small)


def adam(grad, moment_one, moment_two):
    moment_one_new = BETA_ONE * moment_one + (1.0 - BETA_ONE) * grad
    moment_two_new = BETA_TWO * moment_two + (1.0 - BETA_TWO) * grad * grad
    update = (
        moment_one_new / CORRECT_ONE / (jnp.sqrt(moment_two_new / CORRECT_TWO) + ADAM_EPS)
    ).astype(jnp.bfloat16)
    return moment_one_new, moment_two_new, update


def plain_body(acts, grad_out, projection, moment_one, moment_two, master):
    projected = jnp.dot(acts, projection, preferred_element_type=jnp.float32).astype(jnp.bfloat16)
    group_proj = lax.all_gather(projected, "fsdp", axis=0, tiled=True)
    partial_value = jnp.einsum(
        "tr,tc->rc", group_proj, grad_out, preferred_element_type=jnp.float32
    )
    partial_value = lax.optimization_barrier(partial_value.astype(jnp.bfloat16))
    grad = lax.psum_scatter(
        partial_value.astype(jnp.float32), "dp", scatter_dimension=0, tiled=True
    )
    moment_one_new, moment_two_new, update = adam(grad, moment_one, moment_two)
    slab_rows = master.shape[0]
    proj_slab = lax.dynamic_slice_in_dim(projection, lax.axis_index("dp") * slab_rows, slab_rows, 0)
    piece = lax.all_gather(update, "dp", axis=0, tiled=True)
    expanded = jnp.dot(proj_slab, piece, preferred_element_type=jnp.float32)
    master_new = master - LEARN_RATE * expanded
    weight_cols = lax.all_gather(master_new.astype(jnp.bfloat16), "dp", axis=0, tiled=True)
    return (moment_one_new, moment_two_new, master_new, weight_cols)


def send(value, axis, size, mask):
    return lax.ppermute(value, axis, [(i, i ^ mask) for i in range(size)])


def other(me, masks):
    return me ^ jnp.where((me & 1) == 0, masks[0], masks[1])


def take_kernel(source, out, held, sems):
    count = held.shape[1]
    ways = []
    for at in range(held.shape[0]):
        rows = pl.ds(at * count, count)
        ways.append((
            pltpu.make_async_copy(source.at[rows, :], held.at[at], sems.at[0, at]),
            pltpu.make_async_copy(held.at[at], out.at[rows, :], sems.at[1, at]),
        ))
    for into, _ in ways:
        into.start()
    for into, back in ways:
        into.wait()
        back.start()
    for _, back in ways:
        back.wait()


def take(array, count):
    parts = count // 48 if count % 48 == 0 else 1
    return pl.pallas_call(
        take_kernel,
        out_shape=jax.ShapeDtypeStruct((count, array.shape[1]), array.dtype),
        in_specs=[ANY],
        out_specs=ANY,
        scratch_shapes=[
            pltpu.VMEM((parts, count // parts, array.shape[1]), array.dtype),
            pltpu.SemaphoreType.DMA((2, parts)),
        ],
        compiler_params=pltpu.CompilerParams(vmem_limit_bytes=60 * 2**20),
    )(array)


def partial_kernel(grad_t, *refs, n_fsdp, n_dp):
    pieces, outs, (tokens, across) = refs[:n_fsdp], refs[n_fsdp : n_fsdp + n_dp], refs[n_fsdp + n_dp :]
    count = pieces[0].shape[0]
    rows = outs[0].shape[0]
    me = lax.axis_index("fsdp")
    for k, piece in enumerate(pieces):
        tokens[pl.ds(pl.multiple_of((me ^ k) * count, count), count), :] = piece[...]
    across[...] = tokens[...].T
    me = lax.axis_index("dp")
    left = jnp.concatenate(
        [across[pl.ds(pl.multiple_of(other(me, masks) * rows, rows), rows), :] for masks in SWAP_MASKS], axis=0
    )
    result = lax.dot_general(
        left, grad_t[...], (((1,), (1,)), ((), ())), preferred_element_type=jnp.float32
    ).astype(jnp.bfloat16)
    for k, out in enumerate(outs):
        out[...] = result[k * rows : (k + 1) * rows, :]


def adam_kernel(moment_one, moment_two, *refs, outs):
    parts, outs = refs[:-outs], refs[-outs:]
    grad = parts[0][...].astype(jnp.float32)
    for part in parts[1:]:
        grad = grad + part[...].astype(jnp.float32)
    one, two, value = adam(grad, moment_one[...], moment_two[...])
    if len(outs) == 2:
        outs[0][...] = one
        outs[1][...] = two
    else:
        outs[0][:, outs[0].shape[1] - 128 :] = jnp.zeros((value.shape[0], 128), value.dtype)
        outs[0][:, : value.shape[1]] = value


def adam_call(moment_one, moment_two, parts, out_shape):
    return pl.pallas_call(
        functools.partial(adam_kernel, outs=len(out_shape)),
        out_shape=out_shape,
        in_specs=[VMEM] * (2 + len(parts)),
        out_specs=[VMEM] * len(out_shape),
        compiler_params=pltpu.CompilerParams(vmem_limit_bytes=16 * 2**20),
    )(moment_one, moment_two, *parts)


def expand(tall, slab, first, count):
    return lax.dot_general(
        tall[pl.ds(first, count), :], slab, (((1,), (1,)), ((), ())),
        preferred_element_type=jnp.float32,
    )


def weight_kernel(projection, master_t, *refs, n_in, spans, block):
    pieces, outs = refs[:n_in], refs[n_in:]
    me = lax.axis_index("dp")
    if n_in > 1:
        tall, wide = outs[0], outs[-1]
        outs = outs[1:-1]
        rows = pieces[0].shape[0]
        for k, piece in enumerate(pieces):
            wide[pl.ds(pl.multiple_of((me ^ k) * rows, rows), rows), :] = piece[...]
        tall[...] = wide[...].T
    else:
        tall = pieces[0]
    slab_rows = master_t.shape[1]
    slab = projection[pl.ds(pl.multiple_of(me * slab_rows, slab_rows), slab_rows), :]
    for (first, count), out in zip(spans, outs):
        for at in range(0, count, block):
            size = min(block, count - at)
            master_new = master_t[pl.ds(first + at, size), :] - LEARN_RATE * expand(
                tall, slab, first + at, size
            )
            out[pl.ds(at, size), :] = master_new.astype(jnp.bfloat16)


def weights(projection, master_t, pieces, spans):
    slab_rows, rank = master_t.shape[1], projection.shape[1]
    wide = pieces[0].shape[1]
    out_shape = [jax.ShapeDtypeStruct((count, slab_rows), jnp.bfloat16) for _, count in spans]
    scratch = []
    if len(pieces) > 1:
        out_shape = [jax.ShapeDtypeStruct((wide, rank), jnp.bfloat16)] + out_shape
        scratch = [pltpu.VMEM((rank, wide), jnp.bfloat16)]
    size = sum(count for _, count in spans) * slab_rows
    return pl.pallas_call(
        functools.partial(weight_kernel, n_in=len(pieces), spans=spans, block=144),
        out_shape=out_shape,
        in_specs=[VMEM] * (2 + len(pieces)),
        out_specs=[VMEM] * len(out_shape),
        scratch_shapes=scratch,
        compiler_params=pltpu.CompilerParams(vmem_limit_bytes=20 * 2**20),
        cost_estimate=pl.CostEstimate(flops=2 * size * rank, bytes_accessed=4 * size, transcendentals=0),
    )(projection, master_t, *pieces)


def ahead_kernel(projection, tall, *refs, block):
    parts, out = refs[:-1], refs[-1]
    slab_rows = out.shape[1]
    owner = other(lax.axis_index("dp"), TURN_MASKS[0])
    slab = projection[pl.ds(pl.multiple_of(owner * slab_rows, slab_rows), slab_rows), :]
    first = 0
    for part in parts:
        for at in range(0, part.shape[0], block):
            size = min(block, part.shape[0] - at)
            master_new = part[pl.ds(at, size), :] - LEARN_RATE * expand(tall, slab, first, size)
            out[pl.ds(first, size), :] = master_new.astype(jnp.bfloat16)
            first += size


def ahead_weights(projection, tall, parts):
    shape = (sum(part.shape[0] for part in parts), parts[0].shape[1])
    size = shape[0] * shape[1]
    return pl.pallas_call(
        functools.partial(ahead_kernel, block=144),
        out_shape=jax.ShapeDtypeStruct(shape, jnp.bfloat16),
        in_specs=[VMEM] * (2 + len(parts)),
        out_specs=VMEM,
        compiler_params=pltpu.CompilerParams(vmem_limit_bytes=20 * 2**20),
        cost_estimate=pl.CostEstimate(
            flops=2 * size * projection.shape[1], bytes_accessed=4 * size, transcendentals=0
        ),
    )(projection, tall, *parts)


def master_kernel(projection, master_t, tall, out):
    slab_rows = master_t.shape[1]
    first = pl.multiple_of(lax.axis_index("dp") * slab_rows, slab_rows)
    slab = projection[pl.ds(first, slab_rows), :]
    block = master_t.shape[0]
    first = pl.multiple_of(pl.program_id(0) * block, block)
    out[...] = master_t[...] - LEARN_RATE * expand(tall, slab, first, block)


def new_master(projection, master_t, tall, block):
    cols, slab_rows = master_t.shape
    rank = projection.shape[1]
    return pl.pallas_call(
        master_kernel,
        out_shape=jax.ShapeDtypeStruct((cols, slab_rows), jnp.float32),
        grid=(cols // block,),
        in_specs=[
            pl.BlockSpec(projection.shape, lambda i: (0, 0)),
            pl.BlockSpec((block, slab_rows), lambda i: (i, 0)),
            pl.BlockSpec(tall.shape, lambda i: (0, 0)),
        ],
        out_specs=pl.BlockSpec((block, slab_rows), lambda i: (i, 0)),
        compiler_params=pltpu.CompilerParams(vmem_limit_bytes=20 * 2**20),
        cost_estimate=pl.CostEstimate(
            flops=2 * cols * slab_rows * rank, bytes_accessed=8 * cols * slab_rows, transcendentals=0
        ),
    )(projection, master_t, tall)


def lay_kernel(*refs, places, fresh):
    refs = refs if fresh else refs[1:]
    pieces, out, sems = refs[:-2], refs[-2], refs[-1]
    me = lax.axis_index("dp")
    copies = []
    for at, (index, first, count, kind) in enumerate(places):
        piece = pieces[index]
        width = piece.shape[1]
        column = pl.multiple_of(other(me, OWNER_MASKS[kind]) * width, 128)
        part = piece if piece.shape[0] == count else piece.at[pl.ds(first, count), :]
        target = out.at[pl.ds(first, count), pl.ds(column, width)]
        copies.append(pltpu.make_async_copy(part, target, sems.at[at]))
    for copy in copies:
        copy.start()
    for copy in copies:
        copy.wait()


def lay(out, shape, parts):
    fresh = out is None
    held = [] if fresh else [out]
    pieces = []
    places = []
    for first, count, kind, piece in parts:
        known = [at for at, other_piece in enumerate(pieces) if other_piece is piece]
        if not known:
            pieces.append(piece)
        places.append((known[0] if known else len(pieces) - 1, first, count, kind))
    size = sum(count for _, _, count, _ in places) * pieces[0].shape[1]
    return pl.pallas_call(
        functools.partial(lay_kernel, places=tuple(places), fresh=fresh),
        out_shape=jax.ShapeDtypeStruct(shape, jnp.bfloat16),
        in_specs=[ANY] * len(held) + [VMEM] * len(pieces),
        out_specs=ANY,
        scratch_shapes=[pltpu.SemaphoreType.DMA((len(places),))],
        input_output_aliases={} if fresh else {0: 0},
        compiler_params=pltpu.CompilerParams(vmem_limit_bytes=20 * 2**20),
        cost_estimate=pl.CostEstimate(flops=0, bytes_accessed=4 * size, transcendentals=0),
    )(*held, *pieces)


def kernel_body(acts, grad_out, projection, moment_one, moment_two, master, n_dp, n_fsdp):
    cols = grad_out.shape[1]
    rank = projection.shape[1]
    rows = moment_one.shape[0]
    slab_rows = master.shape[0]
    wide = -(-cols // 128) * 128
    master_t = master.T

    def hop(value, mask):
        return send(value, "dp", n_dp, mask)

    def turn(value, masks):
        return lax.ppermute(value, "dp", [(i, i ^ masks[i & 1]) for i in range(n_dp)])

    def after(value, earlier):
        return lax.optimization_barrier((value, *earlier))[0] if earlier else value

    early, counts = chunk_sizes(cols)
    spans = [(sum(counts[:at]), count) for at, count in enumerate(counts)]
    taken = take(master_t, early[0])
    ahead = [turn(taken, TURN_MASKS[0])]
    acts = after(acts, [taken])

    projected = jnp.dot(acts, projection, preferred_element_type=jnp.float32).astype(jnp.bfloat16)
    tokens = [projected] + [send(projected, "fsdp", n_fsdp, k) for k in range(1, n_fsdp)]
    parts = pl.pallas_call(
        functools.partial(partial_kernel, n_fsdp=n_fsdp, n_dp=n_dp),
        out_shape=[jax.ShapeDtypeStruct((rows, cols), jnp.bfloat16)] * n_dp,
        in_specs=[VMEM] * (1 + n_fsdp),
        out_specs=[VMEM] * n_dp,
        scratch_shapes=[
            pltpu.VMEM((n_fsdp * projected.shape[0], rank), jnp.bfloat16),
            pltpu.VMEM((rank, n_fsdp * projected.shape[0]), jnp.bfloat16),
        ],
        compiler_params=pltpu.CompilerParams(vmem_limit_bytes=16 * 2**20),
    )(grad_out.T, *tokens)
    parts = lax.optimization_barrier((*parts, *ahead))[:n_dp]
    parts = [part if masks == (0, 0) else turn(part, masks) for part, masks in zip(parts, SWAP_MASKS)]
    (update,) = adam_call(
        moment_one, moment_two, parts, [jax.ShapeDtypeStruct((rows, wide), jnp.bfloat16)]
    )
    updates = {0: update}
    for k in (6, 2, 4, 1):
        updates[k] = hop(update, k)
    for k in (2, 4, 6):
        updates[k ^ 1] = hop(updates[k], 1)
    updates = [updates[k] for k in range(n_dp)]

    tall, *own = weights(projection, master_t, updates, spans[1:3])
    *late, own_first, whole = weights(projection, master_t, [tall], spans[3:] + spans[:1] + [(0, cols)])
    own = [own_first] + own + late
    got = {(0, 0): ahead_weights(projection, tall, ahead)}
    over = {(0, 0): hop(got[(0, 0)], 1)}
    master_new = new_master(projection, master_t, tall, cols // 4)
    moment_one_new, moment_two_new = adam_call(
        moment_one, moment_two, [after(parts[0], [tall])] + parts[1:],
        [jax.ShapeDtypeStruct(moment_one.shape, jnp.float32)] * 2,
    )

    later = range(1, len(counts))
    steps = [(phase, at) for phase in range(3) for at in later] + [(1, 0), (2, 0)]
    outs = [None]
    shape = (cols, n_dp * slab_rows)

    def parts_of(at):
        pieces = [whole, whole_c]
        for which in range(3):
            pieces += [table[(which, at)] for table in (got, over) if (which, at) in table]
        return [(*spans[at], kind, piece) for kind, piece in enumerate(pieces)]

    for step, (phase, at) in enumerate(steps):
        value = got[(0, at)] if phase == 2 else own[at]
        earlier = [got[steps[step - 2]]] if step >= 2 else []
        earlier += [over[steps[step - 4]]] if step >= 4 else []
        if step == 2:
            earlier += [master_new, moment_one_new]
        got[(phase, at)] = turn(after(value, earlier), TURN_MASKS[min(phase, 1)])
        held = [outs[step - len(steps) + 3]] if step >= len(steps) - 2 else []
        over[(phase, at)] = hop(after(got[(phase, at)], held), 1)
        if step == 1:
            whole_c = hop(after(whole, [got[steps[1]]]), 1)
        if phase == 2 and at in (2, 4):
            outs.append(lay(outs[-1], shape, parts_of(at - 1) + parts_of(at) + parts_of(0)[at - 2 : at]))
    parts = parts_of(0)
    outs.append(lay(outs[-1], shape, parts[4:-1]))
    outs.append(lay(outs[-1], shape, parts[-1:]))
    return (moment_one_new, moment_two_new, master_new.T, outs[-1].T)


def solution(mesh):
    n_dp, n_fsdp = mesh.shape["dp"], mesh.shape["fsdp"]

    def body(acts, grad_out, projection, moment_one, moment_two, master):
        args = (acts, grad_out, projection, moment_one, moment_two, master)
        fits = n_dp == 8 and n_fsdp == 4 and moment_one.shape[0] % 32 == 0 and master.shape[0] % 128 == 0
        if fits and grad_out.shape[1] % 64 == 0 and acts.shape[0] % 128 == 0:
            return kernel_body(*args, n_dp, n_fsdp)
        return plain_body(*args)

    in_specs = (
        P(("dp", "fsdp"), None),
        P("dp", "fsdp"),
        P(),
        P("dp", "fsdp"),
        P("dp", "fsdp"),
        P("dp", "fsdp"),
    )
    out_specs = (P("dp", "fsdp"), P("dp", "fsdp"), P("dp", "fsdp"), P(None, "fsdp"))
    return jax.shard_map(body, mesh=mesh, in_specs=in_specs, out_specs=out_specs, check_vma=False)
```

```python
import functools

import jax
import jax.numpy as jnp
from jax import lax
from jax.experimental import pallas as pl
from jax.experimental.pallas import tpu as pltpu
from jax.sharding import PartitionSpec as P

STEP = 1000


BETA_ONE = 0.9
BETA_TWO = 0.999
ADAM_EPS = 1e-08
LEARN_RATE = 0.01
CORRECT_ONE = 1.0 - BETA_ONE**STEP
CORRECT_TWO = 1.0 - BETA_TWO**STEP

VMEM = pl.BlockSpec(memory_space=pltpu.VMEM)
ANY = pl.BlockSpec(memory_space=pl.ANY)


TURN_MASKS = ((2, 4), (4, 2))
UPDATE_MASKS = tuple((k, k) for k in range(8))
SWAP_MASKS = ((0, 0), (4, 2), (2, 4), (6, 6), (7, 7), (5, 3), (3, 5), (1, 1))
OWNER_MASKS = ((0, 0), (1, 1), (2, 4), (5, 3), (4, 2), (3, 5), (6, 6), (7, 7))


def chunk_sizes(cols):
    small = cols // 80 * 16
    part = -(-(cols - 2 * small) // 48) * 16
    return (small, part, part, cols - 2 * part - 2 * small, small)


def adam(grad, moment_one, moment_two):
    moment_one_new = BETA_ONE * moment_one + (1.0 - BETA_ONE) * grad
    moment_two_new = BETA_TWO * moment_two + (1.0 - BETA_TWO) * grad * grad
    update = (
        moment_one_new / CORRECT_ONE / (jnp.sqrt(moment_two_new / CORRECT_TWO) + ADAM_EPS)
    ).astype(jnp.bfloat16)
    return moment_one_new, moment_two_new, update


def plain_body(acts, grad_out, projection, moment_one, moment_two, master):
    projected = jnp.dot(acts, projection, preferred_element_type=jnp.float32).astype(jnp.bfloat16)
    group_proj = lax.all_gather(projected, "fsdp", axis=0, tiled=True)
    partial_value = jnp.einsum(
        "tr,tc->rc", group_proj, grad_out, preferred_element_type=jnp.float32
    )
    partial_value = lax.optimization_barrier(partial_value.astype(jnp.bfloat16))
    grad = lax.psum_scatter(
        partial_value.astype(jnp.float32), "dp", scatter_dimension=0, tiled=True
    )
    moment_one_new, moment_two_new, update = adam(grad, moment_one, moment_two)
    slab_rows = master.shape[0]
    proj_slab = lax.dynamic_slice_in_dim(projection, lax.axis_index("dp") * slab_rows, slab_rows, 0)
    piece = lax.all_gather(update, "dp", axis=0, tiled=True)
    expanded = jnp.dot(proj_slab, piece, preferred_element_type=jnp.float32)
    master_new = master - LEARN_RATE * expanded
    weight_cols = lax.all_gather(master_new.astype(jnp.bfloat16), "dp", axis=0, tiled=True)
    return (moment_one_new, moment_two_new, master_new, weight_cols)


def send(value, axis, size, mask):
    return lax.ppermute(value, axis, [(i, i ^ mask) for i in range(size)])


def other(me, masks):
    return me ^ jnp.where((me & 1) == 0, masks[0], masks[1])


def take_kernel(source, out, held, sems):
    count = held.shape[1]
    ways = []
    for at in range(held.shape[0]):
        rows = pl.ds(at * count, count)
        ways.append((
            pltpu.make_async_copy(source.at[rows, :], held.at[at], sems.at[0, at]),
            pltpu.make_async_copy(held.at[at], out.at[rows, :], sems.at[1, at]),
        ))
    for into, _ in ways:
        into.start()
    for into, back in ways:
        into.wait()
        back.start()
    for _, back in ways:
        back.wait()


def take(array, count):
    parts = count // 48 if count % 48 == 0 else 1
    return pl.pallas_call(
        take_kernel,
        out_shape=jax.ShapeDtypeStruct((count, array.shape[1]), array.dtype),
        in_specs=[ANY],
        out_specs=ANY,
        scratch_shapes=[
            pltpu.VMEM((parts, count // parts, array.shape[1]), array.dtype),
            pltpu.SemaphoreType.DMA((2, parts)),
        ],
        compiler_params=pltpu.CompilerParams(vmem_limit_bytes=60 * 2**20),
    )(array)


def partial_kernel(grad_t, *refs, n_fsdp, n_dp):
    pieces, outs, (tokens, across) = refs[:n_fsdp], refs[n_fsdp : n_fsdp + n_dp], refs[n_fsdp + n_dp :]
    count = pieces[0].shape[0]
    rows = outs[0].shape[0]
    me = lax.axis_index("fsdp")
    for k, piece in enumerate(pieces):
        tokens[pl.ds(pl.multiple_of((me ^ k) * count, count), count), :] = piece[...]
    across[...] = tokens[...].T
    me = lax.axis_index("dp")
    left = jnp.concatenate(
        [across[pl.ds(pl.multiple_of(other(me, masks) * rows, rows), rows), :] for masks in SWAP_MASKS], axis=0
    )
    result = lax.dot_general(
        left, grad_t[...], (((1,), (1,)), ((), ())), preferred_element_type=jnp.float32
    ).astype(jnp.bfloat16)
    for k, out in enumerate(outs):
        out[...] = result[k * rows : (k + 1) * rows, :]


def adam_kernel(moment_one, moment_two, *refs, outs):
    parts, outs = refs[:-outs], refs[-outs:]
    grad = parts[0][...].astype(jnp.float32)
    for part in parts[1:]:
        grad = grad + part[...].astype(jnp.float32)
    one, two, value = adam(grad, moment_one[...], moment_two[...])
    if len(outs) == 2:
        outs[0][...] = one
        outs[1][...] = two
    else:
        outs[0][:, outs[0].shape[1] - 128 :] = jnp.zeros((value.shape[0], 128), value.dtype)
        outs[0][:, : value.shape[1]] = value


def adam_call(moment_one, moment_two, parts, out_shape):
    return pl.pallas_call(
        functools.partial(adam_kernel, outs=len(out_shape)),
        out_shape=out_shape,
        in_specs=[VMEM] * (2 + len(parts)),
        out_specs=[VMEM] * len(out_shape),
        compiler_params=pltpu.CompilerParams(vmem_limit_bytes=16 * 2**20),
    )(moment_one, moment_two, *parts)


def expand(tall, slab, first, count):
    return lax.dot_general(
        tall[pl.ds(first, count), :], slab, (((1,), (1,)), ((), ())),
        preferred_element_type=jnp.float32,
    )


def weight_kernel(projection, master_t, *refs, n_in, spans, block):
    pieces, outs = refs[:n_in], refs[n_in:]
    me = lax.axis_index("dp")
    if n_in > 1:
        tall, wide = outs[0], outs[-1]
        outs = outs[1:-1]
        rows = pieces[0].shape[0]
        for k, piece in enumerate(pieces):
            wide[pl.ds(pl.multiple_of((me ^ k) * rows, rows), rows), :] = piece[...]
        tall[...] = wide[...].T
    else:
        tall = pieces[0]
    slab_rows = master_t.shape[1]
    slab = projection[pl.ds(pl.multiple_of(me * slab_rows, slab_rows), slab_rows), :]
    for (first, count), out in zip(spans, outs):
        for at in range(0, count, block):
            size = min(block, count - at)
            master_new = master_t[pl.ds(first + at, size), :] - LEARN_RATE * expand(
                tall, slab, first + at, size
            )
            out[pl.ds(at, size), :] = master_new.astype(jnp.bfloat16)


def weights(projection, master_t, pieces, spans):
    slab_rows, rank = master_t.shape[1], projection.shape[1]
    wide = pieces[0].shape[1]
    out_shape = [jax.ShapeDtypeStruct((count, slab_rows), jnp.bfloat16) for _, count in spans]
    scratch = []
    if len(pieces) > 1:
        out_shape = [jax.ShapeDtypeStruct((wide, rank), jnp.bfloat16)] + out_shape
        scratch = [pltpu.VMEM((rank, wide), jnp.bfloat16)]
    size = sum(count for _, count in spans) * slab_rows
    return pl.pallas_call(
        functools.partial(weight_kernel, n_in=len(pieces), spans=spans, block=144),
        out_shape=out_shape,
        in_specs=[VMEM] * (2 + len(pieces)),
        out_specs=[VMEM] * len(out_shape),
        scratch_shapes=scratch,
        compiler_params=pltpu.CompilerParams(vmem_limit_bytes=20 * 2**20),
        cost_estimate=pl.CostEstimate(flops=2 * size * rank, bytes_accessed=4 * size, transcendentals=0),
    )(projection, master_t, *pieces)


def ahead_kernel(projection, tall, *refs, block):
    parts, out = refs[:-1], refs[-1]
    slab_rows = out.shape[1]
    owner = other(lax.axis_index("dp"), TURN_MASKS[0])
    slab = projection[pl.ds(pl.multiple_of(owner * slab_rows, slab_rows), slab_rows), :]
    first = 0
    for part in parts:
        for at in range(0, part.shape[0], block):
            size = min(block, part.shape[0] - at)
            master_new = part[pl.ds(at, size), :] - LEARN_RATE * expand(tall, slab, first, size)
            out[pl.ds(first, size), :] = master_new.astype(jnp.bfloat16)
            first += size


def ahead_weights(projection, tall, parts):
    shape = (sum(part.shape[0] for part in parts), parts[0].shape[1])
    size = shape[0] * shape[1]
    return pl.pallas_call(
        functools.partial(ahead_kernel, block=144),
        out_shape=jax.ShapeDtypeStruct(shape, jnp.bfloat16),
        in_specs=[VMEM] * (2 + len(parts)),
        out_specs=VMEM,
        compiler_params=pltpu.CompilerParams(vmem_limit_bytes=20 * 2**20),
        cost_estimate=pl.CostEstimate(
            flops=2 * size * projection.shape[1], bytes_accessed=4 * size, transcendentals=0
        ),
    )(projection, tall, *parts)


def master_kernel(projection, master_t, tall, out):
    slab_rows = master_t.shape[1]
    first = pl.multiple_of(lax.axis_index("dp") * slab_rows, slab_rows)
    slab = projection[pl.ds(first, slab_rows), :]
    block = master_t.shape[0]
    first = pl.multiple_of(pl.program_id(0) * block, block)
    out[...] = master_t[...] - LEARN_RATE * expand(tall, slab, first, block)


def new_master(projection, master_t, tall, block):
    cols, slab_rows = master_t.shape
    rank = projection.shape[1]
    return pl.pallas_call(
        master_kernel,
        out_shape=jax.ShapeDtypeStruct((cols, slab_rows), jnp.float32),
        grid=(cols // block,),
        in_specs=[
            pl.BlockSpec(projection.shape, lambda i: (0, 0)),
            pl.BlockSpec((block, slab_rows), lambda i: (i, 0)),
            pl.BlockSpec(tall.shape, lambda i: (0, 0)),
        ],
        out_specs=pl.BlockSpec((block, slab_rows), lambda i: (i, 0)),
        compiler_params=pltpu.CompilerParams(vmem_limit_bytes=20 * 2**20),
        cost_estimate=pl.CostEstimate(
            flops=2 * cols * slab_rows * rank, bytes_accessed=8 * cols * slab_rows, transcendentals=0
        ),
    )(projection, master_t, tall)


def lay_kernel(*refs, places, fresh):
    refs = refs if fresh else refs[1:]
    pieces, out, sems = refs[:-2], refs[-2], refs[-1]
    me = lax.axis_index("dp")
    copies = []
    for at, (index, first, count, kind) in enumerate(places):
        piece = pieces[index]
        width = piece.shape[1]
        column = pl.multiple_of(other(me, OWNER_MASKS[kind]) * width, 128)
        part = piece if piece.shape[0] == count else piece.at[pl.ds(first, count), :]
        target = out.at[pl.ds(first, count), pl.ds(column, width)]
        copies.append(pltpu.make_async_copy(part, target, sems.at[at]))
    for copy in copies:
        copy.start()
    for copy in copies:
        copy.wait()


def lay(out, shape, parts):
    fresh = out is None
    held = [] if fresh else [out]
    pieces = []
    places = []
    for first, count, kind, piece in parts:
        known = [at for at, other_piece in enumerate(pieces) if other_piece is piece]
        if not known:
            pieces.append(piece)
        places.append((known[0] if known else len(pieces) - 1, first, count, kind))
    size = sum(count for _, _, count, _ in places) * pieces[0].shape[1]
    return pl.pallas_call(
        functools.partial(lay_kernel, places=tuple(places), fresh=fresh),
        out_shape=jax.ShapeDtypeStruct(shape, jnp.bfloat16),
        in_specs=[ANY] * len(held) + [VMEM] * len(pieces),
        out_specs=ANY,
        scratch_shapes=[pltpu.SemaphoreType.DMA((len(places),))],
        input_output_aliases={} if fresh else {0: 0},
        compiler_params=pltpu.CompilerParams(vmem_limit_bytes=20 * 2**20),
        cost_estimate=pl.CostEstimate(flops=0, bytes_accessed=4 * size, transcendentals=0),
    )(*held, *pieces)


def kernel_body(acts, grad_out, projection, moment_one, moment_two, master, n_dp, n_fsdp):
    cols = grad_out.shape[1]
    rank = projection.shape[1]
    rows = moment_one.shape[0]
    slab_rows = master.shape[0]
    wide = -(-cols // 128) * 128
    master_t = master.T

    def hop(value, mask):
        return send(value, "dp", n_dp, mask)

    def turn(value, masks):
        return lax.ppermute(value, "dp", [(i, i ^ masks[i & 1]) for i in range(n_dp)])

    def after(value, earlier):
        return lax.optimization_barrier((value, *earlier))[0] if earlier else value

    counts = chunk_sizes(cols)
    spans = [(sum(counts[:at]), count) for at, count in enumerate(counts)]
    taken = take(master_t, counts[0])
    ahead = turn(taken, TURN_MASKS[0])
    acts = after(acts, [taken])

    projected = jnp.dot(acts, projection, preferred_element_type=jnp.float32).astype(jnp.bfloat16)
    tokens = [projected] + [send(projected, "fsdp", n_fsdp, k) for k in range(1, n_fsdp)]
    parts = pl.pallas_call(
        functools.partial(partial_kernel, n_fsdp=n_fsdp, n_dp=n_dp),
        out_shape=[jax.ShapeDtypeStruct((rows, cols), jnp.bfloat16)] * n_dp,
        in_specs=[VMEM] * (1 + n_fsdp),
        out_specs=[VMEM] * n_dp,
        scratch_shapes=[
            pltpu.VMEM((n_fsdp * projected.shape[0], rank), jnp.bfloat16),
            pltpu.VMEM((rank, n_fsdp * projected.shape[0]), jnp.bfloat16),
        ],
        compiler_params=pltpu.CompilerParams(vmem_limit_bytes=16 * 2**20),
    )(grad_out.T, *tokens)
    parts = lax.optimization_barrier((*parts, ahead))[:n_dp]
    parts = [part if masks == (0, 0) else turn(part, masks) for part, masks in zip(parts, SWAP_MASKS)]
    (update,) = adam_call(
        moment_one, moment_two, parts, [jax.ShapeDtypeStruct((rows, wide), jnp.bfloat16)]
    )
    updates = {0: update}
    for k in (6, 2, 4, 1):
        updates[k] = hop(update, k)
    for k in (2, 4, 6):
        updates[k ^ 1] = hop(updates[k], 1)
    updates = [updates[k] for k in range(n_dp)]

    tall, *own = weights(projection, master_t, updates, spans[1:2])
    own += weights(projection, master_t, [tall], spans[2:3])
    *late, own_first, whole = weights(projection, master_t, [tall], spans[3:] + spans[:1] + [(0, cols)])
    own = [own_first] + own + late
    got = {(0, 0): ahead_weights(projection, tall, [ahead])}
    over = {(0, 0): hop(got[(0, 0)], 1)}
    master_new = new_master(projection, master_t, tall, cols // 4)
    moment_one_new, moment_two_new = adam_call(
        moment_one, moment_two, [after(parts[0], [tall])] + parts[1:],
        [jax.ShapeDtypeStruct(moment_one.shape, jnp.float32)] * 2,
    )

    later = range(1, len(counts))
    steps = [(phase, at) for phase in range(3) for at in later] + [(1, 0), (2, 0)]
    outs = [None]
    shape = (cols, n_dp * slab_rows)

    def parts_of(at):
        pieces = [whole, whole_c]
        for which in range(3):
            pieces += [table[(which, at)] for table in (got, over) if (which, at) in table]
        return [(*spans[at], kind, piece) for kind, piece in enumerate(pieces)]

    for step, (phase, at) in enumerate(steps):
        value = got[(0, at)] if phase == 2 else own[at]
        earlier = [got[steps[step - 2]]] if step >= 2 else []
        earlier += [over[steps[step - 4]]] if step >= 4 else []
        if step == 2:
            earlier += [master_new, moment_one_new]
        got[(phase, at)] = turn(after(value, earlier), TURN_MASKS[min(phase, 1)])
        held = [outs[step - len(steps) + 3]] if step >= len(steps) - 2 else []
        over[(phase, at)] = hop(after(got[(phase, at)], held), 1)
        if step == 1:
            whole_c = hop(after(whole, [got[steps[1]]]), 1)
        if phase == 2 and at in (2, 4):
            outs.append(lay(outs[-1], shape, parts_of(at - 1) + parts_of(at) + parts_of(0)[at - 2 : at]))
    parts = parts_of(0)
    outs.append(lay(outs[-1], shape, parts[4:-1]))
    outs.append(lay(outs[-1], shape, parts[-1:]))
    return (moment_one_new, moment_two_new, master_new.T, outs[-1].T)


def solution(mesh):
    n_dp, n_fsdp = mesh.shape["dp"], mesh.shape["fsdp"]

    def body(acts, grad_out, projection, moment_one, moment_two, master):
        args = (acts, grad_out, projection, moment_one, moment_two, master)
        fits = n_dp == 8 and n_fsdp == 4 and moment_one.shape[0] % 32 == 0 and master.shape[0] % 128 == 0
        if fits and grad_out.shape[1] % 64 == 0 and acts.shape[0] % 128 == 0:
            return kernel_body(*args, n_dp, n_fsdp)
        return plain_body(*args)

    in_specs = (
        P(("dp", "fsdp"), None),
        P("dp", "fsdp"),
        P(),
        P("dp", "fsdp"),
        P("dp", "fsdp"),
        P("dp", "fsdp"),
    )
    out_specs = (P("dp", "fsdp"), P("dp", "fsdp"), P("dp", "fsdp"), P(None, "fsdp"))
    return jax.shard_map(body, mesh=mesh, in_specs=in_specs, out_specs=out_specs, check_vma=False)
```

```python
import functools

import jax
import jax.numpy as jnp
from jax import lax
from jax.experimental import pallas as pl
from jax.experimental.pallas import tpu as pltpu
from jax.sharding import PartitionSpec as P

STEP = 1000


BETA_ONE = 0.9
BETA_TWO = 0.999
ADAM_EPS = 1e-08
LEARN_RATE = 0.01
CORRECT_ONE = 1.0 - BETA_ONE**STEP
CORRECT_TWO = 1.0 - BETA_TWO**STEP

VMEM = pl.BlockSpec(memory_space=pltpu.VMEM)
ANY = pl.BlockSpec(memory_space=pl.ANY)


TURN_MASKS = ((2, 4), (4, 2))
UPDATE_MASKS = tuple((k, k) for k in range(8))
SWAP_MASKS = ((0, 0), (4, 2), (2, 4), (6, 6), (7, 7), (5, 3), (3, 5), (1, 1))
OWNER_MASKS = ((0, 0), (1, 1), (2, 4), (5, 3), (4, 2), (3, 5), (6, 6), (7, 7))


def chunk_sizes(cols):
    small = cols // 80 * 16
    part = -(-(cols - 2 * small) // 48) * 16
    return (small, part, part, cols - 2 * part - 2 * small, small)


def adam(grad, moment_one, moment_two):
    moment_one_new = BETA_ONE * moment_one + (1.0 - BETA_ONE) * grad
    moment_two_new = BETA_TWO * moment_two + (1.0 - BETA_TWO) * grad * grad
    update = (
        moment_one_new / CORRECT_ONE / (jnp.sqrt(moment_two_new / CORRECT_TWO) + ADAM_EPS)
    ).astype(jnp.bfloat16)
    return moment_one_new, moment_two_new, update


def plain_body(acts, grad_out, projection, moment_one, moment_two, master):
    projected = jnp.dot(acts, projection, preferred_element_type=jnp.float32).astype(jnp.bfloat16)
    group_proj = lax.all_gather(projected, "fsdp", axis=0, tiled=True)
    partial_value = jnp.einsum(
        "tr,tc->rc", group_proj, grad_out, preferred_element_type=jnp.float32
    )
    partial_value = lax.optimization_barrier(partial_value.astype(jnp.bfloat16))
    grad = lax.psum_scatter(
        partial_value.astype(jnp.float32), "dp", scatter_dimension=0, tiled=True
    )
    moment_one_new, moment_two_new, update = adam(grad, moment_one, moment_two)
    slab_rows = master.shape[0]
    proj_slab = lax.dynamic_slice_in_dim(projection, lax.axis_index("dp") * slab_rows, slab_rows, 0)
    piece = lax.all_gather(update, "dp", axis=0, tiled=True)
    expanded = jnp.dot(proj_slab, piece, preferred_element_type=jnp.float32)
    master_new = master - LEARN_RATE * expanded
    weight_cols = lax.all_gather(master_new.astype(jnp.bfloat16), "dp", axis=0, tiled=True)
    return (moment_one_new, moment_two_new, master_new, weight_cols)


def send(value, axis, size, mask):
    return lax.ppermute(value, axis, [(i, i ^ mask) for i in range(size)])


def other(me, masks):
    return me ^ jnp.where((me & 1) == 0, masks[0], masks[1])


def take_kernel(source, out, held, sems):
    count = held.shape[1]
    ways = []
    for at in range(held.shape[0]):
        rows = pl.ds(at * count, count)
        ways.append((
            pltpu.make_async_copy(source.at[rows, :], held.at[at], sems.at[0, at]),
            pltpu.make_async_copy(held.at[at], out.at[rows, :], sems.at[1, at]),
        ))
    for into, _ in ways:
        into.start()
    for into, back in ways:
        into.wait()
        back.start()
    for _, back in ways:
        back.wait()


def take(array, count):
    parts = count // 48 if count % 48 == 0 else 1
    return pl.pallas_call(
        take_kernel,
        out_shape=jax.ShapeDtypeStruct((count, array.shape[1]), array.dtype),
        in_specs=[ANY],
        out_specs=ANY,
        scratch_shapes=[
            pltpu.VMEM((parts, count // parts, array.shape[1]), array.dtype),
            pltpu.SemaphoreType.DMA((2, parts)),
        ],
        compiler_params=pltpu.CompilerParams(vmem_limit_bytes=60 * 2**20),
    )(array)


def partial_kernel(grad_t, *refs, n_fsdp, n_dp):
    pieces, outs, (tokens, across) = refs[:n_fsdp], refs[n_fsdp : n_fsdp + n_dp], refs[n_fsdp + n_dp :]
    count = pieces[0].shape[0]
    rows = outs[0].shape[0]
    me = lax.axis_index("fsdp")
    for k, piece in enumerate(pieces):
        tokens[pl.ds(pl.multiple_of((me ^ k) * count, count), count), :] = piece[...]
    across[...] = tokens[...].T
    me = lax.axis_index("dp")
    left = jnp.concatenate(
        [across[pl.ds(pl.multiple_of(other(me, masks) * rows, rows), rows), :] for masks in SWAP_MASKS], axis=0
    )
    result = lax.dot_general(
        left, grad_t[...], (((1,), (1,)), ((), ())), preferred_element_type=jnp.float32
    ).astype(jnp.bfloat16)
    for k, out in enumerate(outs):
        out[...] = result[k * rows : (k + 1) * rows, :]


def adam_kernel(moment_one, moment_two, *refs, outs):
    parts, outs = refs[:-outs], refs[-outs:]
    grad = parts[0][...].astype(jnp.float32)
    for part in parts[1:]:
        grad = grad + part[...].astype(jnp.float32)
    one, two, value = adam(grad, moment_one[...], moment_two[...])
    if len(outs) == 2:
        outs[0][...] = one
        outs[1][...] = two
    else:
        outs[0][:, outs[0].shape[1] - 128 :] = jnp.zeros((value.shape[0], 128), value.dtype)
        outs[0][:, : value.shape[1]] = value


def adam_call(moment_one, moment_two, parts, out_shape):
    return pl.pallas_call(
        functools.partial(adam_kernel, outs=len(out_shape)),
        out_shape=out_shape,
        in_specs=[VMEM] * (2 + len(parts)),
        out_specs=[VMEM] * len(out_shape),
        compiler_params=pltpu.CompilerParams(vmem_limit_bytes=16 * 2**20),
    )(moment_one, moment_two, *parts)


def expand(tall, slab, first, count):
    return lax.dot_general(
        tall[pl.ds(first, count), :], slab, (((1,), (1,)), ((), ())),
        preferred_element_type=jnp.float32,
    )


def weight_kernel(projection, master_t, *refs, n_in, spans, block):
    pieces, outs = refs[:n_in], refs[n_in:]
    me = lax.axis_index("dp")
    if n_in > 1:
        tall, wide = outs[0], outs[-1]
        outs = outs[1:-1]
        rows = pieces[0].shape[0]
        for k, piece in enumerate(pieces):
            wide[pl.ds(pl.multiple_of((me ^ k) * rows, rows), rows), :] = piece[...]
        tall[...] = wide[...].T
    else:
        tall = pieces[0]
    slab_rows = master_t.shape[1]
    slab = projection[pl.ds(pl.multiple_of(me * slab_rows, slab_rows), slab_rows), :]
    for (first, count), out in zip(spans, outs):
        for at in range(0, count, block):
            size = min(block, count - at)
            master_new = master_t[pl.ds(first + at, size), :] - LEARN_RATE * expand(
                tall, slab, first + at, size
            )
            out[pl.ds(at, size), :] = master_new.astype(jnp.bfloat16)


def weights(projection, master_t, pieces, spans):
    slab_rows, rank = master_t.shape[1], projection.shape[1]
    wide = pieces[0].shape[1]
    out_shape = [jax.ShapeDtypeStruct((count, slab_rows), jnp.bfloat16) for _, count in spans]
    scratch = []
    if len(pieces) > 1:
        out_shape = [jax.ShapeDtypeStruct((wide, rank), jnp.bfloat16)] + out_shape
        scratch = [pltpu.VMEM((rank, wide), jnp.bfloat16)]
    size = sum(count for _, count in spans) * slab_rows
    return pl.pallas_call(
        functools.partial(weight_kernel, n_in=len(pieces), spans=spans, block=144),
        out_shape=out_shape,
        in_specs=[VMEM] * (2 + len(pieces)),
        out_specs=[VMEM] * len(out_shape),
        scratch_shapes=scratch,
        compiler_params=pltpu.CompilerParams(vmem_limit_bytes=20 * 2**20),
        cost_estimate=pl.CostEstimate(flops=2 * size * rank, bytes_accessed=4 * size, transcendentals=0),
    )(projection, master_t, *pieces)


def ahead_kernel(projection, tall, *refs, block):
    parts, out = refs[:-1], refs[-1]
    slab_rows = out.shape[1]
    owner = other(lax.axis_index("dp"), TURN_MASKS[0])
    slab = projection[pl.ds(pl.multiple_of(owner * slab_rows, slab_rows), slab_rows), :]
    first = 0
    for part in parts:
        for at in range(0, part.shape[0], block):
            size = min(block, part.shape[0] - at)
            master_new = part[pl.ds(at, size), :] - LEARN_RATE * expand(tall, slab, first, size)
            out[pl.ds(first, size), :] = master_new.astype(jnp.bfloat16)
            first += size


def ahead_weights(projection, tall, parts):
    shape = (sum(part.shape[0] for part in parts), parts[0].shape[1])
    size = shape[0] * shape[1]
    return pl.pallas_call(
        functools.partial(ahead_kernel, block=144),
        out_shape=jax.ShapeDtypeStruct(shape, jnp.bfloat16),
        in_specs=[VMEM] * (2 + len(parts)),
        out_specs=VMEM,
        compiler_params=pltpu.CompilerParams(vmem_limit_bytes=20 * 2**20),
        cost_estimate=pl.CostEstimate(
            flops=2 * size * projection.shape[1], bytes_accessed=4 * size, transcendentals=0
        ),
    )(projection, tall, *parts)


def master_kernel(projection, master_t, tall, out):
    slab_rows = master_t.shape[1]
    first = pl.multiple_of(lax.axis_index("dp") * slab_rows, slab_rows)
    slab = projection[pl.ds(first, slab_rows), :]
    block = master_t.shape[0]
    first = pl.multiple_of(pl.program_id(0) * block, block)
    out[...] = master_t[...] - LEARN_RATE * expand(tall, slab, first, block)


def new_master(projection, master_t, tall, block):
    cols, slab_rows = master_t.shape
    rank = projection.shape[1]
    return pl.pallas_call(
        master_kernel,
        out_shape=jax.ShapeDtypeStruct((cols, slab_rows), jnp.float32),
        grid=(cols // block,),
        in_specs=[
            pl.BlockSpec(projection.shape, lambda i: (0, 0)),
            pl.BlockSpec((block, slab_rows), lambda i: (i, 0)),
            pl.BlockSpec(tall.shape, lambda i: (0, 0)),
        ],
        out_specs=pl.BlockSpec((block, slab_rows), lambda i: (i, 0)),
        compiler_params=pltpu.CompilerParams(vmem_limit_bytes=20 * 2**20),
        cost_estimate=pl.CostEstimate(
            flops=2 * cols * slab_rows * rank, bytes_accessed=8 * cols * slab_rows, transcendentals=0
        ),
    )(projection, master_t, tall)


def lay_kernel(*refs, places, fresh):
    refs = refs if fresh else refs[1:]
    pieces, out, sems = refs[:-2], refs[-2], refs[-1]
    me = lax.axis_index("dp")
    copies = []
    for at, (index, first, count, kind) in enumerate(places):
        piece = pieces[index]
        width = piece.shape[1]
        column = pl.multiple_of(other(me, OWNER_MASKS[kind]) * width, 128)
        part = piece if piece.shape[0] == count else piece.at[pl.ds(first, count), :]
        target = out.at[pl.ds(first, count), pl.ds(column, width)]
        copies.append(pltpu.make_async_copy(part, target, sems.at[at]))
    for copy in copies:
        copy.start()
    for copy in copies:
        copy.wait()


def lay(out, shape, parts):
    fresh = out is None
    held = [] if fresh else [out]
    pieces = []
    places = []
    for first, count, kind, piece in parts:
        known = [at for at, other_piece in enumerate(pieces) if other_piece is piece]
        if not known:
            pieces.append(piece)
        places.append((known[0] if known else len(pieces) - 1, first, count, kind))
    size = sum(count for _, _, count, _ in places) * pieces[0].shape[1]
    return pl.pallas_call(
        functools.partial(lay_kernel, places=tuple(places), fresh=fresh),
        out_shape=jax.ShapeDtypeStruct(shape, jnp.bfloat16),
        in_specs=[ANY] * len(held) + [VMEM] * len(pieces),
        out_specs=ANY,
        scratch_shapes=[pltpu.SemaphoreType.DMA((len(places),))],
        input_output_aliases={} if fresh else {0: 0},
        compiler_params=pltpu.CompilerParams(vmem_limit_bytes=20 * 2**20),
        cost_estimate=pl.CostEstimate(flops=0, bytes_accessed=4 * size, transcendentals=0),
    )(*held, *pieces)


def kernel_body(acts, grad_out, projection, moment_one, moment_two, master, n_dp, n_fsdp):
    cols = grad_out.shape[1]
    rank = projection.shape[1]
    rows = moment_one.shape[0]
    slab_rows = master.shape[0]
    wide = -(-cols // 128) * 128
    master_t = master.T

    def hop(value, mask):
        return send(value, "dp", n_dp, mask)

    def turn(value, masks):
        return lax.ppermute(value, "dp", [(i, i ^ masks[i & 1]) for i in range(n_dp)])

    def after(value, earlier):
        return lax.optimization_barrier((value, *earlier))[0] if earlier else value

    counts = chunk_sizes(cols)
    spans = [(sum(counts[:at]), count) for at, count in enumerate(counts)]
    taken = take(master_t, counts[0])
    ahead = turn(taken, TURN_MASKS[0])
    acts = after(acts, [taken])

    projected = jnp.dot(acts, projection, preferred_element_type=jnp.float32).astype(jnp.bfloat16)
    tokens = [projected] + [send(projected, "fsdp", n_fsdp, k) for k in range(1, n_fsdp)]
    parts = pl.pallas_call(
        functools.partial(partial_kernel, n_fsdp=n_fsdp, n_dp=n_dp),
        out_shape=[jax.ShapeDtypeStruct((rows, cols), jnp.bfloat16)] * n_dp,
        in_specs=[VMEM] * (1 + n_fsdp),
        out_specs=[VMEM] * n_dp,
        scratch_shapes=[
            pltpu.VMEM((n_fsdp * projected.shape[0], rank), jnp.bfloat16),
            pltpu.VMEM((rank, n_fsdp * projected.shape[0]), jnp.bfloat16),
        ],
        compiler_params=pltpu.CompilerParams(vmem_limit_bytes=16 * 2**20),
    )(grad_out.T, *tokens)
    parts = [part if masks == (0, 0) else turn(part, masks) for part, masks in zip(parts, SWAP_MASKS)]
    (update,) = adam_call(
        after(moment_one, [ahead]), moment_two, parts, [jax.ShapeDtypeStruct((rows, wide), jnp.bfloat16)]
    )
    updates = {0: update}
    for k in (6, 2, 4, 1):
        updates[k] = hop(update, k)
    for k in (2, 4, 6):
        updates[k ^ 1] = hop(updates[k], 1)
    updates = [updates[k] for k in range(n_dp)]

    tall, *own = weights(projection, master_t, updates, spans[1:2])
    own += weights(projection, master_t, [tall], spans[2:3])
    *late, own_first, whole = weights(projection, master_t, [tall], spans[3:] + spans[:1] + [(0, cols)])
    own = [own_first] + own + late
    got = {(0, 0): ahead_weights(projection, tall, [ahead])}
    over = {(0, 0): hop(got[(0, 0)], 1)}
    master_new = new_master(projection, master_t, tall, cols // 4)
    moment_one_new, moment_two_new = adam_call(
        moment_one, moment_two, [after(parts[0], [tall])] + parts[1:],
        [jax.ShapeDtypeStruct(moment_one.shape, jnp.float32)] * 2,
    )

    later = range(1, len(counts))
    steps = [(phase, at) for phase in range(3) for at in later] + [(1, 0), (2, 0)]
    outs = [None]
    shape = (cols, n_dp * slab_rows)

    def parts_of(at):
        pieces = [whole, whole_c]
        for which in range(3):
            pieces += [table[(which, at)] for table in (got, over) if (which, at) in table]
        return [(*spans[at], kind, piece) for kind, piece in enumerate(pieces)]

    for step, (phase, at) in enumerate(steps):
        value = got[(0, at)] if phase == 2 else own[at]
        earlier = [got[steps[step - 2]]] if step >= 2 else []
        earlier += [over[steps[step - 4]]] if step >= 4 else []
        if step == 2:
            earlier += [master_new, moment_one_new]
        got[(phase, at)] = turn(after(value, earlier), TURN_MASKS[min(phase, 1)])
        held = [outs[step - len(steps) + 3]] if step >= len(steps) - 2 else []
        over[(phase, at)] = hop(after(got[(phase, at)], held), 1)
        if step == 1:
            whole_c = hop(after(whole, [got[steps[1]]]), 1)
        if phase == 2 and at in (2, 4):
            outs.append(lay(outs[-1], shape, parts_of(at - 1) + parts_of(at) + parts_of(0)[at - 2 : at]))
    parts = parts_of(0)
    outs.append(lay(outs[-1], shape, parts[4:-1]))
    outs.append(lay(outs[-1], shape, parts[-1:]))
    return (moment_one_new, moment_two_new, master_new.T, outs[-1].T)


def solution(mesh):
    n_dp, n_fsdp = mesh.shape["dp"], mesh.shape["fsdp"]

    def body(acts, grad_out, projection, moment_one, moment_two, master):
        args = (acts, grad_out, projection, moment_one, moment_two, master)
        fits = n_dp == 8 and n_fsdp == 4 and moment_one.shape[0] % 32 == 0 and master.shape[0] % 128 == 0
        if fits and grad_out.shape[1] % 64 == 0 and acts.shape[0] % 128 == 0:
            return kernel_body(*args, n_dp, n_fsdp)
        return plain_body(*args)

    in_specs = (
        P(("dp", "fsdp"), None),
        P("dp", "fsdp"),
        P(),
        P("dp", "fsdp"),
        P("dp", "fsdp"),
        P("dp", "fsdp"),
    )
    out_specs = (P("dp", "fsdp"), P("dp", "fsdp"), P("dp", "fsdp"), P(None, "fsdp"))
    return jax.shard_map(body, mesh=mesh, in_specs=in_specs, out_specs=out_specs, check_vma=False)
```

```python
import functools

import jax
import jax.numpy as jnp
from jax import lax
from jax.experimental import pallas as pl
from jax.experimental.pallas import tpu as pltpu
from jax.sharding import PartitionSpec as P

STEP = 1000


BETA_ONE = 0.9
BETA_TWO = 0.999
ADAM_EPS = 1e-08
LEARN_RATE = 0.01
CORRECT_ONE = 1.0 - BETA_ONE**STEP
CORRECT_TWO = 1.0 - BETA_TWO**STEP

VMEM = pl.BlockSpec(memory_space=pltpu.VMEM)
ANY = pl.BlockSpec(memory_space=pl.ANY)


TURN_MASKS = ((2, 4), (4, 2))
UPDATE_MASKS = tuple((k, k) for k in range(8))
SWAP_MASKS = ((0, 0), (4, 2), (2, 4), (6, 6), (7, 7), (5, 3), (3, 5), (1, 1))
OWNER_MASKS = ((0, 0), (1, 1), (2, 4), (5, 3), (4, 2), (3, 5), (6, 6), (7, 7))


def chunk_sizes(cols):
    small = cols // 80 * 16
    part = -(-(cols - 2 * small) // 48) * 16
    return (small, part, part, cols - 2 * part - 2 * small, small)


def adam(grad, moment_one, moment_two):
    moment_one_new = BETA_ONE * moment_one + (1.0 - BETA_ONE) * grad
    moment_two_new = BETA_TWO * moment_two + (1.0 - BETA_TWO) * grad * grad
    update = (
        moment_one_new / CORRECT_ONE / (jnp.sqrt(moment_two_new / CORRECT_TWO) + ADAM_EPS)
    ).astype(jnp.bfloat16)
    return moment_one_new, moment_two_new, update


def plain_body(acts, grad_out, projection, moment_one, moment_two, master):
    projected = jnp.dot(acts, projection, preferred_element_type=jnp.float32).astype(jnp.bfloat16)
    group_proj = lax.all_gather(projected, "fsdp", axis=0, tiled=True)
    partial_value = jnp.einsum(
        "tr,tc->rc", group_proj, grad_out, preferred_element_type=jnp.float32
    )
    partial_value = lax.optimization_barrier(partial_value.astype(jnp.bfloat16))
    grad = lax.psum_scatter(
        partial_value.astype(jnp.float32), "dp", scatter_dimension=0, tiled=True
    )
    moment_one_new, moment_two_new, update = adam(grad, moment_one, moment_two)
    slab_rows = master.shape[0]
    proj_slab = lax.dynamic_slice_in_dim(projection, lax.axis_index("dp") * slab_rows, slab_rows, 0)
    piece = lax.all_gather(update, "dp", axis=0, tiled=True)
    expanded = jnp.dot(proj_slab, piece, preferred_element_type=jnp.float32)
    master_new = master - LEARN_RATE * expanded
    weight_cols = lax.all_gather(master_new.astype(jnp.bfloat16), "dp", axis=0, tiled=True)
    return (moment_one_new, moment_two_new, master_new, weight_cols)


def send(value, axis, size, mask):
    return lax.ppermute(value, axis, [(i, i ^ mask) for i in range(size)])


def other(me, masks):
    return me ^ jnp.where((me & 1) == 0, masks[0], masks[1])


def take_kernel(source, out, held, sems):
    count = held.shape[1]
    ways = []
    for at in range(held.shape[0]):
        rows = pl.ds(at * count, count)
        ways.append((
            pltpu.make_async_copy(source.at[rows, :], held.at[at], sems.at[0, at]),
            pltpu.make_async_copy(held.at[at], out.at[rows, :], sems.at[1, at]),
        ))
    for into, _ in ways:
        into.start()
    for into, back in ways:
        into.wait()
        back.start()
    for _, back in ways:
        back.wait()


def take(array, count):
    parts = count // 48 if count % 48 == 0 else 1
    return pl.pallas_call(
        take_kernel,
        out_shape=jax.ShapeDtypeStruct((count, array.shape[1]), array.dtype),
        in_specs=[ANY],
        out_specs=ANY,
        scratch_shapes=[
            pltpu.VMEM((parts, count // parts, array.shape[1]), array.dtype),
            pltpu.SemaphoreType.DMA((2, parts)),
        ],
        compiler_params=pltpu.CompilerParams(vmem_limit_bytes=60 * 2**20),
    )(array)


def partial_kernel(grad_t, *refs, n_fsdp, n_dp):
    pieces, outs, (tokens, across) = refs[:n_fsdp], refs[n_fsdp : n_fsdp + n_dp], refs[n_fsdp + n_dp :]
    count = pieces[0].shape[0]
    rows = outs[0].shape[0]
    me = lax.axis_index("fsdp")
    for k, piece in enumerate(pieces):
        tokens[pl.ds(pl.multiple_of((me ^ k) * count, count), count), :] = piece[...]
    across[...] = tokens[...].T
    me = lax.axis_index("dp")
    left = jnp.concatenate(
        [across[pl.ds(pl.multiple_of(other(me, masks) * rows, rows), rows), :] for masks in SWAP_MASKS], axis=0
    )
    result = lax.dot_general(
        left, grad_t[...], (((1,), (1,)), ((), ())), preferred_element_type=jnp.float32
    ).astype(jnp.bfloat16)
    for k, out in enumerate(outs):
        out[...] = result[k * rows : (k + 1) * rows, :]


def adam_kernel(moment_one, moment_two, *refs, outs):
    parts, outs = refs[:-outs], refs[-outs:]
    grad = parts[0][...].astype(jnp.float32)
    for part in parts[1:]:
        grad = grad + part[...].astype(jnp.float32)
    one, two, value = adam(grad, moment_one[...], moment_two[...])
    if len(outs) == 2:
        outs[0][...] = one
        outs[1][...] = two
    else:
        outs[0][:, outs[0].shape[1] - 128 :] = jnp.zeros((value.shape[0], 128), value.dtype)
        outs[0][:, : value.shape[1]] = value


def adam_call(moment_one, moment_two, parts, out_shape):
    return pl.pallas_call(
        functools.partial(adam_kernel, outs=len(out_shape)),
        out_shape=out_shape,
        in_specs=[VMEM] * (2 + len(parts)),
        out_specs=[VMEM] * len(out_shape),
        compiler_params=pltpu.CompilerParams(vmem_limit_bytes=16 * 2**20),
    )(moment_one, moment_two, *parts)


def expand(tall, slab, first, count):
    return lax.dot_general(
        tall[pl.ds(first, count), :], slab, (((1,), (1,)), ((), ())),
        preferred_element_type=jnp.float32,
    )


def weight_kernel(projection, master_t, *refs, n_in, spans, block):
    pieces, outs = refs[:n_in], refs[n_in:]
    me = lax.axis_index("dp")
    if n_in > 1:
        tall, wide = outs[0], outs[-1]
        outs = outs[1:-1]
        rows = pieces[0].shape[0]
        for k, piece in enumerate(pieces):
            wide[pl.ds(pl.multiple_of((me ^ k) * rows, rows), rows), :] = piece[...]
        tall[...] = wide[...].T
    else:
        tall = pieces[0]
    slab_rows = master_t.shape[1]
    slab = projection[pl.ds(pl.multiple_of(me * slab_rows, slab_rows), slab_rows), :]
    for (first, count), out in zip(spans, outs):
        for at in range(0, count, block):
            size = min(block, count - at)
            master_new = master_t[pl.ds(first + at, size), :] - LEARN_RATE * expand(
                tall, slab, first + at, size
            )
            out[pl.ds(at, size), :] = master_new.astype(jnp.bfloat16)


def weights(projection, master_t, pieces, spans):
    slab_rows, rank = master_t.shape[1], projection.shape[1]
    wide = pieces[0].shape[1]
    out_shape = [jax.ShapeDtypeStruct((count, slab_rows), jnp.bfloat16) for _, count in spans]
    scratch = []
    if len(pieces) > 1:
        out_shape = [jax.ShapeDtypeStruct((wide, rank), jnp.bfloat16)] + out_shape
        scratch = [pltpu.VMEM((rank, wide), jnp.bfloat16)]
    size = sum(count for _, count in spans) * slab_rows
    return pl.pallas_call(
        functools.partial(weight_kernel, n_in=len(pieces), spans=spans, block=144),
        out_shape=out_shape,
        in_specs=[VMEM] * (2 + len(pieces)),
        out_specs=[VMEM] * len(out_shape),
        scratch_shapes=scratch,
        compiler_params=pltpu.CompilerParams(vmem_limit_bytes=20 * 2**20),
        cost_estimate=pl.CostEstimate(flops=2 * size * rank, bytes_accessed=4 * size, transcendentals=0),
    )(projection, master_t, *pieces)


def ahead_kernel(projection, tall, *refs, block):
    parts, out = refs[:-1], refs[-1]
    slab_rows = out.shape[1]
    owner = other(lax.axis_index("dp"), TURN_MASKS[0])
    slab = projection[pl.ds(pl.multiple_of(owner * slab_rows, slab_rows), slab_rows), :]
    first = 0
    for part in parts:
        for at in range(0, part.shape[0], block):
            size = min(block, part.shape[0] - at)
            master_new = part[pl.ds(at, size), :] - LEARN_RATE * expand(tall, slab, first, size)
            out[pl.ds(first, size), :] = master_new.astype(jnp.bfloat16)
            first += size


def ahead_weights(projection, tall, parts):
    shape = (sum(part.shape[0] for part in parts), parts[0].shape[1])
    size = shape[0] * shape[1]
    return pl.pallas_call(
        functools.partial(ahead_kernel, block=144),
        out_shape=jax.ShapeDtypeStruct(shape, jnp.bfloat16),
        in_specs=[VMEM] * (2 + len(parts)),
        out_specs=VMEM,
        compiler_params=pltpu.CompilerParams(vmem_limit_bytes=20 * 2**20),
        cost_estimate=pl.CostEstimate(
            flops=2 * size * projection.shape[1], bytes_accessed=4 * size, transcendentals=0
        ),
    )(projection, tall, *parts)


def master_kernel(projection, master_t, tall, out):
    slab_rows = master_t.shape[1]
    first = pl.multiple_of(lax.axis_index("dp") * slab_rows, slab_rows)
    slab = projection[pl.ds(first, slab_rows), :]
    block = master_t.shape[0]
    first = pl.multiple_of(pl.program_id(0) * block, block)
    out[...] = master_t[...] - LEARN_RATE * expand(tall, slab, first, block)


def new_master(projection, master_t, tall, block):
    cols, slab_rows = master_t.shape
    rank = projection.shape[1]
    return pl.pallas_call(
        master_kernel,
        out_shape=jax.ShapeDtypeStruct((cols, slab_rows), jnp.float32),
        grid=(cols // block,),
        in_specs=[
            pl.BlockSpec(projection.shape, lambda i: (0, 0)),
            pl.BlockSpec((block, slab_rows), lambda i: (i, 0)),
            pl.BlockSpec(tall.shape, lambda i: (0, 0)),
        ],
        out_specs=pl.BlockSpec((block, slab_rows), lambda i: (i, 0)),
        compiler_params=pltpu.CompilerParams(vmem_limit_bytes=20 * 2**20),
        cost_estimate=pl.CostEstimate(
            flops=2 * cols * slab_rows * rank, bytes_accessed=8 * cols * slab_rows, transcendentals=0
        ),
    )(projection, master_t, tall)


def lay_kernel(*refs, places, ways, fresh):
    refs = refs if fresh else refs[1:]
    pieces, out, sems = refs[:-2], refs[-2], refs[-1]
    me = lax.axis_index("dp")
    copies = []
    for at, (index, first, count, kind) in enumerate(places):
        piece = pieces[index]
        width = piece.shape[1]
        column = pl.multiple_of(other(me, OWNER_MASKS[kind]) * width, 128)
        origin = 0 if piece.shape[0] == count else first
        size = -(-count // (16 * ways)) * 16
        for way in range(ways):
            start = way * size
            rows = min(size, count - start)
            part = piece.at[pl.ds(origin + start, rows), :]
            target = out.at[pl.ds(first + start, rows), pl.ds(column, width)]
            copies.append(pltpu.make_async_copy(part, target, sems.at[at * ways + way]))
    for copy in copies:
        copy.start()
    for copy in copies:
        copy.wait()


def lay(out, shape, parts):
    fresh = out is None
    held = [] if fresh else [out]
    pieces = []
    places = []
    for first, count, kind, piece in parts:
        known = [at for at, other_piece in enumerate(pieces) if other_piece is piece]
        if not known:
            pieces.append(piece)
        places.append((known[0] if known else len(pieces) - 1, first, count, kind))
    size = sum(count for _, _, count, _ in places) * pieces[0].shape[1]
    ways = 1 if len(places) > 4 else 4
    return pl.pallas_call(
        functools.partial(lay_kernel, places=tuple(places), ways=ways, fresh=fresh),
        out_shape=jax.ShapeDtypeStruct(shape, jnp.bfloat16),
        in_specs=[ANY] * len(held) + [VMEM] * len(pieces),
        out_specs=ANY,
        scratch_shapes=[pltpu.SemaphoreType.DMA((len(places) * ways,))],
        input_output_aliases={} if fresh else {0: 0},
        compiler_params=pltpu.CompilerParams(vmem_limit_bytes=20 * 2**20),
        cost_estimate=pl.CostEstimate(flops=0, bytes_accessed=4 * size, transcendentals=0),
    )(*held, *pieces)


def kernel_body(acts, grad_out, projection, moment_one, moment_two, master, n_dp, n_fsdp):
    cols = grad_out.shape[1]
    rank = projection.shape[1]
    rows = moment_one.shape[0]
    slab_rows = master.shape[0]
    wide = -(-cols // 128) * 128
    master_t = master.T

    def hop(value, mask):
        return send(value, "dp", n_dp, mask)

    def turn(value, masks):
        return lax.ppermute(value, "dp", [(i, i ^ masks[i & 1]) for i in range(n_dp)])

    def after(value, earlier):
        return lax.optimization_barrier((value, *earlier))[0] if earlier else value

    counts = chunk_sizes(cols)
    spans = [(sum(counts[:at]), count) for at, count in enumerate(counts)]
    taken = take(master_t, counts[0])
    ahead = turn(taken, TURN_MASKS[0])
    acts = after(acts, [taken])

    projected = jnp.dot(acts, projection, preferred_element_type=jnp.float32).astype(jnp.bfloat16)
    tokens = [projected] + [send(projected, "fsdp", n_fsdp, k) for k in range(1, n_fsdp)]
    parts = pl.pallas_call(
        functools.partial(partial_kernel, n_fsdp=n_fsdp, n_dp=n_dp),
        out_shape=[jax.ShapeDtypeStruct((rows, cols), jnp.bfloat16)] * n_dp,
        in_specs=[VMEM] * (1 + n_fsdp),
        out_specs=[VMEM] * n_dp,
        scratch_shapes=[
            pltpu.VMEM((n_fsdp * projected.shape[0], rank), jnp.bfloat16),
            pltpu.VMEM((rank, n_fsdp * projected.shape[0]), jnp.bfloat16),
        ],
        compiler_params=pltpu.CompilerParams(vmem_limit_bytes=16 * 2**20),
    )(grad_out.T, *tokens)
    parts = [part if masks == (0, 0) else turn(part, masks) for part, masks in zip(parts, SWAP_MASKS)]
    (update,) = adam_call(
        after(moment_one, [ahead]), moment_two, parts, [jax.ShapeDtypeStruct((rows, wide), jnp.bfloat16)]
    )
    updates = {0: update}
    for k in (6, 2, 4, 1):
        updates[k] = hop(update, k)
    for k in (2, 4, 6):
        updates[k ^ 1] = hop(updates[k], 1)
    updates = [updates[k] for k in range(n_dp)]

    tall, *own = weights(projection, master_t, updates, spans[1:2])
    own += weights(projection, master_t, [tall], spans[2:3])
    *late, own_first, whole = weights(projection, master_t, [tall], spans[3:] + spans[:1] + [(0, cols)])
    own = [own_first] + own + late
    got = {(0, 0): ahead_weights(projection, tall, [ahead])}
    over = {(0, 0): hop(got[(0, 0)], 1)}
    master_new = new_master(projection, master_t, tall, cols // 4)
    moment_one_new, moment_two_new = adam_call(
        moment_one, moment_two, [after(parts[0], [tall])] + parts[1:],
        [jax.ShapeDtypeStruct(moment_one.shape, jnp.float32)] * 2,
    )

    later = range(1, len(counts))
    steps = [(phase, at) for phase in range(3) for at in later] + [(1, 0), (2, 0)]
    outs = [None]
    shape = (cols, n_dp * slab_rows)

    def parts_of(at):
        pieces = [whole, whole_c]
        for which in range(3):
            pieces += [table[(which, at)] for table in (got, over) if (which, at) in table]
        return [(*spans[at], kind, piece) for kind, piece in enumerate(pieces)]

    for step, (phase, at) in enumerate(steps):
        value = got[(0, at)] if phase == 2 else own[at]
        earlier = [got[steps[step - 2]]] if step >= 2 else []
        earlier += [over[steps[step - 4]]] if step >= 4 else []
        if step == 2:
            earlier += [master_new, moment_one_new]
        got[(phase, at)] = turn(after(value, earlier), TURN_MASKS[min(phase, 1)])
        held = [outs[step - len(steps) + 3]] if step >= len(steps) - 2 else []
        over[(phase, at)] = hop(after(got[(phase, at)], held), 1)
        if step == 1:
            whole_c = hop(after(whole, [got[steps[1]]]), 1)
        if phase == 2 and at in (2, 4):
            outs.append(lay(outs[-1], shape, parts_of(at - 1) + parts_of(at) + parts_of(0)[at - 2 : at]))
    parts = parts_of(0)
    outs.append(lay(outs[-1], shape, parts[4:-1]))
    outs.append(lay(outs[-1], shape, parts[-1:]))
    return (moment_one_new, moment_two_new, master_new.T, outs[-1].T)


def solution(mesh):
    n_dp, n_fsdp = mesh.shape["dp"], mesh.shape["fsdp"]

    def body(acts, grad_out, projection, moment_one, moment_two, master):
        args = (acts, grad_out, projection, moment_one, moment_two, master)
        fits = n_dp == 8 and n_fsdp == 4 and moment_one.shape[0] % 32 == 0 and master.shape[0] % 128 == 0
        if fits and grad_out.shape[1] % 64 == 0 and acts.shape[0] % 128 == 0:
            return kernel_body(*args, n_dp, n_fsdp)
        return plain_body(*args)

    in_specs = (
        P(("dp", "fsdp"), None),
        P("dp", "fsdp"),
        P(),
        P("dp", "fsdp"),
        P("dp", "fsdp"),
        P("dp", "fsdp"),
    )
    out_specs = (P("dp", "fsdp"), P("dp", "fsdp"), P("dp", "fsdp"), P(None, "fsdp"))
    return jax.shard_map(body, mesh=mesh, in_specs=in_specs, out_specs=out_specs, check_vma=False)
```

```python
import functools

import jax
import jax.numpy as jnp
from jax import lax
from jax.experimental import pallas as pl
from jax.experimental.pallas import tpu as pltpu
from jax.sharding import PartitionSpec as P

STEP = 1000


BETA_ONE = 0.9
BETA_TWO = 0.999
ADAM_EPS = 1e-08
LEARN_RATE = 0.01
CORRECT_ONE = 1.0 - BETA_ONE**STEP
CORRECT_TWO = 1.0 - BETA_TWO**STEP

VMEM = pl.BlockSpec(memory_space=pltpu.VMEM)
ANY = pl.BlockSpec(memory_space=pl.ANY)


TURN_MASKS = ((2, 4), (4, 2))
UPDATE_MASKS = tuple((k, k) for k in range(8))
SWAP_MASKS = ((0, 0), (4, 2), (2, 4), (6, 6), (7, 7), (5, 3), (3, 5), (1, 1))
OWNER_MASKS = ((0, 0), (1, 1), (2, 4), (5, 3), (4, 2), (3, 5), (6, 6), (7, 7))


def chunk_sizes(cols):
    small = cols // 80 * 16
    part = -(-(cols - 2 * small) // 48) * 16
    return (small, part, part, cols - 2 * part - 2 * small, small)


def adam(grad, moment_one, moment_two):
    moment_one_new = BETA_ONE * moment_one + (1.0 - BETA_ONE) * grad
    moment_two_new = BETA_TWO * moment_two + (1.0 - BETA_TWO) * grad * grad
    update = (
        moment_one_new / CORRECT_ONE / (jnp.sqrt(moment_two_new / CORRECT_TWO) + ADAM_EPS)
    ).astype(jnp.bfloat16)
    return moment_one_new, moment_two_new, update


def plain_body(acts, grad_out, projection, moment_one, moment_two, master):
    projected = jnp.dot(acts, projection, preferred_element_type=jnp.float32).astype(jnp.bfloat16)
    group_proj = lax.all_gather(projected, "fsdp", axis=0, tiled=True)
    partial_value = jnp.einsum(
        "tr,tc->rc", group_proj, grad_out, preferred_element_type=jnp.float32
    )
    partial_value = lax.optimization_barrier(partial_value.astype(jnp.bfloat16))
    grad = lax.psum_scatter(
        partial_value.astype(jnp.float32), "dp", scatter_dimension=0, tiled=True
    )
    moment_one_new, moment_two_new, update = adam(grad, moment_one, moment_two)
    slab_rows = master.shape[0]
    proj_slab = lax.dynamic_slice_in_dim(projection, lax.axis_index("dp") * slab_rows, slab_rows, 0)
    piece = lax.all_gather(update, "dp", axis=0, tiled=True)
    expanded = jnp.dot(proj_slab, piece, preferred_element_type=jnp.float32)
    master_new = master - LEARN_RATE * expanded
    weight_cols = lax.all_gather(master_new.astype(jnp.bfloat16), "dp", axis=0, tiled=True)
    return (moment_one_new, moment_two_new, master_new, weight_cols)


def send(value, axis, size, mask):
    return lax.ppermute(value, axis, [(i, i ^ mask) for i in range(size)])


def other(me, masks):
    return me ^ jnp.where((me & 1) == 0, masks[0], masks[1])


def take_kernel(source, out, held, sems):
    count = held.shape[1]
    ways = []
    for at in range(held.shape[0]):
        rows = pl.ds(at * count, count)
        ways.append((
            pltpu.make_async_copy(source.at[rows, :], held.at[at], sems.at[0, at]),
            pltpu.make_async_copy(held.at[at], out.at[rows, :], sems.at[1, at]),
        ))
    for into, _ in ways:
        into.start()
    for into, back in ways:
        into.wait()
        back.start()
    for _, back in ways:
        back.wait()


def take(array, count):
    parts = count // 48 if count % 48 == 0 else 1
    return pl.pallas_call(
        take_kernel,
        out_shape=jax.ShapeDtypeStruct((count, array.shape[1]), array.dtype),
        in_specs=[ANY],
        out_specs=ANY,
        scratch_shapes=[
            pltpu.VMEM((parts, count // parts, array.shape[1]), array.dtype),
            pltpu.SemaphoreType.DMA((2, parts)),
        ],
        compiler_params=pltpu.CompilerParams(vmem_limit_bytes=60 * 2**20),
    )(array)


def partial_kernel(grad_t, *refs, n_fsdp, n_dp):
    pieces, outs, (tokens, across) = refs[:n_fsdp], refs[n_fsdp : n_fsdp + n_dp], refs[n_fsdp + n_dp :]
    count = pieces[0].shape[0]
    rows = outs[0].shape[0]
    me = lax.axis_index("fsdp")
    for k, piece in enumerate(pieces):
        tokens[pl.ds(pl.multiple_of((me ^ k) * count, count), count), :] = piece[...]
    across[...] = tokens[...].T
    me = lax.axis_index("dp")
    left = jnp.concatenate(
        [across[pl.ds(pl.multiple_of(other(me, masks) * rows, rows), rows), :] for masks in SWAP_MASKS], axis=0
    )
    result = lax.dot_general(
        left, grad_t[...], (((1,), (1,)), ((), ())), preferred_element_type=jnp.float32
    ).astype(jnp.bfloat16)
    for k, out in enumerate(outs):
        out[...] = result[k * rows : (k + 1) * rows, :]


def adam_kernel(moment_one, moment_two, *refs, outs):
    parts, outs = refs[:-outs], refs[-outs:]
    grad = parts[0][...].astype(jnp.float32)
    for part in parts[1:]:
        grad = grad + part[...].astype(jnp.float32)
    one, two, value = adam(grad, moment_one[...], moment_two[...])
    if len(outs) == 2:
        outs[0][...] = one
        outs[1][...] = two
    else:
        outs[0][:, outs[0].shape[1] - 128 :] = jnp.zeros((value.shape[0], 128), value.dtype)
        outs[0][:, : value.shape[1]] = value


def adam_call(moment_one, moment_two, parts, out_shape):
    return pl.pallas_call(
        functools.partial(adam_kernel, outs=len(out_shape)),
        out_shape=out_shape,
        in_specs=[VMEM] * (2 + len(parts)),
        out_specs=[VMEM] * len(out_shape),
        compiler_params=pltpu.CompilerParams(vmem_limit_bytes=16 * 2**20),
    )(moment_one, moment_two, *parts)


def expand(tall, slab, first, count):
    return lax.dot_general(
        tall[pl.ds(first, count), :], slab, (((1,), (1,)), ((), ())),
        preferred_element_type=jnp.float32,
    )


def weight_kernel(projection, master_t, *refs, n_in, spans, block):
    pieces, outs = refs[:n_in], refs[n_in:]
    me = lax.axis_index("dp")
    if n_in > 1:
        tall, wide = outs[0], outs[-1]
        outs = outs[1:-1]
        rows = pieces[0].shape[0]
        for k, piece in enumerate(pieces):
            wide[pl.ds(pl.multiple_of((me ^ k) * rows, rows), rows), :] = piece[...]
        tall[...] = wide[...].T
    else:
        tall = pieces[0]
    slab_rows = master_t.shape[1]
    slab = projection[pl.ds(pl.multiple_of(me * slab_rows, slab_rows), slab_rows), :]
    for (first, count), out in zip(spans, outs):
        for at in range(0, count, block):
            size = min(block, count - at)
            master_new = master_t[pl.ds(first + at, size), :] - LEARN_RATE * expand(
                tall, slab, first + at, size
            )
            out[pl.ds(at, size), :] = master_new.astype(jnp.bfloat16)


def weights(projection, master_t, pieces, spans):
    slab_rows, rank = master_t.shape[1], projection.shape[1]
    wide = pieces[0].shape[1]
    out_shape = [jax.ShapeDtypeStruct((count, slab_rows), jnp.bfloat16) for _, count in spans]
    scratch = []
    if len(pieces) > 1:
        out_shape = [jax.ShapeDtypeStruct((wide, rank), jnp.bfloat16)] + out_shape
        scratch = [pltpu.VMEM((rank, wide), jnp.bfloat16)]
    size = sum(count for _, count in spans) * slab_rows
    return pl.pallas_call(
        functools.partial(weight_kernel, n_in=len(pieces), spans=spans, block=144),
        out_shape=out_shape,
        in_specs=[VMEM] * (2 + len(pieces)),
        out_specs=[VMEM] * len(out_shape),
        scratch_shapes=scratch,
        compiler_params=pltpu.CompilerParams(vmem_limit_bytes=20 * 2**20),
        cost_estimate=pl.CostEstimate(flops=2 * size * rank, bytes_accessed=4 * size, transcendentals=0),
    )(projection, master_t, *pieces)


def ahead_kernel(projection, tall, *refs, block):
    parts, out = refs[:-1], refs[-1]
    slab_rows = out.shape[1]
    owner = other(lax.axis_index("dp"), TURN_MASKS[0])
    slab = projection[pl.ds(pl.multiple_of(owner * slab_rows, slab_rows), slab_rows), :]
    first = 0
    for part in parts:
        for at in range(0, part.shape[0], block):
            size = min(block, part.shape[0] - at)
            master_new = part[pl.ds(at, size), :] - LEARN_RATE * expand(tall, slab, first, size)
            out[pl.ds(first, size), :] = master_new.astype(jnp.bfloat16)
            first += size


def ahead_weights(projection, tall, parts):
    shape = (sum(part.shape[0] for part in parts), parts[0].shape[1])
    size = shape[0] * shape[1]
    return pl.pallas_call(
        functools.partial(ahead_kernel, block=144),
        out_shape=jax.ShapeDtypeStruct(shape, jnp.bfloat16),
        in_specs=[VMEM] * (2 + len(parts)),
        out_specs=VMEM,
        compiler_params=pltpu.CompilerParams(vmem_limit_bytes=20 * 2**20),
        cost_estimate=pl.CostEstimate(
            flops=2 * size * projection.shape[1], bytes_accessed=4 * size, transcendentals=0
        ),
    )(projection, tall, *parts)


def master_kernel(projection, master_t, tall, out):
    slab_rows = master_t.shape[1]
    first = pl.multiple_of(lax.axis_index("dp") * slab_rows, slab_rows)
    slab = projection[pl.ds(first, slab_rows), :]
    block = master_t.shape[0]
    first = pl.multiple_of(pl.program_id(0) * block, block)
    out[...] = master_t[...] - LEARN_RATE * expand(tall, slab, first, block)


def new_master(projection, master_t, tall, block):
    cols, slab_rows = master_t.shape
    rank = projection.shape[1]
    return pl.pallas_call(
        master_kernel,
        out_shape=jax.ShapeDtypeStruct((cols, slab_rows), jnp.float32),
        grid=(cols // block,),
        in_specs=[
            pl.BlockSpec(projection.shape, lambda i: (0, 0)),
            pl.BlockSpec((block, slab_rows), lambda i: (i, 0)),
            pl.BlockSpec(tall.shape, lambda i: (0, 0)),
        ],
        out_specs=pl.BlockSpec((block, slab_rows), lambda i: (i, 0)),
        compiler_params=pltpu.CompilerParams(vmem_limit_bytes=20 * 2**20),
        cost_estimate=pl.CostEstimate(
            flops=2 * cols * slab_rows * rank, bytes_accessed=8 * cols * slab_rows, transcendentals=0
        ),
    )(projection, master_t, tall)


def lay_kernel(*refs, places, fresh):
    refs = refs if fresh else refs[1:]
    pieces, out, sems = refs[:-2], refs[-2], refs[-1]
    me = lax.axis_index("dp")
    copies = []
    for at, (index, first, count, kind) in enumerate(places):
        piece = pieces[index]
        width = piece.shape[1]
        column = pl.multiple_of(other(me, OWNER_MASKS[kind]) * width, 128)
        part = piece if piece.shape[0] == count else piece.at[pl.ds(first, count), :]
        target = out.at[pl.ds(first, count), pl.ds(column, width)]
        copies.append(pltpu.make_async_copy(part, target, sems.at[at]))
    for copy in copies:
        copy.start()
    for copy in copies:
        copy.wait()


def lay(out, shape, parts):
    fresh = out is None
    held = [] if fresh else [out]
    pieces = []
    places = []
    for first, count, kind, piece in parts:
        known = [at for at, other_piece in enumerate(pieces) if other_piece is piece]
        if not known:
            pieces.append(piece)
        places.append((known[0] if known else len(pieces) - 1, first, count, kind))
    size = sum(count for _, _, count, _ in places) * pieces[0].shape[1]
    return pl.pallas_call(
        functools.partial(lay_kernel, places=tuple(places), fresh=fresh),
        out_shape=jax.ShapeDtypeStruct(shape, jnp.bfloat16),
        in_specs=[ANY] * len(held) + [VMEM] * len(pieces),
        out_specs=ANY,
        scratch_shapes=[pltpu.SemaphoreType.DMA((len(places),))],
        input_output_aliases={} if fresh else {0: 0},
        compiler_params=pltpu.CompilerParams(vmem_limit_bytes=20 * 2**20),
        cost_estimate=pl.CostEstimate(flops=0, bytes_accessed=4 * size, transcendentals=0),
    )(*held, *pieces)


def kernel_body(acts, grad_out, projection, moment_one, moment_two, master, n_dp, n_fsdp):
    cols = grad_out.shape[1]
    rank = projection.shape[1]
    rows = moment_one.shape[0]
    slab_rows = master.shape[0]
    wide = -(-cols // 128) * 128
    master_t = master.T

    def hop(value, mask):
        return send(value, "dp", n_dp, mask)

    def turn(value, masks):
        return lax.ppermute(value, "dp", [(i, i ^ masks[i & 1]) for i in range(n_dp)])

    def after(value, earlier):
        return lax.optimization_barrier((value, *earlier))[0] if earlier else value

    counts = chunk_sizes(cols)
    spans = [(sum(counts[:at]), count) for at, count in enumerate(counts)]
    taken = take(master_t, counts[0])
    ahead = turn(taken, TURN_MASKS[0])
    acts = after(acts, [taken])

    projected = jnp.dot(acts, projection, preferred_element_type=jnp.float32).astype(jnp.bfloat16)
    tokens = [projected] + [send(projected, "fsdp", n_fsdp, k) for k in range(1, n_fsdp)]
    parts = pl.pallas_call(
        functools.partial(partial_kernel, n_fsdp=n_fsdp, n_dp=n_dp),
        out_shape=[jax.ShapeDtypeStruct((rows, cols), jnp.bfloat16)] * n_dp,
        in_specs=[VMEM] * (1 + n_fsdp),
        out_specs=[VMEM] * n_dp,
        scratch_shapes=[
            pltpu.VMEM((n_fsdp * projected.shape[0], rank), jnp.bfloat16),
            pltpu.VMEM((rank, n_fsdp * projected.shape[0]), jnp.bfloat16),
        ],
        compiler_params=pltpu.CompilerParams(vmem_limit_bytes=16 * 2**20),
    )(grad_out.T, *tokens)
    parts = [part if masks == (0, 0) else turn(part, masks) for part, masks in zip(parts, SWAP_MASKS)]
    (update,) = adam_call(
        after(moment_one, [ahead]), moment_two, parts, [jax.ShapeDtypeStruct((rows, wide), jnp.bfloat16)]
    )
    updates = {0: update}
    for k in (6, 2, 4, 1):
        updates[k] = hop(update, k)
    for k in (2, 4, 6):
        updates[k ^ 1] = hop(updates[k], 1)
    updates = [updates[k] for k in range(n_dp)]

    tall, *own = weights(projection, master_t, updates, spans[1:2])
    own += weights(projection, master_t, [tall], spans[2:3])
    *late, own_first, whole = weights(projection, master_t, [tall], spans[3:] + spans[:1] + [(0, cols)])
    own = [own_first] + own + late
    got = {(0, 0): ahead_weights(projection, tall, [ahead])}
    over = {(0, 0): hop(got[(0, 0)], 1)}
    master_new = new_master(projection, master_t, tall, cols // 4)
    moment_one_new, moment_two_new = adam_call(
        moment_one, moment_two, [after(parts[0], [tall])] + parts[1:],
        [jax.ShapeDtypeStruct(moment_one.shape, jnp.float32)] * 2,
    )

    later = range(1, len(counts))
    steps = [(phase, at) for phase in range(3) for at in later] + [(1, 0), (2, 0)]
    outs = [None]
    shape = (cols, n_dp * slab_rows)

    def parts_of(at):
        pieces = [whole, whole_c]
        for which in range(3):
            pieces += [table[(which, at)] for table in (got, over) if (which, at) in table]
        return [(*spans[at], kind, piece) for kind, piece in enumerate(pieces)]

    for step, (phase, at) in enumerate(steps):
        value = got[(0, at)] if phase == 2 else own[at]
        earlier = [got[steps[step - 2]]] if step >= 2 else []
        earlier += [over[steps[step - 4]]] if step >= 4 else []
        if step == 2:
            earlier.append(moment_one_new)
        if step == 3:
            earlier.append(master_new)
        got[(phase, at)] = turn(after(value, earlier), TURN_MASKS[min(phase, 1)])
        held = [outs[step - len(steps) + 3]] if step >= len(steps) - 2 else []
        over[(phase, at)] = hop(after(got[(phase, at)], held), 1)
        if step == 1:
            whole_c = hop(after(whole, [got[steps[1]]]), 1)
        if phase == 2 and at in (2, 4):
            outs.append(lay(outs[-1], shape, parts_of(at - 1) + parts_of(at) + parts_of(0)[at - 2 : at]))
    parts = parts_of(0)
    outs.append(lay(outs[-1], shape, parts[4:-1]))
    outs.append(lay(outs[-1], shape, parts[-1:]))
    return (moment_one_new, moment_two_new, master_new.T, outs[-1].T)


def solution(mesh):
    n_dp, n_fsdp = mesh.shape["dp"], mesh.shape["fsdp"]

    def body(acts, grad_out, projection, moment_one, moment_two, master):
        args = (acts, grad_out, projection, moment_one, moment_two, master)
        fits = n_dp == 8 and n_fsdp == 4 and moment_one.shape[0] % 32 == 0 and master.shape[0] % 128 == 0
        if fits and grad_out.shape[1] % 64 == 0 and acts.shape[0] % 128 == 0:
            return kernel_body(*args, n_dp, n_fsdp)
        return plain_body(*args)

    in_specs = (
        P(("dp", "fsdp"), None),
        P("dp", "fsdp"),
        P(),
        P("dp", "fsdp"),
        P("dp", "fsdp"),
        P("dp", "fsdp"),
    )
    out_specs = (P("dp", "fsdp"), P("dp", "fsdp"), P("dp", "fsdp"), P(None, "fsdp"))
    return jax.shard_map(body, mesh=mesh, in_specs=in_specs, out_specs=out_specs, check_vma=False)
```
